128 devices in a mesh: ctx: 16 (over z_lo, x, core), fsdp: 8 (over z_hi, y).
Axes of the slice: x: 4, y: 4, z: 4 (z_hi: 2, z_lo: 2; z = z_hi * 2 + z_lo), core: 2. Of those that a mesh axis runs over, the one named last changes fastest.
Arguments:
- tokens: bfloat16 [8, 2048, 2048], P('fsdp', 'ctx'), may hold values from -6 to 6
- cotangent: bfloat16 [8, 2048, 2048], P('fsdp', 'ctx'), may hold values from -6 to 6
- attn_gain: float32 [2048], replicated, may hold values from 0.5 to 1.5
- q_weight: bfloat16 [2048, 2048], P(None, 'fsdp'), may hold values from -0.125 to 0.125
- k_weight: bfloat16 [2048, 1024], P(None, 'fsdp'), may hold values from -0.125 to 0.125
- v_weight: bfloat16 [2048, 1024], P(None, 'fsdp'), may hold values from -0.125 to 0.125
- q_gain: float32 [128], replicated, may hold values from 0.5 to 1.5
- k_gain: float32 [128], replicated, may hold values from 0.5 to 1.5
- o_weight: bfloat16 [2048, 2048], P('fsdp'), may hold values from -2 to 2
- mlp_gain: float32 [2048], replicated, may hold values from 0.5 to 1.5
- gate_weight: bfloat16 [2048, 6144], P(None, 'fsdp'), may hold values from -0.125 to 0.125
- up_weight: bfloat16 [2048, 6144], P(None, 'fsdp'), may hold values from -0.125 to 0.125
- down_weight: bfloat16 [6144, 2048], P('fsdp'), may hold values from -0.078125 to 0.078125
- doc_lengths: int32 [8, 4], replicated, may hold values from 1 to 1984, 2048 in all within a row
- block_place: int32 [32], replicated, may hold values from 0 to 31, as said below
Outputs:
- out_rows: bfloat16 [8, 2048, 2048], P('fsdp', 'ctx')
- tokens_grad: bfloat16 [8, 2048, 2048], P('fsdp', 'ctx')
- attn_gain_grad: float32 [2048], replicated
- q_weight_grad: float32 [2048, 2048], P('ctx', 'fsdp')
- k_weight_grad: float32 [2048, 1024], P('ctx', 'fsdp')
- v_weight_grad: float32 [2048, 1024], P('ctx', 'fsdp')
- q_gain_grad: float32 [128], replicated
- k_gain_grad: float32 [128], replicated
- o_weight_grad: float32 [2048, 2048], P('fsdp', 'ctx')
- mlp_gain_grad: float32 [2048], replicated
- gate_weight_grad: float32 [2048, 6144], P('ctx', 'fsdp')
- up_weight_grad: float32 [2048, 6144], P('ctx', 'fsdp')
- down_weight_grad: float32 [6144, 2048], P('fsdp', 'ctx')
The draws below stay inside these ranges and needn't reach their ends.
Inputs may be any that keep to these rules, and one draw needn't show every extreme that they name: `block_place`: stored blocks 2 j and 2 j + 1 hold blocks b and 31 - b of the sequence, in either order; each block is held once. `doc_lengths`: each row sums to 2048; one document of each row has exactly 1984 tokens.
All inputs are finite; a program needn't handle non-finite values.
Results may differ from the reference program's by a relative error of at most 0.028.
Values may be sent and summed in bfloat16 or wider, within the bound.
A program may use at most 192 MiB of HBM per device.

```python
import math
from functools import partial
import jax
import jax.numpy as jnp
import numpy as np
from jax import lax

D = 2048
FF = 6144
H = 16
KV = 8
HD = 128
BLK = 64
DOCS = 4
BLOCKS = 32
SEQ_LEN = 2048
SEQS = 8


def draw_block_place(key, part):
    key = jax.random.fold_in(key, 7)
    order_key, flip_key = jax.random.split(key)
    pair_count = BLOCKS // 2
    owners = jax.random.permutation(order_key, pair_count).astype(jnp.int32)
    flip_bits = jax.random.randint(flip_key, (pair_count,), 0, 2).astype(jnp.int32)
    low_block = owners
    high_block = BLOCKS - 1 - owners
    leading = jnp.where(flip_bits == 1, high_block, low_block)
    second = jnp.where(flip_bits == 1, low_block, high_block)
    return jnp.stack([leading, second], axis=1).reshape(BLOCKS).astype(jnp.int32)


def shard_levels(key, shape, pieces, least, largest):
    def one(dim, blocks):
        draws = jax.random.uniform(jax.random.fold_in(jax.random.fold_in(key, 6), dim), (blocks,), jnp.float32, least / len(pieces), largest / len(pieces))
        return jnp.repeat(jnp.exp(draws), shape[dim] // blocks).reshape((-1,) + (1,) * (len(shape) - dim - 1))

    loudness = one(*pieces[0])
    for cut in pieces[1:]:
        loudness = loudness * one(*cut)
    return loudness


def length_profile(count, total, limit, lean):
    loads = [(1 << 20) // math.isqrt(rank ** lean) + 1 for rank in range(2, count + 1)]
    spare, counts = total - limit - (count - 1), [1] * (count - 1)
    while spare > 0:
        free = [i for i in range(count - 1) if counts[i] < limit]
        pool, left = sum([loads[i] for i in free]), spare
        for i in free:
            extra = min(limit - counts[i], max(1, left * loads[i] // pool), spare)
            counts[i] = counts[i] + extra
            spare = spare - extra
    return np.array([limit] + counts)


def uneven_parts(stream_key, number_of, total, bound, slope):
    if number_of == 2:
        one = jax.random.randint(stream_key, (), max(1, total - bound), min(bound, total - 1) + 1)
        return jnp.stack([one, total - one])
    tallies = jnp.asarray(length_profile(number_of, total, bound, slope), jnp.int32)
    pairs = (number_of - 1) // 2
    donor, sink = tallies[1:1 + 2 * pairs:2], tallies[2:2 + 2 * pairs:2]
    slack = jnp.minimum(donor - 1, bound - sink)
    moved = jax.random.randint(jax.random.fold_in(stream_key, 1), (pairs,), 0, 1 << 20) % (slack + 1)
    tallies = tallies.at[1:1 + 2 * pairs:2].set(donor - moved).at[2:2 + 2 * pairs:2].set(sink + moved)
    return tallies[jax.random.permutation(jax.random.fold_in(stream_key, 2), number_of)]


def bell_draw(own_key, shape, spread, limit, cuts=(), kind=jnp.bfloat16):
    array = spread * jax.random.normal(own_key, shape, jnp.float32)
    if cuts:
        array = array * shard_levels(own_key, shape, cuts, -0.22, 0.18)
    return jnp.clip(array, -limit, limit).astype(kind)


def setup_inputs(seed: int = 0) -> dict:
    key_list = jax.random.split(jax.random.key(seed), 16)
    return {
        "tokens": bell_draw(key_list[0], (SEQS, SEQ_LEN, D), 1.0, 6.0, ((0, 8), (1, 16))),
        "cotangent": bell_draw(key_list[1], (SEQS, SEQ_LEN, D), 1.0, 6.0, ((0, 8), (1, 16))),
        "attn_gain": jnp.clip(1.0 + 0.1 * jax.random.normal(key_list[2], (D,), jnp.float32), 0.5, 1.5),
        "q_weight": bell_draw(key_list[3], (D, H * HD), D ** -0.5, 0.125, ((1, 8),)),
        "k_weight": bell_draw(key_list[4], (D, KV * HD), D ** -0.5, 0.125, ((1, 8),)),
        "v_weight": bell_draw(key_list[5], (D, KV * HD), D ** -0.5, 0.125, ((1, 8),)),
        "q_gain": jnp.clip(1.0 + 0.1 * jax.random.normal(key_list[6], (HD,), jnp.float32), 0.5, 1.5),
        "k_gain": jnp.clip(1.0 + 0.1 * jax.random.normal(key_list[7], (HD,), jnp.float32), 0.5, 1.5),
        "o_weight": bell_draw(key_list[8], (H * HD, D), (max(1, H * HD * 8 // SEQ_LEN)) ** -0.5, 2.0, ((0, 8),)),
        "mlp_gain": jnp.clip(1.0 + 0.1 * jax.random.normal(key_list[9], (D,), jnp.float32), 0.5, 1.5),
        "gate_weight": bell_draw(key_list[10], (D, FF), D ** -0.5, 0.125, ((1, 8),)),
        "up_weight": bell_draw(key_list[11], (D, FF), D ** -0.5, 0.125, ((1, 8),)),
        "down_weight": bell_draw(key_list[12], (FF, D), FF ** -0.5, 0.078125, ((0, 8),)),
        "doc_lengths": jax.vmap(lambda own: uneven_parts(own, DOCS, SEQ_LEN, SEQ_LEN - BLK, 2))(jax.random.split(key_list[13], SEQS)).reshape((SEQS, DOCS)).astype(jnp.int32),
        "block_place": draw_block_place(jax.random.fold_in(key_list[15], 71), 0),
    }


EPSILON = 1e-06
ROPE_BASE = 1000000.0
MASKED_SCORE = -1e+30

@jax.custom_vjp
def low(v):
    return lax.optimization_barrier(v.astype(jnp.bfloat16)).astype(jnp.float32)

@jax.custom_vjp
def low_back(v):
    return v

def low_keep(v):
    return (low(v), None)

def low_pass(kept, grad):
    return (grad,)

def back_keep(v):
    return (v, None)

def back_low(kept, grad):
    return (low(grad),)
low.defvjp(low_keep, low_pass)
low_back.defvjp(back_keep, back_low)

def matmul_hi(left_side, right_side):
    return jnp.dot(left_side, right_side, precision=lax.Precision.HIGHEST, preferred_element_type=jnp.float32)

def rms_scale(values, gain_vec):
    inverse = lax.rsqrt(lax.optimization_barrier(jnp.mean(values * values, axis=-1, keepdims=True)) + EPSILON)
    return values * inverse * gain_vec

def head_prep(values, gain_vec, cos_table, sin_table):
    scaled = rms_scale(values, gain_vec)
    midway = scaled.shape[-1] // 2
    turned = jnp.concatenate([-scaled[..., midway:], scaled[..., :midway]], axis=-1)
    return scaled * cos_table + turned * sin_table

def tables(positions, head_dim):
    exponent_steps = jnp.arange(head_dim // 2, dtype=jnp.int32).astype(jnp.float32) * (2.0 / head_dim)
    frequency = ROPE_BASE ** (-exponent_steps)
    phases = positions.astype(jnp.float32)[:, None] * frequency[None, :]
    phases = jnp.concatenate([phases, phases], axis=-1)
    return (jnp.cos(phases), jnp.sin(phases))

def stored_positions(block_place, block_width):
    return (block_place[:, None] * block_width + jnp.arange(block_width, dtype=jnp.int32)[None, :]).reshape(-1)

def document_ids(positions, doc_lengths):
    ends = jnp.cumsum(doc_lengths, axis=-1, dtype=jnp.int32)
    return lax.optimization_barrier(jnp.sum((positions[None, :, None] >= ends[:, None, :]).astype(jnp.int32), axis=-1, dtype=jnp.int32))

def attend_block(queries, places, labels, keys, values, positions, documents):
    scores = jnp.einsum('bkgd,tkd->kgbt', queries, keys, precision=lax.Precision.HIGHEST) * HD ** (-0.5)
    scores = low_back(scores)
    allowed = (positions[None, :] <= places[:, None]) & (documents[None, :] == labels[:, None])
    scores = jnp.where(allowed, scores, MASKED_SCORE)
    weights_soft = low(jax.nn.softmax(scores, axis=-1))
    return jnp.einsum('kgbt,tkd->bkgd', weights_soft, values, precision=lax.Precision.HIGHEST)

def sequence_layer(rows_in, weight_set, positions, documents):
    attn_gain, q_weight, k_weight, v_weight, q_gain, k_gain, o_weight, mlp_gain, gate_weight, up_weight, down_weight = weight_set
    cos_table, sin_table = tables(positions, HD)
    cos_table = cos_table[:, None, :]
    sin_table = sin_table[:, None, :]
    normed = low(rms_scale(rows_in, attn_gain))
    q_raw = low_back(matmul_hi(normed, q_weight)).reshape(SEQ_LEN, H, HD)
    k_raw = low_back(matmul_hi(normed, k_weight)).reshape(SEQ_LEN, KV, HD)
    values = low(low_back(matmul_hi(normed, v_weight))).reshape(SEQ_LEN, KV, HD)
    queries = low(head_prep(q_raw, q_gain, cos_table, sin_table)).reshape(SEQ_LEN, KV, H // KV, HD)
    keys = low(head_prep(k_raw, k_gain, cos_table, sin_table))
    query_block = math.gcd(SEQ_LEN, 512)
    block_count = SEQ_LEN // query_block
    run_block = jax.checkpoint(lambda member: attend_block(member[0], member[1], member[2], keys, values, positions, documents))
    attended = lax.map(run_block, (queries.reshape(block_count, query_block, KV, H // KV, HD), positions.reshape(block_count, query_block), documents.reshape(block_count, query_block)))
    attended = low(low_back(attended.reshape(SEQ_LEN, H * HD)))
    middle = rows_in + low_back(matmul_hi(attended, o_weight))
    hidden = low(rms_scale(middle, mlp_gain))
    gate_pre = low_back(matmul_hi(hidden, gate_weight))
    up_pre = low_back(matmul_hi(hidden, up_weight))
    activation = low(jax.nn.silu(gate_pre) * up_pre)
    return middle + matmul_hi(activation, down_weight)

def forward(tokens, attn_gain, q_weight, k_weight, v_weight, q_gain, k_gain, o_weight, mlp_gain, gate_weight, up_weight, down_weight, positions, documents):
    weight_set = (attn_gain, q_weight, k_weight, v_weight, q_gain, k_gain, o_weight, mlp_gain, gate_weight, up_weight, down_weight)
    run_layer = jax.checkpoint(lambda member: sequence_layer(member[0], weight_set, positions, member[1]))
    return lax.map(run_layer, (tokens, documents))

def reference(tokens, cotangent, attn_gain, q_weight, k_weight, v_weight, q_gain, k_gain, o_weight, mlp_gain, gate_weight, up_weight, down_weight, doc_lengths, block_place):
    positions = stored_positions(block_place, BLK)
    documents = document_ids(positions, doc_lengths)
    run_forward = partial(forward, positions=positions, documents=documents)
    outputs, pull_back = jax.vjp(run_forward, tokens.astype(jnp.float32), attn_gain.astype(jnp.float32), q_weight.astype(jnp.float32), k_weight.astype(jnp.float32), v_weight.astype(jnp.float32), q_gain.astype(jnp.float32), k_gain.astype(jnp.float32), o_weight.astype(jnp.float32), mlp_gain.astype(jnp.float32), gate_weight.astype(jnp.float32), up_weight.astype(jnp.float32), down_weight.astype(jnp.float32))
    grads = pull_back(cotangent.astype(jnp.float32))
    return (outputs.astype(jnp.bfloat16), grads[0].astype(jnp.bfloat16), grads[1], grads[2], grads[3], grads[4], grads[5], grads[6], grads[7], grads[8], grads[9], grads[10], grads[11])
```

```python
import jax
import jax.numpy as jnp
from jax import lax
from jax.experimental import pallas as pl
from jax.experimental.pallas import tpu as pltpu
from jax.sharding import Mesh, PartitionSpec as P

EPSILON = 1e-06
ROPE_BASE = 1000000.0
MASKED_SCORE = -1e30
HD = 128
BLK = 64
AXES = ("zl", "x", "core", "zh", "y")
SIZES = (2, 4, 2, 2, 4)
CTX = ("zl", "x", "core")
FSDP = ("zh", "y")
F32 = jnp.float32
BF16 = jnp.bfloat16


def rms_scale(values, gain_vec):
    inverse = lax.rsqrt(jnp.mean(values * values, axis=-1, keepdims=True) + EPSILON)
    return values * inverse * gain_vec


def head_prep(values, gain_vec, cos_table, sin_table):
    scaled = rms_scale(values, gain_vec)
    midway = scaled.shape[-1] // 2
    turned = jnp.concatenate([-scaled[..., midway:], scaled[..., :midway]], axis=-1)
    return scaled * cos_table + turned * sin_table


def tables(positions, head_dim):
    exponent_steps = jnp.arange(head_dim // 2, dtype=jnp.int32).astype(F32) * (2.0 / head_dim)
    frequency = ROPE_BASE ** (-exponent_steps)
    phases = positions.astype(F32)[:, None] * frequency[None, :]
    phases = jnp.concatenate([phases, phases], axis=-1)
    return (jnp.cos(phases), jnp.sin(phases))


def dot(left, right, contract=((1,), (0,))):
    return lax.dot_general(left, right, (contract, ((), ())), preferred_element_type=F32)


def from_next(value, axis, step):
    size = dict(zip(AXES, SIZES))[axis]
    return lax.ppermute(value, axis, [((i + step) % size, i) for i in range(size)])


def along_z(value, source):
    place = [(z % 2) * 2 + z // 2 for z in range(4)]
    return lax.ppermute(value, ("zl", "zh"), [(place[source(z)], place[z]) for z in range(4)])


def from_next_z(value, step):
    return along_z(value, lambda z: (z + step) % 4)


def gather_y(rows):
    return jnp.stack([rows] + [from_next(rows, "y", k) for k in (1, 2, 3)])


def scatter_y(parts):
    total = parts[0]
    for k in (1, 2, 3):
        total = total + from_next(parts[k].astype(BF16), "y", 4 - k).astype(F32)
    return total


def partner_shard(shard):
    rows, cols = shard.shape
    eighth = rows // 8
    x, core = lax.axis_index("x"), lax.axis_index("core")
    piece = lax.dynamic_slice_in_dim(shard, (x * 2 + core) * eighth, eighth, 0)
    piece = along_z(piece, lambda z: 3 - z)
    ring = jnp.stack([piece] + [from_next(piece, "x", k) for k in (1, 2, 3)])
    other = from_next(ring, "core", 1)
    low = jnp.where(core == 0, ring, other)
    high = jnp.where(core == 0, other, ring)
    both = jnp.stack([low, high], axis=1)
    both = jnp.concatenate([both, both], axis=0)
    both = lax.dynamic_slice_in_dim(both, lax.rem(4 - x, 4), 4, 0)
    return both.reshape(rows, cols)


def weight_grad(left, right):
    rows, width = left.shape
    n = right.shape[1] // 2
    x, core = lax.axis_index("x"), lax.axis_index("core")
    z = lax.axis_index("zh") * 2 + lax.axis_index("zl")
    zh = lax.axis_index("zh")
    split = left.reshape(rows, 8, 2, width // 16)
    theirs = lax.dynamic_index_in_dim(split, 1 - core, 2, keepdims=False).reshape(rows, width // 2)
    mine = lax.dynamic_index_in_dim(split, core, 2, keepdims=False).reshape(rows, width // 2)
    sent = dot(theirs, right, ((0,), (0,))).astype(BF16)
    got = from_next(sent, "core", 1)
    part = (dot(mine, right, ((0,), (0,))) + got.astype(F32)).astype(BF16)
    part = part.reshape(2, 4, width // 16, 2 * n)

    def for_x(k):
        return lax.dynamic_index_in_dim(part, lax.rem(x + k, 4), 1, keepdims=False)

    total = for_x(0).astype(F32)
    for k in (1, 2, 3):
        total = total + from_next(for_x(k), "x", 4 - k).astype(F32)
    part = total.astype(BF16)
    part = part.reshape(2, width // 16, 2, n)

    def for_z(k):
        dest = lax.rem(z + k, 4)
        rows_of = lax.dynamic_index_in_dim(part, lax.rem(dest, 2), 0, keepdims=False)
        side = jnp.where(dest // 2 == zh, 0, 1)
        return lax.dynamic_index_in_dim(rows_of, side, 1, keepdims=False)

    total = for_z(0).astype(F32)
    for k in (1, 2, 3):
        total = total + from_next_z(for_z(k), 4 - k).astype(F32)
    return total


def sum_all(vector):
    for axis, steps in (("y", (1, 2, 3)), ("x", (1, 2, 3)), ("core", (1,))):
        vector = vector + sum(from_next(vector, axis, k) for k in steps)
    return vector + sum(from_next_z(vector, k) for k in (1, 2, 3))


TILE = 256


def keep_mask(ends, first_row, rows, cols):
    place = first_row + lax.broadcasted_iota(jnp.int32, (rows, 1), 0)
    start = jnp.zeros((rows, 1), jnp.int32)
    for j in range(ends.shape[0]):
        start = jnp.where(place >= ends[j], ends[j], start)
    key = lax.broadcasted_iota(jnp.int32, (rows, cols), 1)
    return (key >= start) & (key <= place)


def attend_kernel(place, ends, core, q_in, mine, other, out, q_pos, k_pos, v_pos, log_total, out_pos):
    rows = q_in.shape[0]
    blocks = rows // BLK
    scale = HD ** (-0.5)

    @pl.when(core[0] == 0)
    def _():
        @pl.loop(0, blocks)
        def _(b):
            src = pl.ds(pl.multiple_of(b * BLK, BLK), BLK)
            dst = pl.ds(pl.multiple_of(place[b] * BLK, BLK), BLK)
            q_pos[dst, :] = q_in[src, :]
            k_pos[dst, :] = mine[src, :]
            v_pos[dst, :] = other[src, :]

    @pl.when(core[0] == 1)
    def _():
        @pl.loop(0, blocks)
        def _(b):
            src = pl.ds(pl.multiple_of(b * BLK, BLK), BLK)
            dst = pl.ds(pl.multiple_of(place[b] * BLK, BLK), BLK)
            q_pos[dst, :] = q_in[src, :]
            k_pos[dst, :] = other[src, :]
            v_pos[dst, :] = mine[src, :]

    for i in range(rows // TILE):
        span = pl.ds(i * TILE, TILE)
        n = (i + 1) * TILE
        scores = dot(q_pos[span, :], k_pos[:n, :], ((1,), (1,))) * scale
        scores = jnp.where(keep_mask(ends, i * TILE, TILE, n), scores, MASKED_SCORE)
        top = jnp.max(scores, axis=-1, keepdims=True)
        weights = jnp.exp(scores - top)
        total = jnp.sum(weights, axis=-1, keepdims=True)
        log_total[span, :] = top + jnp.log(total)
        probs = (weights * (1.0 / total)).astype(BF16)
        out_pos[span, :] = dot(probs, v_pos[:n, :]).astype(BF16)

    @pl.loop(0, blocks)
    def _(b):
        src = pl.ds(pl.multiple_of(b * BLK, BLK), BLK)
        dst = pl.ds(pl.multiple_of(place[b] * BLK, BLK), BLK)
        out[src, :] = out_pos[dst, :]


def attend_back_kernel(
    place, ends, core, grad_in, q_pos, k_pos, v_pos, log_total, q_grad, keep_grad, send_grad,
    grad_pos, q_acc, k_acc, v_acc,
):
    rows = grad_in.shape[0]
    blocks = rows // BLK
    scale = HD ** (-0.5)

    @pl.loop(0, blocks)
    def _(b):
        src = pl.ds(pl.multiple_of(b * BLK, BLK), BLK)
        dst = pl.ds(pl.multiple_of(place[b] * BLK, BLK), BLK)
        grad_pos[dst, :] = grad_in[src, :]

    k_acc[...] = jnp.zeros_like(k_acc)
    v_acc[...] = jnp.zeros_like(v_acc)
    for i in range(rows // TILE):
        span = pl.ds(i * TILE, TILE)
        n = (i + 1) * TILE
        queries = q_pos[span, :]
        grads = grad_pos[span, :]
        scores = dot(queries, k_pos[:n, :], ((1,), (1,))) * scale
        kept = keep_mask(ends, i * TILE, TILE, n)
        probs = jnp.where(kept, jnp.exp(scores - log_total[span, :]), 0.0)
        prob_grad = dot(grads, v_pos[:n, :], ((1,), (1,)))
        row_dot = jnp.sum(prob_grad * probs, axis=-1, keepdims=True)
        score_grad = (probs * (prob_grad - row_dot)).astype(BF16)
        q_acc[span, :] = (dot(score_grad, k_pos[:n, :]) * scale).astype(BF16)
        k_acc[:n, :] += dot(score_grad, queries, ((0,), (0,)))
        v_acc[:n, :] += dot(probs.astype(BF16), grads, ((0,), (0,)))

    @pl.loop(0, blocks)
    def _(b):
        src = pl.ds(pl.multiple_of(b * BLK, BLK), BLK)
        dst = pl.ds(pl.multiple_of(place[b] * BLK, BLK), BLK)
        q_grad[src, :] = q_acc[dst, :]
        k_rows = k_acc[dst, :] * scale
        v_rows = v_acc[dst, :]
        first = core[0] == 0
        keep_grad[src, :] = jnp.where(first, k_rows, v_rows)
        send_grad[src, :] = jnp.where(first, v_rows, k_rows).astype(BF16)


def attend(place, ends, core, q_in, mine, other):
    rows = q_in.shape[0]
    low = jax.ShapeDtypeStruct((rows, HD), BF16)
    smem = pl.BlockSpec(memory_space=pltpu.SMEM)
    vmem = pl.BlockSpec(memory_space=pltpu.VMEM)
    return pl.pallas_call(
        attend_kernel,
        out_shape=(low, low, low, low, jax.ShapeDtypeStruct((rows, 1), F32)),
        in_specs=[smem] * 3 + [vmem] * 3,
        out_specs=(vmem,) * 5,
        scratch_shapes=[pltpu.VMEM((rows, HD), BF16)],
        compiler_params=pltpu.CompilerParams(vmem_limit_bytes=40 * 2**20),
        cost_estimate=pl.CostEstimate(
            flops=2 * rows * rows * HD, bytes_accessed=rows * HD * 16, transcendentals=rows * rows // 2
        ),
        name="attend",
    )(place, ends, core, q_in, mine, other)


def attend_back(place, ends, core, grad_in, q_pos, k_pos, v_pos, log_total):
    rows = grad_in.shape[0]
    low = jax.ShapeDtypeStruct((rows, HD), BF16)
    smem = pl.BlockSpec(memory_space=pltpu.SMEM)
    vmem = pl.BlockSpec(memory_space=pltpu.VMEM)
    return pl.pallas_call(
        attend_back_kernel,
        out_shape=(low, jax.ShapeDtypeStruct((rows, HD), F32), low),
        in_specs=[smem] * 3 + [vmem] * 5,
        out_specs=(vmem,) * 3,
        scratch_shapes=[
            pltpu.VMEM((rows, HD), BF16),
            pltpu.VMEM((rows, HD), BF16),
            pltpu.VMEM((rows, HD), F32),
            pltpu.VMEM((rows, HD), F32),
        ],
        compiler_params=pltpu.CompilerParams(vmem_limit_bytes=48 * 2**20),
        cost_estimate=pl.CostEstimate(
            flops=5 * rows * rows * HD, bytes_accessed=rows * HD * 20, transcendentals=rows * rows // 2
        ),
        name="attend_back",
    )(place, ends, core, grad_in, q_pos, k_pos, v_pos, log_total)


def per_device(
    tokens,
    cotangent,
    attn_gain,
    q_weight,
    k_weight,
    v_weight,
    q_gain,
    k_gain,
    o_weight,
    mlp_gain,
    gate_weight,
    up_weight,
    down_weight,
    doc_lengths,
    block_place,
):
    rows = tokens.shape[1]
    zl, x, core = (lax.axis_index(a) for a in CTX)
    zh, y = (lax.axis_index(a) for a in FSDP)
    ctx_place = zl * 8 + x * 2 + core
    sequence = zh * 4 + lax.rem(y + ctx_place // 4, 4)
    ends = jnp.cumsum(lax.dynamic_index_in_dim(doc_lengths, sequence, 0, keepdims=False))
    ends = ends.astype(jnp.int32)
    core_flag = core.astype(jnp.int32).reshape(1)
    own_blocks = lax.dynamic_slice_in_dim(block_place, ctx_place * (rows // BLK), rows // BLK)
    own_positions = (own_blocks[:, None] * BLK + jnp.arange(BLK, dtype=jnp.int32)[None, :]).reshape(-1)
    cos_rows, sin_rows = tables(own_positions, HD)
    cos_rows = cos_rows[None, :, None, :]
    sin_rows = sin_rows[None, :, None, :]

    residual = tokens[0].astype(F32)
    normed = rms_scale(residual, attn_gain).astype(BF16)
    normed_all = gather_y(normed).reshape(4 * rows, -1)
    qkv_own = jnp.concatenate([q_weight, k_weight, v_weight], axis=1)
    qkv_cat = jnp.concatenate([qkv_own, partner_shard(qkv_own)], axis=1)
    raw = dot(normed_all, qkv_cat)
    raw = raw.reshape(4, rows, 2, 4, HD)
    q_raw = raw[:, :, :, :2].reshape(4, rows, 4, HD)
    k_raw = raw[:, :, :, 2]
    values = raw[:, :, :, 3].astype(BF16)
    queries = head_prep(q_raw, q_gain, cos_rows, sin_rows).astype(BF16)
    keys = head_prep(k_raw, k_gain, cos_rows, sin_rows).astype(BF16)
    q_out = queries.transpose(0, 2, 1, 3).reshape(16, 1, rows, HD)
    kv_out = jnp.stack([keys.transpose(0, 2, 1, 3), values.transpose(0, 2, 1, 3)], axis=2)
    kv_out = kv_out.reshape(16, 1, rows, HD)
    got = lax.all_to_all(jnp.concatenate([q_out, kv_out], axis=1), CTX, 0, 0, tiled=True)
    q_in = got[:, 0].reshape(16 * rows, HD)
    mine = got[:, 1].reshape(16 * rows, HD)
    other = from_next(mine, "core", 1)
    out, q_pos, k_pos, v_pos, log_total = attend(block_place, ends, core_flag, q_in, mine, other)
    attended = lax.all_to_all(out.reshape(16, rows, HD), CTX, 0, 0, tiled=True)
    attended = attended.reshape(4, 4, rows, HD).transpose(0, 2, 1, 3).reshape(4 * rows, 4 * HD)

    o_cat = jnp.concatenate([o_weight, partner_shard(o_weight)], axis=0)
    middle = residual + scatter_y(dot(attended, o_cat).reshape(4, rows, -1))
    hidden = rms_scale(middle, mlp_gain).astype(BF16)
    hidden_all = gather_y(hidden).reshape(4 * rows, -1)
    gate_up_own = jnp.concatenate([gate_weight, up_weight], axis=1)
    gate_up = jnp.concatenate([gate_up_own, partner_shard(gate_up_own)], axis=1)
    down_cat = jnp.concatenate([down_weight, partner_shard(down_weight)], axis=0)
    cot_all = gather_y(cotangent[0]).reshape(4 * rows, -1)
    act_grad = dot(cot_all, down_cat, ((1,), (1,)))
    width = gate_weight.shape[1]
    pre = dot(hidden_all, gate_up).reshape(4 * rows, 2, 2, width)
    gate_pre = pre[:, :, 0].reshape(4 * rows, 2 * width)
    up_pre = pre[:, :, 1].reshape(4 * rows, 2 * width)
    activation, silu_back = jax.vjp(lambda g, u: jax.nn.silu(g) * u, gate_pre, up_pre)
    activation = activation.astype(BF16)
    gate_grad, up_grad = silu_back(act_grad)
    gate_up_grad = jnp.stack(
        [gate_grad.reshape(-1, 2, width), up_grad.reshape(-1, 2, width)], axis=2
    )
    gate_up_grad = gate_up_grad.reshape(4 * rows, 4 * width).astype(BF16)
    hidden_grad = scatter_y(dot(gate_up_grad, gate_up, ((1,), (1,))).reshape(4, rows, -1))
    _, second_back = jax.vjp(rms_scale, middle, mlp_gain)
    middle_part, mlp_gain_grad = second_back(hidden_grad)
    middle_grad = cotangent[0].astype(F32) + middle_part
    branch_grad = middle_grad.astype(BF16)
    branch_all = gather_y(branch_grad).reshape(4 * rows, -1)
    attended_grad = dot(branch_all, o_cat, ((1,), (1,))).astype(BF16)
    grad_out = attended_grad.reshape(4, rows, 4, HD).transpose(0, 2, 1, 3).reshape(16, rows, HD)
    grad_in = lax.all_to_all(grad_out, CTX, 0, 0, tiled=True).reshape(16 * rows, HD)
    q_grad, keep_grad, send_grad = attend_back(
        block_place, ends, core_flag, grad_in, q_pos, k_pos, v_pos, log_total
    )
    kv_grad = (keep_grad + from_next(send_grad, "core", 1).astype(F32)).astype(BF16)
    back = jnp.stack([q_grad.reshape(16, rows, HD), kv_grad.reshape(16, rows, HD)], axis=1)
    back = lax.all_to_all(back, CTX, 0, 0, tiled=True)
    query_grad = back[:, 0].reshape(4, 4, rows, HD).transpose(0, 2, 1, 3).astype(F32)
    kv_back = back[:, 1].reshape(4, 2, 2, rows, HD)
    key_grad = kv_back[:, :, 0].transpose(0, 2, 1, 3).astype(F32)
    value_low = kv_back[:, :, 1].transpose(0, 2, 1, 3)
    _, query_back = jax.vjp(lambda u, g: head_prep(u, g, cos_rows, sin_rows), q_raw, q_gain)
    q_raw_grad, q_gain_grad = query_back(query_grad)
    _, key_back = jax.vjp(lambda u, g: head_prep(u, g, cos_rows, sin_rows), k_raw, k_gain)
    k_raw_grad, k_gain_grad = key_back(key_grad)
    low = jnp.concatenate(
        [
            q_raw_grad.astype(BF16).reshape(4, rows, 2, 2, HD),
            k_raw_grad.astype(BF16)[:, :, :, None],
            value_low[:, :, :, None],
        ],
        axis=3,
    ).reshape(4 * rows, 8 * HD)
    normed_grad = scatter_y(dot(low, qkv_cat, ((1,), (1,))).reshape(4, rows, -1))
    _, first_back = jax.vjp(rms_scale, residual, attn_gain)
    residual_part, attn_gain_grad = first_back(normed_grad)
    tokens_grad = (middle_grad + residual_part).astype(BF16)[None]

    mlp_out = scatter_y(dot(activation, down_cat).reshape(4, rows, -1))
    out_rows = (middle + mlp_out).astype(BF16)[None]

    gate_up_wgrad = weight_grad(hidden_all, gate_up_grad)
    down_wgrad = weight_grad(cot_all, activation)
    o_wgrad = weight_grad(branch_all, attended)
    qkv_wgrad = weight_grad(normed_all, low)
    gains = sum_all(jnp.concatenate([attn_gain_grad, q_gain_grad, k_gain_grad, mlp_gain_grad]))
    d = attn_gain.shape[0]
    return (
        out_rows,
        tokens_grad,
        gains[:d],
        qkv_wgrad[:, : 2 * HD],
        qkv_wgrad[:, 2 * HD : 3 * HD],
        qkv_wgrad[:, 3 * HD :],
        gains[d : d + HD],
        gains[d + HD : d + 2 * HD],
        o_wgrad.T,
        gains[d + 2 * HD :],
        gate_up_wgrad[:, :width],
        gate_up_wgrad[:, width:],
        down_wgrad.T,
    )


def solution(mesh):
    fine = Mesh(mesh.devices.reshape(SIZES), AXES)
    rows = P(FSDP, CTX, None)
    in_specs = (
        rows,
        rows,
        P(),
        P(None, FSDP),
        P(None, FSDP),
        P(None, FSDP),
        P(),
        P(),
        P(FSDP, None),
        P(),
        P(None, FSDP),
        P(None, FSDP),
        P(FSDP, None),
        P(),
        P(),
    )
    out_specs = (
        rows,
        rows,
        P(),
        P(CTX, FSDP),
        P(CTX, FSDP),
        P(CTX, FSDP),
        P(),
        P(),
        P(FSDP, CTX),
        P(),
        P(CTX, FSDP),
        P(CTX, FSDP),
        P(FSDP, CTX),
    )
    return jax.shard_map(
        per_device, mesh=fine, in_specs=in_specs, out_specs=out_specs, check_vma=False
    )
```

```python
import jax
import jax.numpy as jnp
from jax import lax
from jax.experimental import pallas as pl
from jax.experimental.pallas import tpu as pltpu
from jax.sharding import Mesh, PartitionSpec as P

EPSILON = 1e-06
ROPE_BASE = 1000000.0
MASKED_SCORE = -1e30
HD = 128
BLK = 64
AXES = ("zl", "x", "core", "zh", "y")
SIZES = (2, 4, 2, 2, 4)
CTX = ("zl", "x", "core")
FSDP = ("zh", "y")
F32 = jnp.float32
BF16 = jnp.bfloat16


def rms_scale(values, gain_vec):
    inverse = lax.rsqrt(jnp.mean(values * values, axis=-1, keepdims=True) + EPSILON)
    return values * inverse * gain_vec


def head_prep(values, gain_vec, cos_table, sin_table):
    scaled = rms_scale(values, gain_vec)
    midway = scaled.shape[-1] // 2
    turned = jnp.concatenate([-scaled[..., midway:], scaled[..., :midway]], axis=-1)
    return scaled * cos_table + turned * sin_table


def tables(positions, head_dim):
    exponent_steps = jnp.arange(head_dim // 2, dtype=jnp.int32).astype(F32) * (2.0 / head_dim)
    frequency = ROPE_BASE ** (-exponent_steps)
    phases = positions.astype(F32)[:, None] * frequency[None, :]
    phases = jnp.concatenate([phases, phases], axis=-1)
    return (jnp.cos(phases), jnp.sin(phases))


def dot(left, right, contract=((1,), (0,))):
    return lax.dot_general(left, right, (contract, ((), ())), preferred_element_type=F32)


def from_next(value, axis, step):
    size = dict(zip(AXES, SIZES))[axis]
    return lax.ppermute(value, axis, [((i + step) % size, i) for i in range(size)])


def along_z(value, source):
    place = [(z % 2) * 2 + z // 2 for z in range(4)]
    return lax.ppermute(value, ("zl", "zh"), [(place[source(z)], place[z]) for z in range(4)])


def from_next_z(value, step):
    return along_z(value, lambda z: (z + step) % 4)


def gather_y(rows):
    return jnp.stack([rows] + [from_next(rows, "y", k) for k in (1, 2, 3)])


def scatter_y(parts):
    total = parts[0]
    for k in (1, 2, 3):
        total = total + from_next(parts[k].astype(BF16), "y", 4 - k).astype(F32)
    return total


def partner_shard(shard):
    rows, cols = shard.shape
    eighth = rows // 8
    x, core = lax.axis_index("x"), lax.axis_index("core")
    piece = lax.dynamic_slice_in_dim(shard, (x * 2 + core) * eighth, eighth, 0)
    piece = along_z(piece, lambda z: 3 - z)
    ring = jnp.stack([piece] + [from_next(piece, "x", k) for k in (1, 2, 3)])
    other = from_next(ring, "core", 1)
    low = jnp.where(core == 0, ring, other)
    high = jnp.where(core == 0, other, ring)
    both = jnp.stack([low, high], axis=1)
    both = jnp.concatenate([both, both], axis=0)
    both = lax.dynamic_slice_in_dim(both, lax.rem(4 - x, 4), 4, 0)
    return both.reshape(rows, cols)


def weight_grad(left, right):
    rows, width = left.shape
    n = right.shape[1] // 2
    x, core = lax.axis_index("x"), lax.axis_index("core")
    z = lax.axis_index("zh") * 2 + lax.axis_index("zl")
    zh = lax.axis_index("zh")
    split = left.reshape(rows, 8, 2, width // 16)
    theirs = lax.dynamic_index_in_dim(split, 1 - core, 2, keepdims=False).reshape(rows, width // 2)
    mine = lax.dynamic_index_in_dim(split, core, 2, keepdims=False).reshape(rows, width // 2)
    sent = dot(theirs, right, ((0,), (0,))).astype(BF16)
    got = from_next(sent, "core", 1)
    part = (dot(mine, right, ((0,), (0,))) + got.astype(F32)).astype(BF16)
    part = part.reshape(2, 4, width // 16, 2 * n)

    def for_x(k):
        return lax.dynamic_index_in_dim(part, lax.rem(x + k, 4), 1, keepdims=False)

    total = for_x(0).astype(F32)
    for k in (1, 2, 3):
        total = total + from_next(for_x(k), "x", 4 - k).astype(F32)
    part = total.astype(BF16)
    part = part.reshape(2, width // 16, 2, n)

    def for_z(k):
        dest = lax.rem(z + k, 4)
        rows_of = lax.dynamic_index_in_dim(part, lax.rem(dest, 2), 0, keepdims=False)
        side = jnp.where(dest // 2 == zh, 0, 1)
        return lax.dynamic_index_in_dim(rows_of, side, 1, keepdims=False)

    total = for_z(0).astype(F32)
    for k in (1, 2, 3):
        total = total + from_next_z(for_z(k), 4 - k).astype(F32)
    return total


def sum_all(vector):
    for axis, steps in (("y", (1, 2, 3)), ("x", (1, 2, 3)), ("core", (1,))):
        vector = vector + sum(from_next(vector, axis, k) for k in steps)
    return vector + sum(from_next_z(vector, k) for k in (1, 2, 3))


TILE = 256


def keep_mask(ends, first_row, rows, cols):
    place = first_row + lax.broadcasted_iota(jnp.int32, (rows, 1), 0)
    start = jnp.zeros((rows, 1), jnp.int32)
    for j in range(ends.shape[0]):
        start = jnp.where(place >= ends[j], ends[j], start)
    key = lax.broadcasted_iota(jnp.int32, (rows, cols), 1)
    return (key >= start) & (key <= place)


def attend_kernel(place, ends, core, q_in, mine, other, out, q_pos, k_pos, v_pos, log_total, out_pos):
    rows = q_in.shape[0]
    blocks = rows // BLK
    scale = HD ** (-0.5)

    @pl.when(core[0] == 0)
    def _():
        @pl.loop(0, blocks)
        def _(b):
            src = pl.ds(pl.multiple_of(b * BLK, BLK), BLK)
            dst = pl.ds(pl.multiple_of(place[b] * BLK, BLK), BLK)
            q_pos[dst, :] = q_in[src, :]
            k_pos[dst, :] = mine[src, :]
            v_pos[dst, :] = other[src, :]

    @pl.when(core[0] == 1)
    def _():
        @pl.loop(0, blocks)
        def _(b):
            src = pl.ds(pl.multiple_of(b * BLK, BLK), BLK)
            dst = pl.ds(pl.multiple_of(place[b] * BLK, BLK), BLK)
            q_pos[dst, :] = q_in[src, :]
            k_pos[dst, :] = other[src, :]
            v_pos[dst, :] = mine[src, :]

    for i in range(rows // TILE):
        span = pl.ds(i * TILE, TILE)
        n = (i + 1) * TILE
        scores = dot(q_pos[span, :], k_pos[:n, :], ((1,), (1,))) * scale
        scores = jnp.where(keep_mask(ends, i * TILE, TILE, n), scores, MASKED_SCORE)
        top = jnp.max(scores, axis=-1, keepdims=True)
        weights = jnp.exp(scores - top)
        total = jnp.sum(weights, axis=-1, keepdims=True)
        log_total[span, :] = top + jnp.log(total)
        probs = (weights * (1.0 / total)).astype(BF16)
        out_pos[span, :] = dot(probs, v_pos[:n, :]).astype(BF16)

    @pl.loop(0, blocks)
    def _(b):
        src = pl.ds(pl.multiple_of(b * BLK, BLK), BLK)
        dst = pl.ds(pl.multiple_of(place[b] * BLK, BLK), BLK)
        out[src, :] = out_pos[dst, :]


def attend_back_kernel(
    place, ends, core, grad_in, q_pos, k_pos, v_pos, log_total, q_grad, keep_grad, send_grad,
    grad_pos, q_acc, k_acc, v_acc,
):
    rows = grad_in.shape[0]
    blocks = rows // BLK
    scale = HD ** (-0.5)

    @pl.loop(0, blocks)
    def _(b):
        src = pl.ds(pl.multiple_of(b * BLK, BLK), BLK)
        dst = pl.ds(pl.multiple_of(place[b] * BLK, BLK), BLK)
        grad_pos[dst, :] = grad_in[src, :]

    k_acc[...] = jnp.zeros_like(k_acc)
    v_acc[...] = jnp.zeros_like(v_acc)
    for i in range(rows // TILE):
        span = pl.ds(i * TILE, TILE)
        n = (i + 1) * TILE
        queries = q_pos[span, :]
        grads = grad_pos[span, :]
        scores = dot(queries, k_pos[:n, :], ((1,), (1,))) * scale
        kept = keep_mask(ends, i * TILE, TILE, n)
        probs = jnp.where(kept, jnp.exp(scores - log_total[span, :]), 0.0)
        prob_grad = dot(grads, v_pos[:n, :], ((1,), (1,)))
        row_dot = jnp.sum(prob_grad * probs, axis=-1, keepdims=True)
        score_grad = (probs * (prob_grad - row_dot)).astype(BF16)
        q_acc[span, :] = (dot(score_grad, k_pos[:n, :]) * scale).astype(BF16)
        k_acc[:n, :] += dot(score_grad, queries, ((0,), (0,)))
        v_acc[:n, :] += dot(probs.astype(BF16), grads, ((0,), (0,)))

    @pl.loop(0, blocks)
    def _(b):
        src = pl.ds(pl.multiple_of(b * BLK, BLK), BLK)
        dst = pl.ds(pl.multiple_of(place[b] * BLK, BLK), BLK)
        q_grad[src, :] = q_acc[dst, :]
        k_rows = k_acc[dst, :] * scale
        v_rows = v_acc[dst, :]
        first = core[0] == 0
        keep_grad[src, :] = jnp.where(first, k_rows, v_rows)
        send_grad[src, :] = jnp.where(first, v_rows, k_rows).astype(BF16)


def attend(place, ends, core, q_in, mine, other):
    rows = q_in.shape[0]
    low = jax.ShapeDtypeStruct((rows, HD), BF16)
    smem = pl.BlockSpec(memory_space=pltpu.SMEM)
    vmem = pl.BlockSpec(memory_space=pltpu.VMEM)
    return pl.pallas_call(
        attend_kernel,
        out_shape=(low, low, low, low, jax.ShapeDtypeStruct((rows, 1), F32)),
        in_specs=[smem] * 3 + [vmem] * 3,
        out_specs=(vmem,) * 5,
        scratch_shapes=[pltpu.VMEM((rows, HD), BF16)],
        compiler_params=pltpu.CompilerParams(vmem_limit_bytes=40 * 2**20),
        cost_estimate=pl.CostEstimate(
            flops=2 * rows * rows * HD, bytes_accessed=rows * HD * 16, transcendentals=rows * rows // 2
        ),
        name="attend",
    )(place, ends, core, q_in, mine, other)


def attend_back(place, ends, core, grad_in, q_pos, k_pos, v_pos, log_total):
    rows = grad_in.shape[0]
    low = jax.ShapeDtypeStruct((rows, HD), BF16)
    smem = pl.BlockSpec(memory_space=pltpu.SMEM)
    vmem = pl.BlockSpec(memory_space=pltpu.VMEM)
    return pl.pallas_call(
        attend_back_kernel,
        out_shape=(low, jax.ShapeDtypeStruct((rows, HD), F32), low),
        in_specs=[smem] * 3 + [vmem] * 5,
        out_specs=(vmem,) * 3,
        scratch_shapes=[
            pltpu.VMEM((rows, HD), BF16),
            pltpu.VMEM((rows, HD), BF16),
            pltpu.VMEM((rows, HD), F32),
            pltpu.VMEM((rows, HD), F32),
        ],
        compiler_params=pltpu.CompilerParams(vmem_limit_bytes=48 * 2**20),
        cost_estimate=pl.CostEstimate(
            flops=5 * rows * rows * HD, bytes_accessed=rows * HD * 20, transcendentals=rows * rows // 2
        ),
        name="attend_back",
    )(place, ends, core, grad_in, q_pos, k_pos, v_pos, log_total)


def peers(pairs):
    barrier = pltpu.get_barrier_semaphore()
    for place in pairs:
        pl.semaphore_signal(barrier, inc=1, device_id=place, device_id_type=pl.DeviceIdType.MESH)
    pl.semaphore_wait(barrier, len(pairs))


def remote(src, dst, sent, landed, place):
    return pltpu.make_async_remote_copy(
        src_ref=src, dst_ref=dst, send_sem=sent, recv_sem=landed, device_id=place,
        device_id_type=pl.DeviceIdType.MESH,
    )


ROWS = 128
WIDE = 256


def mlp_kernel(
    middle, cot, gain, cot_hbm, gate_hbm, up_hbm, down_hbm,
    middle_grad, branch, gain_grad, part_hbm, wgrad_hbm,
    hid, cots, gate_w, up_w, down_w, act_grad, gu_grad, act, parts, got, z_out, z_got, part, stage,
    load_sem, sent, landed, sent_back, landed_back, stage_sem, part_sem,
):
    y, zh = lax.axis_index("y"), lax.axis_index("zh")
    half = 4 * ROWS
    width = gate_w.shape[1]
    model = hid.shape[1]

    def along(k):
        return {"y": lax.rem(y + k, 4)}

    across = {"zh": 1 - zh}
    loads = [
        pltpu.make_async_copy(src, dst, load_sem.at[i])
        for i, (src, dst) in enumerate(
            ((cot_hbm, cots), (down_hbm, down_w), (gate_hbm, gate_w), (up_hbm, up_w))
        )
    ]
    for load in loads:
        load.start()

    rows_in = middle[...]
    inverse = lax.rsqrt(jnp.mean(rows_in * rows_in, axis=-1, keepdims=True) + EPSILON)
    hid[:ROWS, :] = (rows_in * inverse * gain[...]).astype(BF16)
    peers([along(1), along(2), along(3), across])

    def slot(r):
        return hid.at[pl.ds(r * ROWS, ROWS), :]

    out = []
    for k in (1, 3, 2):
        out.append(remote(slot(0), slot(4 - k), sent.at[k], landed.at[4 - k], along(k)))
    out.append(remote(slot(0), slot(4), sent.at[4], landed.at[4], across))
    for copy in out:
        copy.start()

    def grads_of_cot(first):
        rows = pl.ds(first, half)

        @pl.loop(0, width // WIDE)
        def _(n):
            cols = pl.ds(pl.multiple_of(n * WIDE, WIDE), WIDE)
            act_grad[rows, cols] = dot(cots[rows, :], down_w[cols, :], ((1,), (1,)))

    loads[0].wait()
    loads[1].wait()
    grads_of_cot(0)
    loads[2].wait()
    loads[3].wait()
    grads_of_cot(half)

    out[3].wait_recv()
    on = []
    for k in (1, 3, 2):
        on.append(remote(slot(4), slot(8 - k), sent.at[4 + k], landed.at[8 - k], along(k)))
    for copy in on:
        copy.start()

    def forward(first):
        rows = pl.ds(first, half)

        @pl.loop(0, width // WIDE)
        def _(n):
            cols = pl.ds(pl.multiple_of(n * WIDE, WIDE), WIDE)
            gate = dot(hid[rows, :], gate_w[:, cols])
            up = dot(hid[rows, :], up_w[:, cols])
            sig = jax.nn.sigmoid(gate)
            silu = gate * sig
            grad = act_grad[rows, cols]
            act[rows, cols] = (silu * up).astype(BF16)
            gu_grad[rows, cols] = (grad * up * sig * (1.0 + gate * (1.0 - sig))).astype(BF16)
            gu_grad[rows, pl.ds(pl.multiple_of(width + n * WIDE, WIDE), WIDE)] = (grad * silu).astype(BF16)

    def backward(first):
        rows = pl.ds(first, half)

        @pl.loop(0, model // WIDE)
        def _(n):
            cols = pl.ds(pl.multiple_of(n * WIDE, WIDE), WIDE)
            total = dot(gu_grad[rows, :width], gate_w[cols, :], ((1,), (1,)))
            total += dot(gu_grad[rows, width:], up_w[cols, :], ((1,), (1,)))
            parts[rows, cols] = total.astype(BF16)

    def share(r):
        return parts.at[pl.ds(r * ROWS, ROWS), :]

    def got_at(r):
        return got.at[pl.ds(r * ROWS, ROWS), :]

    for copy in out[:3]:
        copy.wait_recv()
    forward(0)
    backward(0)
    for copy in on:
        copy.wait_recv()
    forward(half)
    backward(half)
    back = {}
    for r in (4, 0):
        for k in (1, 3, 2):
            copy = remote(share(r + k), got_at(r + 4 - k), sent_back.at[r + k], landed_back.at[r + 4 - k], along(k))
            copy.start()
            back[r + 4 - k] = copy

    def down_part(first):
        rows = pl.ds(first, half)

        @pl.loop(0, model // WIDE)
        def _(n):
            cols = pl.ds(pl.multiple_of(n * WIDE, WIDE), WIDE)
            part[rows, cols] = dot(act[rows, :], down_w[:, cols]).astype(BF16)

    down_part(0)
    down_part(half)
    part_copy = pltpu.make_async_copy(part, part_hbm, part_sem)
    part_copy.start()

    def stage_copy(b, n):
        rows = pl.ds(pl.multiple_of(n * WIDE, WIDE), WIDE)
        return pltpu.make_async_copy(stage.at[b], wgrad_hbm.at[rows, :], stage_sem.at[b])

    def weight_grads(begin, end):
        @pl.loop(begin, end)
        def _(m):
            for b in range(2):
                n = m * 2 + b
                cols = pl.ds(pl.multiple_of(n * WIDE, WIDE), WIDE)

                @pl.when(m > 0)
                def _():
                    stage_copy(b, n - 2).wait()

                stage[b, :, : 2 * width] = dot(hid[:, cols], gu_grad[...], ((0,), (0,))).astype(BF16)
                stage[b, :, 2 * width :] = dot(cots[:, cols], act[...], ((0,), (0,))).astype(BF16)
                stage_copy(b, n).start()

    steps = model // WIDE // 2
    weight_grads(0, steps // 2)
    for k in (1, 2, 3):
        back[4 + k].wait_recv()

    def summed(r):
        total = parts[pl.ds(r * ROWS, ROWS), :].astype(F32)
        for k in (1, 2, 3):
            total += got[pl.ds((r + k) * ROWS, ROWS), :].astype(F32)
        return total

    z_out[...] = summed(4).astype(BF16)
    z_copy = remote(z_out, z_got, sent_back.at[0], landed_back.at[0], across)
    z_copy.start()
    weight_grads(steps // 2, steps)
    for k in (1, 2, 3):
        back[k].wait_recv()
    z_copy.wait_recv()

    grad = summed(0) + z_got[...].astype(F32)
    rows_in = middle[...]
    inverse = lax.rsqrt(jnp.mean(rows_in * rows_in, axis=-1, keepdims=True) + EPSILON)
    gain_grad[...] = jnp.sum(grad * rows_in * inverse, axis=0, keepdims=True)
    scaled = grad * gain[...]
    inner = jnp.mean(rows_in * scaled, axis=-1, keepdims=True)
    total = cot[...].astype(F32) + inverse * scaled - rows_in * (inverse * inverse * inverse * inner)
    middle_grad[...] = total
    branch[...] = total.astype(BF16)

    for copy in out + on:
        copy.wait_send()
    for copy in back.values():
        copy.wait_send()
    z_copy.wait_send()
    part_copy.wait()
    for b in range(2):
        stage_copy(b, 2 * steps - 2 + b).wait()


def mlp(middle, cot, gain, cot_all, gate_w, up_w, down_w):
    rows, model = middle.shape
    width = gate_w.shape[1]
    anywhere = pl.BlockSpec(memory_space=pl.ANY)
    vmem = pl.BlockSpec(memory_space=pltpu.VMEM)
    dma = pltpu.SemaphoreType.DMA
    return pl.pallas_call(
        mlp_kernel,
        out_shape=(
            jax.ShapeDtypeStruct((rows, model), F32),
            jax.ShapeDtypeStruct((rows, model), BF16),
            jax.ShapeDtypeStruct((1, model), F32),
            jax.ShapeDtypeStruct((8 * rows, model), BF16),
            jax.ShapeDtypeStruct((model, 3 * width), BF16),
        ),
        in_specs=[vmem] * 3 + [anywhere] * 4,
        out_specs=(vmem, vmem, vmem, anywhere, anywhere),
        scratch_shapes=[
            pltpu.VMEM((8 * rows, model), BF16),
            pltpu.VMEM((8 * rows, model), BF16),
            pltpu.VMEM((model, width), BF16),
            pltpu.VMEM((model, width), BF16),
            pltpu.VMEM((width, model), BF16),
            pltpu.VMEM((8 * rows, width), F32),
            pltpu.VMEM((8 * rows, 2 * width), BF16),
            pltpu.VMEM((8 * rows, width), BF16),
            pltpu.VMEM((8 * rows, model), BF16),
            pltpu.VMEM((8 * rows, model), BF16),
            pltpu.VMEM((rows, model), BF16),
            pltpu.VMEM((rows, model), BF16),
            pltpu.VMEM((8 * rows, model), BF16),
            pltpu.VMEM((2, WIDE, 3 * width), BF16),
            dma((4,)),
            dma((8,)),
            dma((8,)),
            dma((8,)),
            dma((8,)),
            dma((2,)),
            dma,
        ],
        compiler_params=pltpu.CompilerParams(
            collective_id=1, has_side_effects=True, vmem_limit_bytes=58 * 2**20
        ),
        cost_estimate=pl.CostEstimate(
            flops=2 * 9 * 8 * rows * model * width, bytes_accessed=40 * 2**20, transcendentals=8 * rows * width
        ),
        name="mlp",
    )(middle, cot, gain.reshape(1, model), cot_all, gate_w, up_w, down_w)


def per_device(
    tokens,
    cotangent,
    attn_gain,
    q_weight,
    k_weight,
    v_weight,
    q_gain,
    k_gain,
    o_weight,
    mlp_gain,
    gate_weight,
    up_weight,
    down_weight,
    doc_lengths,
    block_place,
):
    rows = tokens.shape[1]
    zl, x, core = (lax.axis_index(a) for a in CTX)
    zh, y = (lax.axis_index(a) for a in FSDP)
    ctx_place = zl * 8 + x * 2 + core
    sequence = zh * 4 + lax.rem(y + ctx_place // 4, 4)
    ends = jnp.cumsum(lax.dynamic_index_in_dim(doc_lengths, sequence, 0, keepdims=False))
    ends = ends.astype(jnp.int32)
    core_flag = core.astype(jnp.int32).reshape(1)
    own_blocks = lax.dynamic_slice_in_dim(block_place, ctx_place * (rows // BLK), rows // BLK)
    own_positions = (own_blocks[:, None] * BLK + jnp.arange(BLK, dtype=jnp.int32)[None, :]).reshape(-1)
    cos_rows, sin_rows = tables(own_positions, HD)
    cos_rows = cos_rows[None, :, None, :]
    sin_rows = sin_rows[None, :, None, :]

    residual = tokens[0].astype(F32)
    normed = rms_scale(residual, attn_gain).astype(BF16)
    normed_all = gather_y(normed).reshape(4 * rows, -1)
    pair = jnp.stack([cotangent[0], from_next(cotangent[0], "zh", 1)])
    cot_all = jnp.stack([pair] + [from_next(pair, "y", k) for k in (1, 2, 3)], axis=1).reshape(8 * rows, -1)
    qkv_own = jnp.concatenate([q_weight, k_weight, v_weight], axis=1)
    qkv_cat = jnp.concatenate([qkv_own, partner_shard(qkv_own)], axis=1)
    raw = dot(normed_all, qkv_cat)
    raw = raw.reshape(4, rows, 2, 4, HD)
    q_raw = raw[:, :, :, :2].reshape(4, rows, 4, HD)
    k_raw = raw[:, :, :, 2]
    values = raw[:, :, :, 3].astype(BF16)
    queries = head_prep(q_raw, q_gain, cos_rows, sin_rows).astype(BF16)
    keys = head_prep(k_raw, k_gain, cos_rows, sin_rows).astype(BF16)
    q_out = queries.transpose(0, 2, 1, 3).reshape(16, 1, rows, HD)
    kv_out = jnp.stack([keys.transpose(0, 2, 1, 3), values.transpose(0, 2, 1, 3)], axis=2)
    kv_out = kv_out.reshape(16, 1, rows, HD)
    got = lax.all_to_all(jnp.concatenate([q_out, kv_out], axis=1), CTX, 0, 0, tiled=True)
    q_in = got[:, 0].reshape(16 * rows, HD)
    mine = got[:, 1].reshape(16 * rows, HD)
    other = from_next(mine, "core", 1)
    out, q_pos, k_pos, v_pos, log_total = attend(block_place, ends, core_flag, q_in, mine, other)
    attended = lax.all_to_all(out.reshape(16, rows, HD), CTX, 0, 0, tiled=True)
    attended = attended.reshape(4, 4, rows, HD).transpose(0, 2, 1, 3).reshape(4 * rows, 4 * HD)

    o_cat = jnp.concatenate([o_weight, partner_shard(o_weight)], axis=0)
    middle = residual + scatter_y(dot(attended, o_cat).reshape(4, rows, -1))
    middle_grad, branch_grad, mlp_gain_grad, mlp_part, mlp_wgrad = mlp(
        middle, cotangent[0], mlp_gain, cot_all, gate_weight, up_weight, down_weight
    )
    branch_all = gather_y(branch_grad).reshape(4 * rows, -1)
    attended_grad = dot(branch_all, o_cat, ((1,), (1,))).astype(BF16)
    grad_out = attended_grad.reshape(4, rows, 4, HD).transpose(0, 2, 1, 3).reshape(16, rows, HD)
    grad_in = lax.all_to_all(grad_out, CTX, 0, 0, tiled=True).reshape(16 * rows, HD)
    q_grad, keep_grad, send_grad = attend_back(
        block_place, ends, core_flag, grad_in, q_pos, k_pos, v_pos, log_total
    )
    kv_grad = (keep_grad + from_next(send_grad, "core", 1).astype(F32)).astype(BF16)
    back = jnp.stack([q_grad.reshape(16, rows, HD), kv_grad.reshape(16, rows, HD)], axis=1)
    back = lax.all_to_all(back, CTX, 0, 0, tiled=True)
    query_grad = back[:, 0].reshape(4, 4, rows, HD).transpose(0, 2, 1, 3).astype(F32)
    kv_back = back[:, 1].reshape(4, 2, 2, rows, HD)
    key_grad = kv_back[:, :, 0].transpose(0, 2, 1, 3).astype(F32)
    value_low = kv_back[:, :, 1].transpose(0, 2, 1, 3)
    _, query_back = jax.vjp(lambda u, g: head_prep(u, g, cos_rows, sin_rows), q_raw, q_gain)
    q_raw_grad, q_gain_grad = query_back(query_grad)
    _, key_back = jax.vjp(lambda u, g: head_prep(u, g, cos_rows, sin_rows), k_raw, k_gain)
    k_raw_grad, k_gain_grad = key_back(key_grad)
    low = jnp.concatenate(
        [
            q_raw_grad.astype(BF16).reshape(4, rows, 2, 2, HD),
            k_raw_grad.astype(BF16)[:, :, :, None],
            value_low[:, :, :, None],
        ],
        axis=3,
    ).reshape(4 * rows, 8 * HD)
    normed_grad = scatter_y(dot(low, qkv_cat, ((1,), (1,))).reshape(4, rows, -1))
    _, first_back = jax.vjp(rms_scale, residual, attn_gain)
    residual_part, attn_gain_grad = first_back(normed_grad)
    tokens_grad = (middle_grad + residual_part).astype(BF16)[None]

    mlp_part = mlp_part.reshape(2, 4, rows, -1)
    mlp_sum = mlp_part[:, 0].astype(F32)
    for k in (1, 2, 3):
        mlp_sum = mlp_sum + from_next(mlp_part[:, k], "y", 4 - k).astype(F32)
    mlp_out = mlp_sum[0] + from_next(mlp_sum[1].astype(BF16), "zh", 1).astype(F32)
    out_rows = (middle + mlp_out).astype(BF16)[None]
    mlp_wgrad = lax.psum_scatter(mlp_wgrad, CTX, scatter_dimension=0, tiled=True).astype(F32)
    width = gate_weight.shape[1]

    o_wgrad = weight_grad(branch_all, attended)
    qkv_wgrad = weight_grad(normed_all, low)
    gains = sum_all(jnp.concatenate([attn_gain_grad, q_gain_grad, k_gain_grad, mlp_gain_grad[0]]))
    d = attn_gain.shape[0]
    return (
        out_rows,
        tokens_grad,
        gains[:d],
        qkv_wgrad[:, : 2 * HD],
        qkv_wgrad[:, 2 * HD : 3 * HD],
        qkv_wgrad[:, 3 * HD :],
        gains[d : d + HD],
        gains[d + HD : d + 2 * HD],
        o_wgrad.T,
        gains[d + 2 * HD :],
        mlp_wgrad[:, :width],
        mlp_wgrad[:, width : 2 * width],
        mlp_wgrad[:, 2 * width :].T,
    )


def solution(mesh):
    fine = Mesh(mesh.devices.reshape(SIZES), AXES)
    rows = P(FSDP, CTX, None)
    in_specs = (
        rows,
        rows,
        P(),
        P(None, FSDP),
        P(None, FSDP),
        P(None, FSDP),
        P(),
        P(),
        P(FSDP, None),
        P(),
        P(None, FSDP),
        P(None, FSDP),
        P(FSDP, None),
        P(),
        P(),
    )
    out_specs = (
        rows,
        rows,
        P(),
        P(CTX, FSDP),
        P(CTX, FSDP),
        P(CTX, FSDP),
        P(),
        P(),
        P(FSDP, CTX),
        P(),
        P(CTX, FSDP),
        P(CTX, FSDP),
        P(FSDP, CTX),
    )
    return jax.shard_map(
        per_device, mesh=fine, in_specs=in_specs, out_specs=out_specs, check_vma=False
    )
```

```python
import functools

import jax
import jax.numpy as jnp
from jax import lax
from jax.experimental import pallas as pl
from jax.experimental.pallas import tpu as pltpu
from jax.sharding import Mesh, PartitionSpec as P

EPSILON = 1e-06
ROPE_BASE = 1000000.0
MASKED_SCORE = -1e30
HD = 128
BLK = 64
AXES = ("zl", "x", "core", "zh", "y")
SIZES = (2, 4, 2, 2, 4)
CTX = ("zl", "x", "core")
FSDP = ("zh", "y")
F32 = jnp.float32
BF16 = jnp.bfloat16


def tables(positions, head_dim):
    exponent_steps = jnp.arange(head_dim // 2, dtype=jnp.int32).astype(F32) * (2.0 / head_dim)
    frequency = ROPE_BASE ** (-exponent_steps)
    phases = positions.astype(F32)[:, None] * frequency[None, :]
    phases = jnp.concatenate([phases, phases], axis=-1)
    return (jnp.cos(phases), jnp.sin(phases))


def dot(left, right, contract=((1,), (0,))):
    return lax.dot_general(left, right, (contract, ((), ())), preferred_element_type=F32)


TILE = 256


def keep_mask(ends, first_row, rows, cols):
    place = first_row + lax.broadcasted_iota(jnp.int32, (rows, 1), 0)
    start = jnp.zeros((rows, 1), jnp.int32)
    for j in range(ends.shape[0]):
        start = jnp.where(place >= ends[j], ends[j], start)
    key = lax.broadcasted_iota(jnp.int32, (rows, cols), 1)
    return (key >= start) & (key <= place)


def attend_kernel(place, ends, core, q_in, mine, other, out, q_pos, k_pos, v_pos, log_total, out_pos):
    rows = q_in.shape[0]
    blocks = rows // BLK
    scale = HD ** (-0.5)

    @pl.when(core[0] == 0)
    def _():
        @pl.loop(0, blocks)
        def _(b):
            src = pl.ds(pl.multiple_of(b * BLK, BLK), BLK)
            dst = pl.ds(pl.multiple_of(place[b] * BLK, BLK), BLK)
            q_pos[dst, :] = q_in[src, :]
            k_pos[dst, :] = mine[src, :]
            v_pos[dst, :] = other[src, :]

    @pl.when(core[0] == 1)
    def _():
        @pl.loop(0, blocks)
        def _(b):
            src = pl.ds(pl.multiple_of(b * BLK, BLK), BLK)
            dst = pl.ds(pl.multiple_of(place[b] * BLK, BLK), BLK)
            q_pos[dst, :] = q_in[src, :]
            k_pos[dst, :] = other[src, :]
            v_pos[dst, :] = mine[src, :]

    for i in range(rows // TILE):
        span = pl.ds(i * TILE, TILE)
        n = (i + 1) * TILE
        scores = dot(q_pos[span, :], k_pos[:n, :], ((1,), (1,))) * scale
        scores = jnp.where(keep_mask(ends, i * TILE, TILE, n), scores, MASKED_SCORE)
        top = jnp.max(scores, axis=-1, keepdims=True)
        weights = jnp.exp(scores - top)
        total = jnp.sum(weights, axis=-1, keepdims=True)
        log_total[span, :] = top + jnp.log(total)
        probs = (weights * (1.0 / total)).astype(BF16)
        out_pos[span, :] = dot(probs, v_pos[:n, :]).astype(BF16)

    @pl.loop(0, blocks)
    def _(b):
        src = pl.ds(pl.multiple_of(b * BLK, BLK), BLK)
        dst = pl.ds(pl.multiple_of(place[b] * BLK, BLK), BLK)
        out[src, :] = out_pos[dst, :]


def attend_back_kernel(
    place, ends, core, grad_in, q_pos, k_pos, v_pos, log_total, q_grad, keep_grad, send_grad,
    grad_pos, q_acc, k_acc, v_acc,
):
    rows = grad_in.shape[0]
    blocks = rows // BLK
    scale = HD ** (-0.5)

    @pl.loop(0, blocks)
    def _(b):
        src = pl.ds(pl.multiple_of(b * BLK, BLK), BLK)
        dst = pl.ds(pl.multiple_of(place[b] * BLK, BLK), BLK)
        grad_pos[dst, :] = grad_in[src, :]

    k_acc[...] = jnp.zeros_like(k_acc)
    v_acc[...] = jnp.zeros_like(v_acc)
    for i in range(rows // TILE):
        span = pl.ds(i * TILE, TILE)
        n = (i + 1) * TILE
        queries = q_pos[span, :]
        grads = grad_pos[span, :]
        scores = dot(queries, k_pos[:n, :], ((1,), (1,))) * scale
        kept = keep_mask(ends, i * TILE, TILE, n)
        probs = jnp.where(kept, jnp.exp(scores - log_total[span, :]), 0.0)
        prob_grad = dot(grads, v_pos[:n, :], ((1,), (1,)))
        row_dot = jnp.sum(prob_grad * probs, axis=-1, keepdims=True)
        score_grad = (probs * (prob_grad - row_dot)).astype(BF16)
        q_acc[span, :] = (dot(score_grad, k_pos[:n, :]) * scale).astype(BF16)
        k_acc[:n, :] += dot(score_grad, queries, ((0,), (0,)))
        v_acc[:n, :] += dot(probs.astype(BF16), grads, ((0,), (0,)))

    @pl.loop(0, blocks)
    def _(b):
        src = pl.ds(pl.multiple_of(b * BLK, BLK), BLK)
        dst = pl.ds(pl.multiple_of(place[b] * BLK, BLK), BLK)
        q_grad[src, :] = q_acc[dst, :]
        k_rows = k_acc[dst, :] * scale
        v_rows = v_acc[dst, :]
        first = core[0] == 0
        keep_grad[src, :] = jnp.where(first, k_rows, v_rows)
        send_grad[src, :] = jnp.where(first, v_rows, k_rows).astype(BF16)


def attend(place, ends, core, q_in, mine, other):
    rows = q_in.shape[0]
    low = jax.ShapeDtypeStruct((rows, HD), BF16)
    smem = pl.BlockSpec(memory_space=pltpu.SMEM)
    vmem = pl.BlockSpec(memory_space=pltpu.VMEM)
    return pl.pallas_call(
        attend_kernel,
        out_shape=(low, low, low, low, jax.ShapeDtypeStruct((rows, 1), F32)),
        in_specs=[smem] * 3 + [vmem] * 3,
        out_specs=(vmem,) * 5,
        scratch_shapes=[pltpu.VMEM((rows, HD), BF16)],
        compiler_params=pltpu.CompilerParams(vmem_limit_bytes=40 * 2**20),
        cost_estimate=pl.CostEstimate(
            flops=2 * rows * rows * HD, bytes_accessed=rows * HD * 16, transcendentals=rows * rows // 2
        ),
        name="attend",
    )(place, ends, core, q_in, mine, other)


def attend_back(place, ends, core, grad_in, q_pos, k_pos, v_pos, log_total):
    rows = grad_in.shape[0]
    low = jax.ShapeDtypeStruct((rows, HD), BF16)
    smem = pl.BlockSpec(memory_space=pltpu.SMEM)
    vmem = pl.BlockSpec(memory_space=pltpu.VMEM)
    return pl.pallas_call(
        attend_back_kernel,
        out_shape=(low, jax.ShapeDtypeStruct((rows, HD), F32), low),
        in_specs=[smem] * 3 + [vmem] * 5,
        out_specs=(vmem,) * 3,
        scratch_shapes=[
            pltpu.VMEM((rows, HD), BF16),
            pltpu.VMEM((rows, HD), BF16),
            pltpu.VMEM((rows, HD), F32),
            pltpu.VMEM((rows, HD), F32),
        ],
        compiler_params=pltpu.CompilerParams(vmem_limit_bytes=48 * 2**20),
        cost_estimate=pl.CostEstimate(
            flops=5 * rows * rows * HD, bytes_accessed=rows * HD * 20, transcendentals=rows * rows // 2
        ),
        name="attend_back",
    )(place, ends, core, grad_in, q_pos, k_pos, v_pos, log_total)


def peers(pairs):
    barrier = pltpu.get_barrier_semaphore()
    for place in pairs:
        pl.semaphore_signal(barrier, inc=1, device_id=place, device_id_type=pl.DeviceIdType.MESH)
    pl.semaphore_wait(barrier, len(pairs))


def remote(src, dst, sent, landed, place):
    return pltpu.make_async_remote_copy(
        src_ref=src, dst_ref=dst, send_sem=sent, recv_sem=landed, device_id=place,
        device_id_type=pl.DeviceIdType.MESH,
    )


ROWS = 128
WIDE = 256


def ctx_at(index):
    return {"zl": index // 8, "x": lax.rem(index // 2, 4), "core": lax.rem(index, 2)}


def block(ref, index):
    return ref.at[pl.ds(pl.multiple_of(index * ROWS, ROWS), ROWS), :]


def inverse_rms(values):
    return lax.rsqrt(jnp.mean(values * values, axis=-1, keepdims=True) + EPSILON)


def rms_back(grad, values, gain):
    inverse = inverse_rms(values)
    scaled = grad * gain
    inner = jnp.mean(values * scaled, axis=-1, keepdims=True)
    back = inverse * scaled - values * (inverse * inverse * inverse * inner)
    return back, jnp.sum(grad * values * inverse, axis=0, keepdims=True)


def pre_kernel(
    tokens, cos, sin, attn_gain, q_gain, k_gain, cot_hbm, q_hbm, k_hbm, v_hbm, o_hbm,
    q_got, mine, other, raw_hbm, normed_hbm, own_hbm, par_hbm, o_par_hbm, cot_got,
    normed, w_own, w_par, o_own, o_par, raw, q_out, kv_out,
    load_sem, y_sent, y_land, cot_sent, cot_land, z_sent, z_land, x_sent, x_land, core_sent, core_land,
    q_sent, q_land, kv_sent, kv_land, swap_sem, local_sem, out_sem,
):
    zl, x, core = (lax.axis_index(a) for a in CTX)
    zh, y = (lax.axis_index(a) for a in FSDP)
    me = zl * 8 + x * 2 + core
    half = 4 * HD
    waits = []

    def along_y(k):
        return {"y": lax.rem(y + k, 4)}

    def along_x(k):
        return {"x": lax.rem(x + k, 4)}

    other_core = {"core": 1 - core}
    cross = {"zl": 1 - zl, "zh": 1 - zh}
    q_width, k_width = q_hbm.shape[1], k_hbm.shape[1]
    pieces = (
        (q_hbm, w_own.at[:, pl.ds(0, q_width)]),
        (k_hbm, w_own.at[:, pl.ds(q_width, k_width)]),
        (v_hbm, w_own.at[:, pl.ds(q_width + k_width, k_width)]),
        (o_hbm, o_own),
    )
    loads = [pltpu.make_async_copy(src, dst, load_sem.at[i]) for i, (src, dst) in enumerate(pieces)]
    for load in loads:
        load.start()
    own_cot = pltpu.make_async_copy(cot_hbm, cot_got.at[pl.ds(0, ROWS), :], local_sem.at[0])
    own_cot.start()
    rows_in = tokens[...].astype(F32)
    normed[:ROWS, :] = (rows_in * inverse_rms(rows_in) * attn_gain[...]).astype(BF16)
    peers([ctx_at(lax.rem(me + k, 16)) for k in range(1, 16)] + [along_y(k) for k in (1, 2, 3)] + [cross])

    y_copies = []
    for k in (1, 3, 2):
        copy = remote(
            normed.at[pl.ds(0, ROWS), :], normed.at[pl.ds((4 - k) * ROWS, ROWS), :], y_sent.at[k], y_land.at[4 - k],
            along_y(k),
        )
        copy.start()
        y_copies.append(copy)
    for load in loads:
        load.wait()

    def shard_stage(src, dst, first):
        eighth = src.shape[0] // 8

        def piece(ref, at_x, at_core):
            return ref.at[pl.ds(pl.multiple_of((at_x * 2 + at_core) * eighth, eighth), eighth), :]

        over_z = remote(piece(src, x, core), piece(dst, x, core), z_sent.at[first], z_land.at[first], cross)
        over_z.start()
        waits.append(over_z)

        def to_core(k):
            at_x = lax.rem(x + k, 4)
            copy = remote(
                piece(dst, at_x, core), piece(dst, at_x, core), core_sent.at[first * 4 + k],
                core_land.at[first * 4 + k], other_core,
            )
            copy.start()
            waits.append(copy)
            return copy

        def next_stage():
            over_z.wait_recv()
            copies = []
            for k in (1, 3, 2):
                copy = remote(
                    piece(dst, x, core), piece(dst, x, core), x_sent.at[first * 4 + k],
                    x_land.at[first * 4 + 4 - k], along_x(k),
                )
                copy.start()
                copies.append((4 - k, copy))
            waits.extend(copy for _, copy in copies)
            cores = [to_core(0)]

            def last_stage():
                for k, copy in copies:
                    copy.wait_recv()
                    cores.append(to_core(k))

                def finish():
                    for copy in cores:
                        copy.wait_recv()

                return finish

            return last_stage

        return next_stage

    qkv_stage = shard_stage(w_own, w_par, 0)
    o_stage = shard_stage(o_own, o_par, 1)
    qkv_stage = qkv_stage()
    o_stage = o_stage()
    qkv_stage = qkv_stage()
    o_stage = o_stage()

    for copy in y_copies:
        copy.wait_recv()
    waits.extend(y_copies)
    cot_copies = []
    for k in (1, 3, 2):
        copy = remote(
            cot_hbm, cot_got.at[pl.ds((4 - k) * ROWS, ROWS), :], cot_sent.at[k], cot_land.at[4 - k], along_y(k)
        )
        copy.start()
        cot_copies.append(copy)
    waits.extend(cot_copies)

    def prepared(value, gain):
        scaled = value * inverse_rms(value) * gain
        turned = jnp.concatenate([-scaled[:, HD // 2 :], scaled[:, : HD // 2]], axis=1)
        return (scaled * cos[...] + turned * sin[...]).astype(BF16)

    def unit_copy(src, dst, sent, landed, dest):
        return remote(block(src, dest), block(dst, me), sent.at[dest], landed.at[me], ctx_at(dest))

    def side_units(side):
        @pl.loop(0, 4)
        def _(s):
            rows = pl.ds(pl.multiple_of(s * ROWS, ROWS), ROWS)
            for g in range(2):
                at = side * half + g * HD
                unit = s * 4 + side * 2 + g
                q_out[pl.ds(pl.multiple_of(unit * ROWS, ROWS), ROWS), :] = prepared(raw[rows, at : at + HD], q_gain[...])
            at = side * half + 2 * HD
            unit = s * 4 + side * 2
            kv_out[pl.ds(pl.multiple_of(unit * ROWS, ROWS), ROWS), :] = prepared(raw[rows, at : at + HD], k_gain[...])
            kv_out[pl.ds(pl.multiple_of((unit + 1) * ROWS, ROWS), ROWS), :] = raw[rows, at + HD : at + 2 * HD].astype(BF16)

        @pl.loop(0, 8)
        def _(j):
            turn = lax.rem(me + j, 8)
            dest = (turn // 2) * 4 + side * 2 + lax.rem(turn, 2)

            @pl.when(dest != me)
            def _():
                unit_copy(kv_out, mine, kv_sent, kv_land, dest).start()
                unit_copy(q_out, q_got, q_sent, q_land, dest).start()

    raw[:, :half] = dot(normed[...], w_own[...])
    side_units(0)
    qkv_finish = qkv_stage
    qkv_finish()
    raw[:, half:] = dot(normed[...], w_par[...])
    side_units(1)
    local = [
        pltpu.make_async_copy(block(q_out, me), block(q_got, me), local_sem.at[1]),
        pltpu.make_async_copy(block(kv_out, me), block(mine, me), local_sem.at[2]),
    ]
    for copy in local:
        copy.start()
    o_finish = o_stage
    o_finish()
    outs = [
        pltpu.make_async_copy(src, dst, out_sem.at[i])
        for i, (src, dst) in enumerate(
            ((raw, raw_hbm), (normed, normed_hbm), (w_own, own_hbm), (w_par, par_hbm), (o_par, o_par_hbm))
        )
    ]
    for copy in outs:
        copy.start()

    def from_unit(src, dst, sent, landed, source):
        return remote(block(src, source), block(dst, source), sent.at[source], landed.at[source], ctx_at(source))

    local[1].wait()

    @pl.loop(0, 16)
    def _(source):
        @pl.when(source != me)
        def _():
            from_unit(kv_out, mine, kv_sent, kv_land, source).wait_recv()

    swap = remote(mine, other, swap_sem.at[0], swap_sem.at[1], other_core)
    swap.start()

    @pl.loop(0, 16)
    def _(source):
        @pl.when(source != me)
        def _():
            from_unit(q_out, q_got, q_sent, q_land, source).wait_recv()
            from_unit(q_out, q_got, q_sent, q_land, source).wait_send()
            from_unit(kv_out, mine, kv_sent, kv_land, source).wait_send()

    for copy in cot_copies:
        copy.wait_recv()
    swap.wait()
    local[0].wait()
    own_cot.wait()
    for copy in outs:
        copy.wait()
    for copy in waits:
        copy.wait_send()


def pre(tokens, cos, sin, attn_gain, q_gain, k_gain, cot, q_w, k_w, v_w, o_w):
    rows, model = tokens.shape
    wide = q_w.shape[1] + k_w.shape[1] + v_w.shape[1]
    anywhere = pl.BlockSpec(memory_space=pl.ANY)
    vmem = pl.BlockSpec(memory_space=pltpu.VMEM)
    dma = pltpu.SemaphoreType.DMA
    unit = jax.ShapeDtypeStruct((16 * rows, HD), BF16)
    return pl.pallas_call(
        pre_kernel,
        out_shape=(
            unit,
            unit,
            unit,
            jax.ShapeDtypeStruct((4 * rows, 2 * wide), F32),
            jax.ShapeDtypeStruct((4 * rows, model), BF16),
            jax.ShapeDtypeStruct((model, wide), BF16),
            jax.ShapeDtypeStruct((model, wide), BF16),
            jax.ShapeDtypeStruct(o_w.shape, BF16),
            jax.ShapeDtypeStruct((4 * rows, model), BF16),
        ),
        in_specs=[vmem] * 6 + [anywhere] * 5,
        out_specs=(anywhere,) * 9,
        scratch_shapes=[
            pltpu.VMEM((4 * rows, model), BF16),
            pltpu.VMEM((model, wide), BF16),
            pltpu.VMEM((model, wide), BF16),
            pltpu.VMEM(o_w.shape, BF16),
            pltpu.VMEM(o_w.shape, BF16),
            pltpu.VMEM((4 * rows, 2 * wide), F32),
            pltpu.VMEM((16 * rows, HD), BF16),
            pltpu.VMEM((16 * rows, HD), BF16),
            dma((4,)),
            dma((4,)),
            dma((4,)),
            dma((4,)),
            dma((4,)),
            dma((2,)),
            dma((2,)),
            dma((8,)),
            dma((8,)),
            dma((8,)),
            dma((8,)),
            dma((16,)),
            dma((16,)),
            dma((16,)),
            dma((16,)),
            dma((2,)),
            dma((3,)),
            dma((5,)),
        ],
        compiler_params=pltpu.CompilerParams(
            collective_id=3, has_side_effects=True, vmem_limit_bytes=58 * 2**20
        ),
        cost_estimate=pl.CostEstimate(
            flops=2 * 4 * rows * model * 2 * wide, bytes_accessed=24 * 2**20, transcendentals=0
        ),
        name="pre",
    )(tokens, cos, sin, attn_gain, q_gain, k_gain, cot, q_w, k_w, v_w, o_w)


def middle_kernel(
    tokens, cot, gain, att_hbm, o_own_hbm, o_par_hbm, cot_hbm, gate_hbm, up_hbm, down_hbm,
    middle, middle_grad, gain_grad, grad_got, att_out, branch_out, part_hbm, part_got, wgrad_hbm,
    att, o_own, o_par, o_parts, o_got, hid, cots, gate_w, up_w, down_w, act_grad, gu_grad, act, parts, got, z_out, z_got,
    part, stage, branch_all, att_grad,
    load_sem, att_sent, att_land, o_sent, o_land, sent, landed, sent_back, landed_back, cot_sent, cot_land,
    part_sent, part_land, branch_sent, branch_land, grad_sent, grad_land, stage_sem, out_sem, local_sem,
):
    zl, x, core = (lax.axis_index(a) for a in CTX)
    zh, y = (lax.axis_index(a) for a in FSDP)
    me = zl * 8 + x * 2 + core
    half = 4 * ROWS
    width = gate_w.shape[1]
    model = hid.shape[1]
    side = 2 * HD
    waits = []

    def along(k):
        return {"y": lax.rem(y + k, 4)}

    across = {"zh": 1 - zh}
    loads = [
        pltpu.make_async_copy(src, dst, load_sem.at[i])
        for i, (src, dst) in enumerate(
            (
                (o_own_hbm, o_own),
                (o_par_hbm, o_par),
                (cot_hbm, cots.at[pl.ds(0, half), :]),
                (down_hbm, down_w),
                (gate_hbm, gate_w),
                (up_hbm, up_w),
            )
        )
    ]
    for load in loads:
        load.start()
    peers([ctx_at(lax.rem(me + k, 16)) for k in range(1, 16)] + [along(1), along(2), along(3), across])

    def att_at(unit):
        return att.at[
            pl.ds(pl.multiple_of(unit // 4 * ROWS, ROWS), ROWS), pl.ds(pl.multiple_of(lax.rem(unit, 4) * HD, HD), HD)
        ]

    def att_copy(dest, source):
        return remote(block(att_hbm, dest), att_at(source), att_sent.at[dest], att_land.at[source], ctx_at(dest))

    @pl.loop(1, 16)
    def _(k):
        att_copy(lax.rem(me + k, 16), me).start()

    own_att = pltpu.make_async_copy(block(att_hbm, me), att_at(me), local_sem.at[0])
    own_att.start()
    cot_copy = remote(cot_hbm, cots.at[pl.ds(half, half), :], cot_sent, cot_land, across)
    cot_copy.start()
    waits.append(cot_copy)
    loads[0].wait()
    loads[1].wait()
    own_att.wait()

    @pl.loop(1, 16)
    def _(k):
        att_copy(lax.rem(me + k, 16), lax.rem(me + k, 16)).wait_recv()

    def rows_at(ref, r):
        return ref.at[pl.ds(r * ROWS, ROWS), :]

    @pl.loop(0, model // WIDE)
    def _(n):
        cols = pl.ds(pl.multiple_of(n * WIDE, WIDE), WIDE)
        total = dot(att[:, :side], o_own[:, cols]) + dot(att[:, side:], o_par[:, cols])
        o_parts[:, cols] = total.astype(BF16)

    o_copies = []
    for k in (1, 3, 2):
        copy = remote(rows_at(o_parts, k), rows_at(o_got, 4 - k), o_sent.at[k], o_land.at[4 - k], along(k))
        copy.start()
        o_copies.append(copy)
    waits.extend(o_copies)

    def grads_of_cot(first):
        rows = pl.ds(first, half)

        @pl.loop(0, width // WIDE)
        def _(n):
            cols = pl.ds(pl.multiple_of(n * WIDE, WIDE), WIDE)
            act_grad[rows, cols] = dot(cots[rows, :], down_w[cols, :], ((1,), (1,)))

    loads[2].wait()
    loads[3].wait()
    grads_of_cot(0)
    for copy in o_copies:
        copy.wait_recv()
    total = tokens[...].astype(F32) + o_parts[:ROWS, :].astype(F32)
    for k in (1, 2, 3):
        total += o_got[k * ROWS : (k + 1) * ROWS, :].astype(F32)
    middle[...] = total
    hid[:ROWS, :] = (total * inverse_rms(total) * gain[...]).astype(BF16)

    out = []
    for k in (1, 3, 2):
        out.append(remote(rows_at(hid, 0), rows_at(hid, 4 - k), sent.at[k], landed.at[4 - k], along(k)))
    out.append(remote(rows_at(hid, 0), rows_at(hid, 4), sent.at[4], landed.at[4], across))
    for copy in out:
        copy.start()
    loads[4].wait()
    loads[5].wait()
    cot_copy.wait_recv()
    grads_of_cot(half)

    out[3].wait_recv()
    on = []
    for k in (1, 3, 2):
        on.append(remote(rows_at(hid, 4), rows_at(hid, 8 - k), sent.at[4 + k], landed.at[8 - k], along(k)))
    for copy in on:
        copy.start()
    waits.extend(out + on)

    def forward(first):
        rows = pl.ds(first, half)

        @pl.loop(0, width // WIDE)
        def _(n):
            cols = pl.ds(pl.multiple_of(n * WIDE, WIDE), WIDE)
            gate = dot(hid[rows, :], gate_w[:, cols])
            up = dot(hid[rows, :], up_w[:, cols])
            sig = jax.nn.sigmoid(gate)
            silu = gate * sig
            grad = act_grad[rows, cols]
            act[rows, cols] = (silu * up).astype(BF16)
            gu_grad[rows, cols] = (grad * up * sig * (1.0 + gate * (1.0 - sig))).astype(BF16)
            gu_grad[rows, pl.ds(pl.multiple_of(width + n * WIDE, WIDE), WIDE)] = (grad * silu).astype(BF16)

    def backward(first):
        rows = pl.ds(first, half)

        @pl.loop(0, model // WIDE)
        def _(n):
            cols = pl.ds(pl.multiple_of(n * WIDE, WIDE), WIDE)
            total = dot(gu_grad[rows, :width], gate_w[cols, :], ((1,), (1,)))
            total += dot(gu_grad[rows, width:], up_w[cols, :], ((1,), (1,)))
            parts[rows, cols] = total.astype(BF16)

    for copy in out[:3]:
        copy.wait_recv()
    forward(0)
    backward(0)
    for copy in on:
        copy.wait_recv()
    forward(half)
    backward(half)
    back = {}
    for r in (4, 0):
        for k in (1, 3, 2):
            copy = remote(
                rows_at(parts, r + k), rows_at(got, r + 4 - k), sent_back.at[r + k], landed_back.at[r + 4 - k], along(k)
            )
            copy.start()
            back[r + 4 - k] = copy
    waits.extend(back.values())

    def down_part(first):
        rows = pl.ds(first, half)

        @pl.loop(0, model // WIDE)
        def _(n):
            cols = pl.ds(pl.multiple_of(n * WIDE, WIDE), WIDE)
            part[rows, cols] = dot(act[rows, :], down_w[:, cols]).astype(BF16)

    down_part(half)
    down_part(0)
    outs = [
        pltpu.make_async_copy(part.at[pl.ds(0, half), :], part_hbm, out_sem.at[0]),
        pltpu.make_async_copy(att, att_out, out_sem.at[1]),
    ]
    for copy in outs:
        copy.start()

    def stage_copy(b, n):
        rows = pl.ds(pl.multiple_of(n * WIDE, WIDE), WIDE)
        return pltpu.make_async_copy(stage.at[b], wgrad_hbm.at[rows, :], stage_sem.at[b])

    def weight_grads(begin, end):
        @pl.loop(begin, end)
        def _(m):
            for b in range(2):
                n = m * 2 + b
                cols = pl.ds(pl.multiple_of(n * WIDE, WIDE), WIDE)

                @pl.when(m > 0)
                def _():
                    stage_copy(b, n - 2).wait()

                stage[b, :, : 2 * width] = dot(hid[:, cols], gu_grad[...], ((0,), (0,))).astype(BF16)
                stage[b, :, 2 * width :] = dot(cots[:, cols], act[...], ((0,), (0,))).astype(BF16)
                stage_copy(b, n).start()

    steps = model // WIDE // 2
    weight_grads(0, steps // 2)
    for k in (1, 2, 3):
        back[4 + k].wait_recv()

    def summed(r):
        total = parts[r * ROWS : (r + 1) * ROWS, :].astype(F32)
        for k in (1, 2, 3):
            total += got[(r + k) * ROWS : (r + k + 1) * ROWS, :].astype(F32)
        return total

    z_out[...] = summed(4).astype(BF16)
    z_copy = remote(z_out, z_got, sent_back.at[0], landed_back.at[0], across)
    z_copy.start()
    waits.append(z_copy)
    weight_grads(steps // 2, steps)
    for k in (1, 2, 3):
        back[k].wait_recv()
    z_copy.wait_recv()

    rows_back, gain_sum = rms_back(summed(0) + z_got[...].astype(F32), middle[...], gain[...])
    gain_grad[...] = gain_sum
    total = cot[...].astype(F32) + rows_back
    middle_grad[...] = total
    branch_all[:ROWS, :] = total.astype(BF16)

    branch_copies = []
    for k in (1, 3, 2):
        copy = remote(
            rows_at(branch_all, 0), rows_at(branch_all, 4 - k), branch_sent.at[k], branch_land.at[4 - k], along(k)
        )
        copy.start()
        branch_copies.append(copy)
    waits.extend(branch_copies)
    part_copy = remote(part.at[pl.ds(half, half), :], part_got, part_sent, part_land, across)
    part_copy.start()
    for copy in branch_copies:
        copy.wait_recv()
    att_grad[:, :side] = dot(branch_all[...], o_own[...], ((1,), (1,))).astype(BF16)
    att_grad[:, side:] = dot(branch_all[...], o_par[...], ((1,), (1,))).astype(BF16)

    def unit_of(unit):
        return att_grad.at[
            pl.ds(pl.multiple_of(unit // 4 * ROWS, ROWS), ROWS), pl.ds(pl.multiple_of(lax.rem(unit, 4) * HD, HD), HD)
        ]

    def grad_copy(dest, source):
        return remote(unit_of(dest), block(grad_got, source), grad_sent.at[dest], grad_land.at[source], ctx_at(dest))

    @pl.loop(1, 16)
    def _(k):
        grad_copy(lax.rem(me + k, 16), me).start()

    own_grad = pltpu.make_async_copy(unit_of(me), block(grad_got, me), local_sem.at[1])
    own_grad.start()
    branch_copy = pltpu.make_async_copy(branch_all, branch_out, out_sem.at[2])
    branch_copy.start()
    outs.append(branch_copy)

    @pl.loop(1, 16)
    def _(k):
        peer = lax.rem(me + k, 16)
        grad_copy(peer, peer).wait_recv()
        grad_copy(peer, peer).wait_send()
        att_copy(peer, peer).wait_send()

    own_grad.wait()
    part_copy.wait()
    for copy in waits:
        copy.wait_send()
    for copy in outs:
        copy.wait()
    for b in range(2):
        stage_copy(b, 2 * steps - 2 + b).wait()


def middle_part(tokens, cot, gain, att, o_own, o_par, cot_half, gate_w, up_w, down_w):
    rows, model = tokens.shape
    width = gate_w.shape[1]
    anywhere = pl.BlockSpec(memory_space=pl.ANY)
    vmem = pl.BlockSpec(memory_space=pltpu.VMEM)
    dma = pltpu.SemaphoreType.DMA
    half = jax.ShapeDtypeStruct((4 * rows, model), BF16)
    low = functools.partial(pltpu.VMEM, dtype=BF16)
    return pl.pallas_call(
        middle_kernel,
        out_shape=(
            jax.ShapeDtypeStruct((rows, model), F32),
            jax.ShapeDtypeStruct((rows, model), F32),
            jax.ShapeDtypeStruct((1, model), F32),
            jax.ShapeDtypeStruct((16 * rows, HD), BF16),
            jax.ShapeDtypeStruct((4 * rows, 4 * HD), BF16),
            half,
            half,
            half,
            jax.ShapeDtypeStruct((model, 3 * width), BF16),
        ),
        in_specs=[vmem] * 3 + [anywhere] * 7,
        out_specs=(vmem,) * 3 + (anywhere,) * 6,
        scratch_shapes=[
            low((4 * rows, 4 * HD)),
            low((2 * HD, model)),
            low((2 * HD, model)),
            low((4 * rows, model)),
            low((4 * rows, model)),
            low((8 * rows, model)),
            low((8 * rows, model)),
            low((model, width)),
            low((model, width)),
            low((width, model)),
            pltpu.VMEM((8 * rows, width), F32),
            low((8 * rows, 2 * width)),
            low((8 * rows, width)),
            low((8 * rows, model)),
            low((8 * rows, model)),
            low((rows, model)),
            low((rows, model)),
            low((8 * rows, model)),
            low((2, WIDE, 3 * width)),
            low((4 * rows, model)),
            low((4 * rows, 4 * HD)),
            dma((6,)),
            dma((16,)),
            dma((16,)),
            dma((4,)),
            dma((4,)),
            dma((8,)),
            dma((8,)),
            dma((8,)),
            dma((8,)),
            dma,
            dma,
            dma,
            dma,
            dma((4,)),
            dma((4,)),
            dma((16,)),
            dma((16,)),
            dma((2,)),
            dma((3,)),
            dma((2,)),
        ],
        compiler_params=pltpu.CompilerParams(
            collective_id=1, has_side_effects=True, vmem_limit_bytes=60 * 2**20
        ),
        cost_estimate=pl.CostEstimate(
            flops=2 * 9 * 8 * rows * model * width, bytes_accessed=40 * 2**20, transcendentals=8 * rows * width
        ),
        name="middle",
    )(tokens, cot, gain, att, o_own, o_par, cot_half, gate_w, up_w, down_w)


def back_kernel(
    q_grad, keep, send, raw, cos, sin, q_gain, k_gain, tokens, middle_grad, attn_gain, mlp_gain_grad,
    middle, normed_hbm, own_hbm, par_hbm, branch_hbm, att_hbm, part_hbm, part_got_hbm,
    tokens_grad, wgrad, gains, out_rows, o_wgrad,
    normed, w_own, w_par, branch_all, att, part, part_across, out_got, swap_got, kv_out, q_got, kv_got, low, parts, y_got,
    core_out, core_got, red, x_got, z_out, z_low, z_got, o_core_out, o_core_got, o_red, o_x_got, o_z_out, o_z_low, o_z_got,
    g_out, g_got,
    load_sem, swap_sem, q_sent, q_land, kv_sent, kv_land, y_sent, y_land, out_sent, out_land,
    core_sent, core_land, x_sent, x_land, z_sent, z_land, g_sent, g_land,
):
    zl, x, core = (lax.axis_index(a) for a in CTX)
    zh, y = (lax.axis_index(a) for a in FSDP)
    me = zl * 8 + x * 2 + core
    half = 4 * HD

    def along_y(k):
        return {"y": lax.rem(y + k, 4)}

    def along_x(k):
        return {"x": lax.rem(x + k, 4)}

    def along_ctx(k):
        return ctx_at(lax.rem(me + k, 16))

    other_core = {"core": 1 - core}
    zs = {1: {"zl": 1 - zl}, 2: {"zh": 1 - zh}, 3: {"zl": 1 - zl, "zh": 1 - zh}}

    loads = [
        pltpu.make_async_copy(src, dst, load_sem.at[i])
        for i, (src, dst) in enumerate(
            (
                (part_hbm, part),
                (part_got_hbm, part_across),
                (branch_hbm, branch_all),
                (att_hbm, att),
                (normed_hbm, normed),
                (own_hbm, w_own),
                (par_hbm, w_par),
            )
        )
    ]
    for load in loads:
        load.start()
    peers([along_ctx(k) for k in range(1, 16)] + [along_y(k) for k in (1, 2, 3)] + [zs[2], zs[3]])

    swap = remote(send, swap_got, swap_sem.at[0], swap_sem.at[1], other_core)
    swap.start()

    waits = [swap]

    def to_rows(src, dst, sent, landed):
        copies = []
        for k in range(1, 16):
            copy = remote(block(src, lax.rem(me + k, 16)), block(dst, 16 - k), sent.at[k], landed.at[16 - k], along_ctx(k))
            copy.start()
            copies.append(copy)
        waits.extend(copies)
        return copies

    q_copies = to_rows(q_grad, q_got, q_sent, q_land)
    mine = pl.ds(pl.multiple_of(me * ROWS, ROWS), ROWS)
    q_got[:ROWS, :] = q_grad[mine, :]
    swap.wait_recv()
    kv_out[...] = (keep[...] + swap_got[...].astype(F32)).astype(BF16)
    kv_copies = to_rows(kv_out, kv_got, kv_sent, kv_land)
    kv_got[:ROWS, :] = kv_out[mine, :]

    loads[0].wait()
    loads[1].wait()
    part[...] = (part[...].astype(F32) + part_across[...].astype(F32)).astype(BF16)
    out_copies = []
    for k in (1, 3, 2):
        copy = remote(
            part.at[pl.ds(k * ROWS, ROWS), :], out_got.at[4 - k], out_sent.at[k], out_land.at[4 - k], along_y(k)
        )
        copy.start()
        out_copies.append(copy)
    waits.extend(out_copies)

    def grad_stages(first, tile, to_other, from_other, summed, from_x, total, total_low, from_z):
        n = total.shape[2] // 2

        def over_cores():
            @pl.loop(0, 8)
            def _(t):
                to_other[t] = tile(t * 2 + 1 - core).astype(BF16)

            copy = remote(to_other, from_other, core_sent.at[first], core_land.at[first], other_core)
            copy.start()
            waits.append(copy)
            return copy

        def over_x(core_copy):
            core_copy.wait_recv()

            @pl.loop(0, 8)
            def _(t):
                summed[t] = (tile(t * 2 + core) + from_other[t].astype(F32)).astype(BF16)

            copies = []
            for k in (1, 3, 2):
                for a in range(2):
                    copy = remote(
                        summed.at[a * 4 + lax.rem(x + k, 4)], from_x.at[4 - k, a],
                        x_sent.at[first * 8 + k * 2 + a], x_land.at[first * 8 + (4 - k) * 2 + a], along_x(k),
                    )
                    copy.start()
                    copies.append(copy)
            waits.extend(copies)
            return copies

        def over_z(x_copies):
            for copy in x_copies:
                copy.wait_recv()
            for a in range(2):
                value = summed[a * 4 + x].astype(F32)
                for k in (1, 2, 3):
                    value += from_x[k, a].astype(F32)
                total[a] = value
                total_low[a] = value.astype(BF16)
            copies = []
            for d in (1, 2, 3):
                rows_of = 1 - zl if d % 2 else zl
                copy = remote(
                    total_low.at[rows_of, :, pl.ds(n if d >= 2 else 0, n)], from_z.at[d - 1],
                    z_sent.at[first * 3 + d - 1], z_land.at[first * 3 + d - 1], zs[d],
                )
                copy.start()
                copies.append(copy)
            waits.extend(copies)
            return copies

        def finish(z_copies):
            for copy in z_copies:
                copy.wait_recv()
            value = total[zl, :, :n]
            for d in range(3):
                value = value + from_z[d].astype(F32)
            return value

        return over_cores, over_x, over_z, finish

    def tile_of(left, right):
        def tile(t):
            cols = pl.ds(pl.multiple_of(t * ROWS, ROWS), ROWS)
            return dot(left[:, cols], right[...], ((0,), (0,)))

        return tile

    qkv_cores, qkv_x, qkv_z, qkv_finish = grad_stages(
        0, tile_of(normed, low), core_out, core_got, red, x_got, z_out, z_low, z_got
    )
    o_cores, o_x, o_z, o_finish = grad_stages(
        1, tile_of(branch_all, att), o_core_out, o_core_got, o_red, o_x_got, o_z_out, o_z_low, o_z_got
    )
    loads[2].wait()
    loads[3].wait()
    o_x_copies = o_x(o_cores())
    for load in loads[4:]:
        load.wait()
    for copy in q_copies:
        copy.wait_recv()
    for copy in kv_copies:
        copy.wait_recv()

    g_out[0] = jnp.zeros_like(g_out[0])

    def from_unit(ref, unit):
        return ref[pl.ds(pl.multiple_of(lax.rem(unit - me + 16, 16) * ROWS, ROWS), ROWS), :]

    def head_back(grad, value, gain):
        turned = grad * sin[...]
        turned = jnp.concatenate([turned[:, HD // 2 :], -turned[:, : HD // 2]], axis=1)
        back, gain_sum = rms_back(grad * cos[...] + turned, value, gain)
        return back.astype(BF16), gain_sum

    @pl.loop(0, 4)
    def _(s):
        rows = pl.ds(pl.multiple_of(s * ROWS, ROWS), ROWS)
        for h in range(4):
            at = (h // 2) * half + (h % 2) * HD
            cols = slice(at, at + HD)
            grad = from_unit(q_got, s * 4 + h).astype(F32)
            back, gain_sum = head_back(grad, raw[rows, cols], q_gain[...])
            low[rows, cols] = back
            g_out[0, 32:33, :] += gain_sum
        for kv in range(2):
            at = kv * half + 2 * HD
            cols = slice(at, at + HD)
            grad = from_unit(kv_got, s * 4 + kv * 2).astype(F32)
            back, gain_sum = head_back(grad, raw[rows, cols], k_gain[...])
            low[rows, cols] = back
            g_out[0, 33:34, :] += gain_sum
            low[rows, at + HD : at + 2 * HD] = from_unit(kv_got, s * 4 + kv * 2 + 1)

    core_copy = qkv_cores()

    @pl.loop(0, parts.shape[1] // WIDE)
    def _(n):
        cols = pl.ds(pl.multiple_of(n * WIDE, WIDE), WIDE)
        total = dot(low[:, :half], w_own[cols, :], ((1,), (1,)))
        total += dot(low[:, half:], w_par[cols, :], ((1,), (1,)))
        parts[:, cols] = total.astype(BF16)

    y_copies = []
    for k in (1, 3, 2):
        copy = remote(
            parts.at[pl.ds(k * ROWS, ROWS), :], y_got.at[4 - k], y_sent.at[k], y_land.at[4 - k], along_y(k)
        )
        copy.start()
        y_copies.append(copy)
    waits.extend(y_copies)

    x_copies = qkv_x(core_copy)
    for copy in out_copies:
        copy.wait_recv()
    total = middle[...] + part[:ROWS, :].astype(F32)
    for k in (1, 2, 3):
        total += out_got[k].astype(F32)
    out_rows[...] = total.astype(BF16)
    o_z_copies = o_z(o_x_copies)

    for copy in y_copies:
        copy.wait_recv()
    grad = parts[:ROWS, :].astype(F32)
    for k in (1, 2, 3):
        grad += y_got[k].astype(F32)
    rows_back, gain_sum = rms_back(grad, tokens[...].astype(F32), attn_gain[...])
    tokens_grad[...] = (middle_grad[...] + rows_back).astype(BF16)
    for i in range(16):
        g_out[0, i : i + 1, :] = gain_sum[:, i * HD : (i + 1) * HD]
        g_out[0, 16 + i : 17 + i, :] = mlp_gain_grad[:, i * HD : (i + 1) * HD]

    def gain_stage(stage, places):
        copies = []
        for i, (place, back_slot) in enumerate(places):
            copy = remote(
                g_out.at[stage], g_got.at[stage, back_slot], g_sent.at[stage * 3 + i],
                g_land.at[stage * 3 + back_slot], place,
            )
            copy.start()
            copies.append(copy)
        waits.extend(copies)
        return copies

    def gain_sum_of(stage, copies):
        for copy in copies:
            copy.wait_recv()
        total = g_out[stage]
        for i in range(len(copies)):
            total = total + g_got[stage, i]
        return total

    copies = gain_stage(0, [(along_y(k), 3 - k) for k in (1, 2, 3)])

    z_copies = qkv_z(x_copies)
    o_wgrad[...] = o_finish(o_z_copies)
    g_out[1] = gain_sum_of(0, copies)
    copies = gain_stage(1, [(along_x(k), 3 - k) for k in (1, 2, 3)])
    g_out[2] = gain_sum_of(1, copies)
    copies = gain_stage(2, [(zs[d], d - 1) for d in (1, 2, 3)])
    wgrad[...] = qkv_finish(z_copies)
    g_out[3] = gain_sum_of(2, copies)
    copies = gain_stage(3, [(other_core, 0)])
    gains[...] = gain_sum_of(3, copies)
    for copy in waits:
        copy.wait_send()


def back(q_grad, keep, send, raw, cos, sin, q_gain, k_gain, tokens, middle_grad, attn_gain, mlp_gain_grad,
         middle, normed, w_own, w_par, branch_all, att, part, part_across):
    rows, model = tokens.shape
    wide = raw.shape[1]
    anywhere = pl.BlockSpec(memory_space=pl.ANY)
    vmem = pl.BlockSpec(memory_space=pltpu.VMEM)
    dma = pltpu.SemaphoreType.DMA
    return pl.pallas_call(
        back_kernel,
        out_shape=(
            jax.ShapeDtypeStruct((rows, model), BF16),
            jax.ShapeDtypeStruct((rows, wide // 2), F32),
            jax.ShapeDtypeStruct((40, HD), F32),
            jax.ShapeDtypeStruct((rows, model), BF16),
            jax.ShapeDtypeStruct((rows, 2 * HD), F32),
        ),
        in_specs=[vmem] * 13 + [anywhere] * 7,
        out_specs=(vmem,) * 5,
        scratch_shapes=[
            pltpu.VMEM((4 * rows, model), BF16),
            pltpu.VMEM((model, wide // 2), BF16),
            pltpu.VMEM((model, wide // 2), BF16),
            pltpu.VMEM((4 * rows, model), BF16),
            pltpu.VMEM((4 * rows, 4 * HD), BF16),
            pltpu.VMEM((4 * rows, model), BF16),
            pltpu.VMEM((4 * rows, model), BF16),
            pltpu.VMEM((4, rows, model), BF16),
            pltpu.VMEM((16 * rows, HD), BF16),
            pltpu.VMEM((16 * rows, HD), BF16),
            pltpu.VMEM((16 * rows, HD), BF16),
            pltpu.VMEM((16 * rows, HD), BF16),
            pltpu.VMEM((4 * rows, wide), BF16),
            pltpu.VMEM((4 * rows, model), BF16),
            pltpu.VMEM((4, rows, model), BF16),
            pltpu.VMEM((8, rows, wide), BF16),
            pltpu.VMEM((8, rows, wide), BF16),
            pltpu.VMEM((8, rows, wide), BF16),
            pltpu.VMEM((4, 2, rows, wide), BF16),
            pltpu.VMEM((2, rows, wide), F32),
            pltpu.VMEM((2, rows, wide), BF16),
            pltpu.VMEM((3, rows, wide // 2), BF16),
            pltpu.VMEM((8, rows, 4 * HD), BF16),
            pltpu.VMEM((8, rows, 4 * HD), BF16),
            pltpu.VMEM((8, rows, 4 * HD), BF16),
            pltpu.VMEM((4, 2, rows, 4 * HD), BF16),
            pltpu.VMEM((2, rows, 4 * HD), F32),
            pltpu.VMEM((2, rows, 4 * HD), BF16),
            pltpu.VMEM((3, rows, 2 * HD), BF16),
            pltpu.VMEM((4, 40, HD), F32),
            pltpu.VMEM((4, 3, 40, HD), F32),
            dma((7,)),
            dma((2,)),
            dma((16,)),
            dma((16,)),
            dma((16,)),
            dma((16,)),
            dma((4,)),
            dma((4,)),
            dma((4,)),
            dma((4,)),
            dma((2,)),
            dma((2,)),
            dma((16,)),
            dma((16,)),
            dma((6,)),
            dma((6,)),
            dma((12,)),
            dma((12,)),
        ],
        compiler_params=pltpu.CompilerParams(
            collective_id=2, has_side_effects=True, vmem_limit_bytes=58 * 2**20
        ),
        cost_estimate=pl.CostEstimate(
            flops=4 * 4 * rows * model * wide, bytes_accessed=24 * 2**20, transcendentals=0
        ),
        name="back",
    )(
        q_grad, keep, send, raw, cos, sin, q_gain, k_gain, tokens, middle_grad, attn_gain, mlp_gain_grad,
        middle, normed, w_own, w_par, branch_all, att, part, part_across,
    )


def per_device(
    tokens,
    cotangent,
    attn_gain,
    q_weight,
    k_weight,
    v_weight,
    q_gain,
    k_gain,
    o_weight,
    mlp_gain,
    gate_weight,
    up_weight,
    down_weight,
    doc_lengths,
    block_place,
):
    rows = tokens.shape[1]
    zl, x, core = (lax.axis_index(a) for a in CTX)
    zh, y = (lax.axis_index(a) for a in FSDP)
    ctx_place = zl * 8 + x * 2 + core
    sequence = zh * 4 + lax.rem(y + ctx_place // 4, 4)
    ends = jnp.cumsum(lax.dynamic_index_in_dim(doc_lengths, sequence, 0, keepdims=False))
    ends = ends.astype(jnp.int32)
    core_flag = core.astype(jnp.int32).reshape(1)
    own_blocks = lax.dynamic_slice_in_dim(block_place, ctx_place * (rows // BLK), rows // BLK)
    own_positions = (own_blocks[:, None] * BLK + jnp.arange(BLK, dtype=jnp.int32)[None, :]).reshape(-1)
    cos_rows, sin_rows = tables(own_positions, HD)
    q_gain, k_gain = q_gain.reshape(1, HD), k_gain.reshape(1, HD)
    attn_gain, mlp_gain = attn_gain.reshape(1, -1), mlp_gain.reshape(1, -1)
    cot = cotangent[0]

    q_in, mine, other, raw, normed, w_own, w_par, o_par, cot_half = pre(
        tokens[0], cos_rows, sin_rows, attn_gain, q_gain, k_gain, cot, q_weight, k_weight, v_weight, o_weight
    )
    out, q_pos, k_pos, v_pos, log_total = attend(block_place, ends, core_flag, q_in, mine, other)
    middle, middle_grad, mlp_gain_grad, grad_in, att, branch_all, part, part_across, mlp_wgrad = middle_part(
        tokens[0], cot, mlp_gain, out, o_weight, o_par, cot_half, gate_weight, up_weight, down_weight
    )
    mlp_wgrad = lax.psum_scatter(mlp_wgrad, CTX, scatter_dimension=0, tiled=True).astype(F32)
    width = gate_weight.shape[1]
    q_grad, keep_grad, send_grad = attend_back(
        block_place, ends, core_flag, grad_in, q_pos, k_pos, v_pos, log_total
    )
    tokens_grad, qkv_wgrad, gains, out_rows, o_wgrad = back(
        q_grad, keep_grad, send_grad, raw, cos_rows, sin_rows, q_gain, k_gain, tokens[0], middle_grad, attn_gain,
        mlp_gain_grad, middle, normed, w_own, w_par, branch_all, att, part, part_across,
    )
    return (
        out_rows[None],
        tokens_grad[None],
        gains[:16].reshape(-1),
        qkv_wgrad[:, : 2 * HD],
        qkv_wgrad[:, 2 * HD : 3 * HD],
        qkv_wgrad[:, 3 * HD :],
        gains[32],
        gains[33],
        o_wgrad.T,
        gains[16:32].reshape(-1),
        mlp_wgrad[:, :width],
        mlp_wgrad[:, width : 2 * width],
        mlp_wgrad[:, 2 * width :].T,
    )


def solution(mesh):
    fine = Mesh(mesh.devices.reshape(SIZES), AXES)
    rows = P(FSDP, CTX, None)
    in_specs = (
        rows,
        rows,
        P(),
        P(None, FSDP),
        P(None, FSDP),
        P(None, FSDP),
        P(),
        P(),
        P(FSDP, None),
        P(),
        P(None, FSDP),
        P(None, FSDP),
        P(FSDP, None),
        P(),
        P(),
    )
    out_specs = (
        rows,
        rows,
        P(),
        P(CTX, FSDP),
        P(CTX, FSDP),
        P(CTX, FSDP),
        P(),
        P(),
        P(FSDP, CTX),
        P(),
        P(CTX, FSDP),
        P(CTX, FSDP),
        P(FSDP, CTX),
    )
    return jax.shard_map(
        per_device, mesh=fine, in_specs=in_specs, out_specs=out_specs, check_vma=False
    )
```

```python
import functools

import jax
import jax.numpy as jnp
from jax import lax
from jax.experimental import pallas as pl
from jax.experimental.pallas import tpu as pltpu
from jax.sharding import Mesh, PartitionSpec as P

EPSILON = 1e-06
ROPE_BASE = 1000000.0
MASKED_SCORE = -1e30
HD = 128
BLK = 64
AXES = ("zl", "x", "core", "zh", "y")
SIZES = (2, 4, 2, 2, 4)
CTX = ("zl", "x", "core")
FSDP = ("zh", "y")
F32 = jnp.float32
BF16 = jnp.bfloat16


def tables(positions, head_dim):
    exponent_steps = jnp.arange(head_dim // 2, dtype=jnp.int32).astype(F32) * (2.0 / head_dim)
    frequency = ROPE_BASE ** (-exponent_steps)
    phases = positions.astype(F32)[:, None] * frequency[None, :]
    phases = jnp.concatenate([phases, phases], axis=-1)
    return (jnp.cos(phases), jnp.sin(phases))


def dot(left, right, contract=((1,), (0,))):
    return lax.dot_general(left, right, (contract, ((), ())), preferred_element_type=F32)


TILE = 256


def keep_mask(ends, first_row, rows, cols):
    place = first_row + lax.broadcasted_iota(jnp.int32, (rows, 1), 0)
    start = jnp.zeros((rows, 1), jnp.int32)
    for j in range(ends.shape[0]):
        start = jnp.where(place >= ends[j], ends[j], start)
    key = lax.broadcasted_iota(jnp.int32, (rows, cols), 1)
    return (key >= start) & (key <= place)


def attend_kernel(place, ends, core, q_in, mine, other, out, q_pos, k_pos, v_pos, log_total, out_pos):
    rows = q_in.shape[0]
    blocks = rows // BLK
    scale = HD ** (-0.5)

    @pl.when(core[0] == 0)
    def _():
        @pl.loop(0, blocks)
        def _(b):
            src = pl.ds(pl.multiple_of(b * BLK, BLK), BLK)
            dst = pl.ds(pl.multiple_of(place[b] * BLK, BLK), BLK)
            q_pos[dst, :] = q_in[src, :]
            k_pos[dst, :] = mine[src, :]
            v_pos[dst, :] = other[src, :]

    @pl.when(core[0] == 1)
    def _():
        @pl.loop(0, blocks)
        def _(b):
            src = pl.ds(pl.multiple_of(b * BLK, BLK), BLK)
            dst = pl.ds(pl.multiple_of(place[b] * BLK, BLK), BLK)
            q_pos[dst, :] = q_in[src, :]
            k_pos[dst, :] = other[src, :]
            v_pos[dst, :] = mine[src, :]

    for i in range(rows // TILE):
        span = pl.ds(i * TILE, TILE)
        n = (i + 1) * TILE
        scores = dot(q_pos[span, :], k_pos[:n, :], ((1,), (1,))) * scale
        scores = jnp.where(keep_mask(ends, i * TILE, TILE, n), scores, MASKED_SCORE)
        top = jnp.max(scores, axis=-1, keepdims=True)
        weights = jnp.exp(scores - top)
        total = jnp.sum(weights, axis=-1, keepdims=True)
        log_total[span, :] = top + jnp.log(total)
        probs = (weights * (1.0 / total)).astype(BF16)
        out_pos[span, :] = dot(probs, v_pos[:n, :]).astype(BF16)

    @pl.loop(0, blocks)
    def _(b):
        src = pl.ds(pl.multiple_of(b * BLK, BLK), BLK)
        dst = pl.ds(pl.multiple_of(place[b] * BLK, BLK), BLK)
        out[src, :] = out_pos[dst, :]


def attend_back_kernel(
    place, ends, core, grad_in, q_pos, k_pos, v_pos, log_total, q_grad, keep_grad, send_grad,
    grad_pos, q_acc, k_acc, v_acc,
):
    rows = grad_in.shape[0]
    blocks = rows // BLK
    scale = HD ** (-0.5)

    @pl.loop(0, blocks)
    def _(b):
        src = pl.ds(pl.multiple_of(b * BLK, BLK), BLK)
        dst = pl.ds(pl.multiple_of(place[b] * BLK, BLK), BLK)
        grad_pos[dst, :] = grad_in[src, :]

    k_acc[...] = jnp.zeros_like(k_acc)
    v_acc[...] = jnp.zeros_like(v_acc)
    for i in range(rows // TILE):
        span = pl.ds(i * TILE, TILE)
        n = (i + 1) * TILE
        queries = q_pos[span, :]
        grads = grad_pos[span, :]
        scores = dot(queries, k_pos[:n, :], ((1,), (1,))) * scale
        kept = keep_mask(ends, i * TILE, TILE, n)
        probs = jnp.where(kept, jnp.exp(scores - log_total[span, :]), 0.0)
        prob_grad = dot(grads, v_pos[:n, :], ((1,), (1,)))
        row_dot = jnp.sum(prob_grad * probs, axis=-1, keepdims=True)
        score_grad = (probs * (prob_grad - row_dot)).astype(BF16)
        q_acc[span, :] = (dot(score_grad, k_pos[:n, :]) * scale).astype(BF16)
        k_acc[:n, :] += dot(score_grad, queries, ((0,), (0,)))
        v_acc[:n, :] += dot(probs.astype(BF16), grads, ((0,), (0,)))

    @pl.loop(0, blocks)
    def _(b):
        src = pl.ds(pl.multiple_of(b * BLK, BLK), BLK)
        dst = pl.ds(pl.multiple_of(place[b] * BLK, BLK), BLK)
        q_grad[src, :] = q_acc[dst, :]
        k_rows = k_acc[dst, :] * scale
        v_rows = v_acc[dst, :]
        first = core[0] == 0
        keep_grad[src, :] = jnp.where(first, k_rows, v_rows)
        send_grad[src, :] = jnp.where(first, v_rows, k_rows).astype(BF16)


def attend(place, ends, core, q_in, mine, other):
    rows = q_in.shape[0]
    low = jax.ShapeDtypeStruct((rows, HD), BF16)
    smem = pl.BlockSpec(memory_space=pltpu.SMEM)
    vmem = pl.BlockSpec(memory_space=pltpu.VMEM)
    return pl.pallas_call(
        attend_kernel,
        out_shape=(low, low, low, low, jax.ShapeDtypeStruct((rows, 1), F32)),
        in_specs=[smem] * 3 + [vmem] * 3,
        out_specs=(vmem,) * 5,
        scratch_shapes=[pltpu.VMEM((rows, HD), BF16)],
        compiler_params=pltpu.CompilerParams(vmem_limit_bytes=40 * 2**20),
        cost_estimate=pl.CostEstimate(
            flops=2 * rows * rows * HD, bytes_accessed=rows * HD * 16, transcendentals=rows * rows // 2
        ),
        name="attend",
    )(place, ends, core, q_in, mine, other)


def attend_back(place, ends, core, grad_in, q_pos, k_pos, v_pos, log_total):
    rows = grad_in.shape[0]
    low = jax.ShapeDtypeStruct((rows, HD), BF16)
    smem = pl.BlockSpec(memory_space=pltpu.SMEM)
    vmem = pl.BlockSpec(memory_space=pltpu.VMEM)
    return pl.pallas_call(
        attend_back_kernel,
        out_shape=(low, jax.ShapeDtypeStruct((rows, HD), F32), low),
        in_specs=[smem] * 3 + [vmem] * 5,
        out_specs=(vmem,) * 3,
        scratch_shapes=[
            pltpu.VMEM((rows, HD), BF16),
            pltpu.VMEM((rows, HD), BF16),
            pltpu.VMEM((rows, HD), F32),
            pltpu.VMEM((rows, HD), F32),
        ],
        compiler_params=pltpu.CompilerParams(vmem_limit_bytes=48 * 2**20),
        cost_estimate=pl.CostEstimate(
            flops=5 * rows * rows * HD, bytes_accessed=rows * HD * 20, transcendentals=rows * rows // 2
        ),
        name="attend_back",
    )(place, ends, core, grad_in, q_pos, k_pos, v_pos, log_total)


def peers(pairs):
    barrier = pltpu.get_barrier_semaphore()
    for place in pairs:
        pl.semaphore_signal(barrier, inc=1, device_id=place, device_id_type=pl.DeviceIdType.MESH)
    pl.semaphore_wait(barrier, len(pairs))


def remote(src, dst, sent, landed, place):
    return pltpu.make_async_remote_copy(
        src_ref=src, dst_ref=dst, send_sem=sent, recv_sem=landed, device_id=place,
        device_id_type=pl.DeviceIdType.MESH,
    )


ROWS = 128
WIDE = 256


def ctx_at(index):
    return {"zl": index // 8, "x": lax.rem(index // 2, 4), "core": lax.rem(index, 2)}


def block(ref, index):
    return ref.at[pl.ds(pl.multiple_of(index * ROWS, ROWS), ROWS), :]


def inverse_rms(values):
    return lax.rsqrt(jnp.mean(values * values, axis=-1, keepdims=True) + EPSILON)


def rms_back(grad, values, gain):
    inverse = inverse_rms(values)
    scaled = grad * gain
    inner = jnp.mean(values * scaled, axis=-1, keepdims=True)
    back = inverse * scaled - values * (inverse * inverse * inverse * inner)
    return back, jnp.sum(grad * values * inverse, axis=0, keepdims=True)


def gather_ring(slot, along, sent, landed, waits, own=None):
    def move(src, dst, i, k):
        copy = remote(src, dst, sent.at[i], landed.at[i], along(k))
        copy.start()
        waits.append(copy)
        return copy

    own = slot(0) if own is None else own
    near = [move(own, slot(1), 0, 3), move(own, slot(3), 1, 1)]
    far = []

    def pass_on():
        for h, k in ((0, 3), (1, 1)):
            near[h].wait_recv()
            far.append(move(slot(1 + 2 * h, h), slot(2, h), 2 + h, k))

    def finish():
        for copy in far:
            copy.wait_recv()

    return pass_on, finish


def scatter_ring(part, relay, got, along, sent, landed, waits):
    def move(src, dst, i, k):
        copy = remote(src, dst, sent.at[i], landed.at[i], along(k))
        copy.start()
        waits.append(copy)
        return copy

    first = [move(part(2, 0), relay(0), 0, 1), move(part(2, 1), relay(1), 1, 3)]
    last = [move(part(1, 1), got(0, 1), 2, 1), move(part(3, 0), got(1, 0), 3, 3)]

    def pass_on():
        for h, k in ((0, 1), (1, 3)):
            first[h].wait_recv()
            ref = part(k, h)
            ref[...] = (ref[...].astype(F32) + relay(h)[...].astype(F32)).astype(BF16)
            last.append(move(ref, got(h, h), 4 + h, k))

    def finish():
        for copy in last:
            copy.wait_recv()

    return pass_on, finish


def row_slots(ref, base=0):
    def slot(r, h=None):
        if h is None:
            return ref.at[pl.ds((base + r) * ROWS, ROWS), :]
        return ref.at[pl.ds((base + r) * ROWS + h * (ROWS // 2), ROWS // 2), :]

    return slot


def pre_kernel(
    tokens, cos, sin, attn_gain, q_gain, k_gain, cot_hbm, q_hbm, k_hbm, v_hbm, o_hbm,
    q_got, mine, other, raw_hbm, normed_hbm, own_hbm, par_hbm, o_par_hbm, cot_got,
    normed, w_own, w_par, o_own, o_par, raw, q_out, kv_out,
    load_sem, y_sent, y_land, cot_sent, cot_land, z_sent, z_land, x_sent, x_land, core_sent, core_land,
    q_sent, q_land, kv_sent, kv_land, swap_sem, local_sem, out_sem,
):
    zl, x, core = (lax.axis_index(a) for a in CTX)
    zh, y = (lax.axis_index(a) for a in FSDP)
    me = zl * 8 + x * 2 + core
    half = 4 * HD
    waits = []

    def along_y(k):
        return {"y": lax.rem(y + k, 4)}

    def along_x(k):
        return {"x": lax.rem(x + k, 4)}

    other_core = {"core": 1 - core}
    cross = {"zl": 1 - zl, "zh": 1 - zh}
    q_width, k_width = q_hbm.shape[1], k_hbm.shape[1]
    pieces = (
        (q_hbm, w_own.at[:, pl.ds(0, q_width)]),
        (k_hbm, w_own.at[:, pl.ds(q_width, k_width)]),
        (v_hbm, w_own.at[:, pl.ds(q_width + k_width, k_width)]),
        (o_hbm, o_own),
    )
    loads = [pltpu.make_async_copy(src, dst, load_sem.at[i]) for i, (src, dst) in enumerate(pieces)]
    for load in loads:
        load.start()
    own_cot = pltpu.make_async_copy(cot_hbm, cot_got.at[pl.ds(0, ROWS), :], local_sem.at[0])
    own_cot.start()
    rows_in = tokens[...].astype(F32)
    normed[:ROWS, :] = (rows_in * inverse_rms(rows_in) * attn_gain[...]).astype(BF16)
    peers([ctx_at(lax.rem(me + k, 16)) for k in range(1, 16)] + [along_y(k) for k in (1, 2, 3)] + [cross])

    normed_pass, normed_finish = gather_ring(row_slots(normed), along_y, y_sent, y_land, waits)
    for load in loads:
        load.wait()

    def shard_stage(src, dst, first):
        eighth = src.shape[0] // 8

        def piece(ref, at_x, at_core):
            return ref.at[pl.ds(pl.multiple_of((at_x * 2 + at_core) * eighth, eighth), eighth), :]

        over_z = remote(piece(src, x, core), piece(dst, x, core), z_sent.at[first], z_land.at[first], cross)
        over_z.start()
        waits.append(over_z)

        def to_core(k):
            at_x = lax.rem(x + k, 4)
            copy = remote(
                piece(dst, at_x, core), piece(dst, at_x, core), core_sent.at[first * 4 + k],
                core_land.at[first * 4 + k], other_core,
            )
            copy.start()
            waits.append(copy)
            return copy

        def next_stage():
            over_z.wait_recv()
            copies = []
            for k in (1, 3, 2):
                copy = remote(
                    piece(dst, x, core), piece(dst, x, core), x_sent.at[first * 4 + k],
                    x_land.at[first * 4 + 4 - k], along_x(k),
                )
                copy.start()
                copies.append((4 - k, copy))
            waits.extend(copy for _, copy in copies)
            cores = [to_core(0)]

            def last_stage():
                for k, copy in copies:
                    copy.wait_recv()
                    cores.append(to_core(k))

                def finish():
                    for copy in cores:
                        copy.wait_recv()

                return finish

            return last_stage

        return next_stage

    def prepared(value, gain):
        scaled = value * inverse_rms(value) * gain
        turned = jnp.concatenate([-scaled[:, HD // 2 :], scaled[:, : HD // 2]], axis=1)
        return (scaled * cos[...] + turned * sin[...]).astype(BF16)

    def unit_copy(src, dst, sent, landed, dest):
        return remote(block(src, dest), block(dst, me), sent.at[dest], landed.at[me], ctx_at(dest))

    def units(s, side):
        rows = slice(s * ROWS, (s + 1) * ROWS)
        unit = s * 4 + side * 2
        for g in range(2):
            at = side * half + g * HD
            q_out[(unit + g) * ROWS : (unit + g + 1) * ROWS, :] = prepared(raw[rows, at : at + HD], q_gain[...])
        at = side * half + 2 * HD
        kv_out[unit * ROWS : (unit + 1) * ROWS, :] = prepared(raw[rows, at : at + HD], k_gain[...])
        kv_out[(unit + 1) * ROWS : (unit + 2) * ROWS, :] = raw[rows, at + HD : at + 2 * HD].astype(BF16)
        for g in range(2):
            dest = unit + lax.rem(me + g, 2)

            @pl.when(dest != me)
            def _():
                unit_copy(kv_out, mine, kv_sent, kv_land, dest).start()
                unit_copy(q_out, q_got, q_sent, q_land, dest).start()

    def own_side(s):
        rows = slice(s * ROWS, (s + 1) * ROWS)
        raw[rows, :half] = dot(normed[rows, :], w_own[...])
        units(s, 0)

    qkv_stage = shard_stage(w_own, w_par, 0)
    o_stage = shard_stage(o_own, o_par, 1)
    own_side(0)
    qkv_stage = qkv_stage()
    o_stage = o_stage()
    normed_pass()
    cot_pass, cot_finish = gather_ring(row_slots(cot_got), along_y, cot_sent, cot_land, waits, cot_hbm)
    own_side(1)
    own_side(3)
    qkv_finish = qkv_stage()
    normed_finish()
    own_side(2)
    qkv_finish()
    raw[:, half:] = dot(normed[...], w_par[...])
    for s in (2, 3, 1, 0):
        units(s, 1)
    o_finish = o_stage()
    cot_pass()
    local = [
        pltpu.make_async_copy(block(q_out, me), block(q_got, me), local_sem.at[1]),
        pltpu.make_async_copy(block(kv_out, me), block(mine, me), local_sem.at[2]),
    ]
    for copy in local:
        copy.start()
    o_finish()
    outs = [
        pltpu.make_async_copy(src, dst, out_sem.at[i])
        for i, (src, dst) in enumerate(
            ((raw, raw_hbm), (normed, normed_hbm), (w_own, own_hbm), (w_par, par_hbm), (o_par, o_par_hbm))
        )
    ]
    for copy in outs:
        copy.start()

    def from_unit(src, dst, sent, landed, source):
        return remote(block(src, source), block(dst, source), sent.at[source], landed.at[source], ctx_at(source))

    local[1].wait()

    @pl.loop(0, 16)
    def _(source):
        @pl.when(source != me)
        def _():
            from_unit(kv_out, mine, kv_sent, kv_land, source).wait_recv()

    swap = remote(mine, other, swap_sem.at[0], swap_sem.at[1], other_core)
    swap.start()

    @pl.loop(0, 16)
    def _(source):
        @pl.when(source != me)
        def _():
            from_unit(q_out, q_got, q_sent, q_land, source).wait_recv()
            from_unit(q_out, q_got, q_sent, q_land, source).wait_send()
            from_unit(kv_out, mine, kv_sent, kv_land, source).wait_send()

    cot_finish()
    swap.wait()
    local[0].wait()
    own_cot.wait()
    for copy in outs:
        copy.wait()
    for copy in waits:
        copy.wait_send()


def pre(tokens, cos, sin, attn_gain, q_gain, k_gain, cot, q_w, k_w, v_w, o_w):
    rows, model = tokens.shape
    wide = q_w.shape[1] + k_w.shape[1] + v_w.shape[1]
    anywhere = pl.BlockSpec(memory_space=pl.ANY)
    vmem = pl.BlockSpec(memory_space=pltpu.VMEM)
    dma = pltpu.SemaphoreType.DMA
    unit = jax.ShapeDtypeStruct((16 * rows, HD), BF16)
    return pl.pallas_call(
        pre_kernel,
        out_shape=(
            unit,
            unit,
            unit,
            jax.ShapeDtypeStruct((4 * rows, 2 * wide), F32),
            jax.ShapeDtypeStruct((4 * rows, model), BF16),
            jax.ShapeDtypeStruct((model, wide), BF16),
            jax.ShapeDtypeStruct((model, wide), BF16),
            jax.ShapeDtypeStruct(o_w.shape, BF16),
            jax.ShapeDtypeStruct((4 * rows, model), BF16),
        ),
        in_specs=[vmem] * 6 + [anywhere] * 5,
        out_specs=(anywhere,) * 9,
        scratch_shapes=[
            pltpu.VMEM((4 * rows, model), BF16),
            pltpu.VMEM((model, wide), BF16),
            pltpu.VMEM((model, wide), BF16),
            pltpu.VMEM(o_w.shape, BF16),
            pltpu.VMEM(o_w.shape, BF16),
            pltpu.VMEM((4 * rows, 2 * wide), F32),
            pltpu.VMEM((16 * rows, HD), BF16),
            pltpu.VMEM((16 * rows, HD), BF16),
            dma((4,)),
            dma((4,)),
            dma((4,)),
            dma((4,)),
            dma((4,)),
            dma((2,)),
            dma((2,)),
            dma((8,)),
            dma((8,)),
            dma((8,)),
            dma((8,)),
            dma((16,)),
            dma((16,)),
            dma((16,)),
            dma((16,)),
            dma((2,)),
            dma((3,)),
            dma((5,)),
        ],
        compiler_params=pltpu.CompilerParams(
            collective_id=3, has_side_effects=True, vmem_limit_bytes=58 * 2**20
        ),
        cost_estimate=pl.CostEstimate(
            flops=2 * 4 * rows * model * 2 * wide, bytes_accessed=24 * 2**20, transcendentals=0
        ),
        name="pre",
    )(tokens, cos, sin, attn_gain, q_gain, k_gain, cot, q_w, k_w, v_w, o_w)


def middle_kernel(
    tokens, cot, gain, att_hbm, o_own_hbm, o_par_hbm, cot_hbm, gate_hbm, up_hbm, down_hbm,
    middle, middle_grad, gain_grad, gate_wgrad, up_wgrad, down_wgrad, grad_got, att_out, branch_out, part_hbm,
    att, o_own, o_par, relay, o_got, hid, cots, gate_w, up_w, down_w, act_grad, gu_grad, act, parts, got, z_out, z_got,
    part, stage, tiles, tile_relay, tile_got, tile_z, down_sum, branch_all, att_grad,
    load_sem, att_sent, att_land, o_sent, o_land, hid_sent, hid_land, far_sent, far_land, across_sent, across_land,
    near_back_sent, near_back_land, far_back_sent, far_back_land, cot_sent, cot_land, part_sent, part_land,
    branch_sent, branch_land, grad_sent, grad_land, core_sent, core_land, x_sent, x_land, zl_sent, zl_land,
    out_sem, local_sem,
):
    zl, x, core = (lax.axis_index(a) for a in CTX)
    zh, y = (lax.axis_index(a) for a in FSDP)
    me = zl * 8 + x * 2 + core
    half = 4 * ROWS
    width = gate_w.shape[1]
    model = hid.shape[1]
    side = 2 * HD
    waits = []

    def along(k):
        return {"y": lax.rem(y + k, 4)}

    def along_x(k):
        return {"x": lax.rem(x + k, 4)}

    across = {"zh": 1 - zh}
    other_core = {"core": 1 - core}
    loads = [
        pltpu.make_async_copy(src, dst, load_sem.at[i])
        for i, (src, dst) in enumerate(
            (
                (o_own_hbm, o_own),
                (o_par_hbm, o_par),
                (cot_hbm, cots.at[pl.ds(0, half), :]),
                (down_hbm, down_w),
                (gate_hbm, gate_w),
                (up_hbm, up_w),
            )
        )
    ]
    for load in loads:
        load.start()
    peers([ctx_at(lax.rem(me + k, 16)) for k in range(1, 16)] + [along(1), along(2), along(3), across])

    def att_at(unit):
        return att.at[
            pl.ds(pl.multiple_of(unit // 4 * ROWS, ROWS), ROWS), pl.ds(pl.multiple_of(lax.rem(unit, 4) * HD, HD), HD)
        ]

    def att_copy(dest, source):
        return remote(block(att_hbm, dest), att_at(source), att_sent.at[dest], att_land.at[source], ctx_at(dest))

    @pl.loop(1, 16)
    def _(k):
        att_copy(lax.rem(me + k, 16), me).start()

    own_att = pltpu.make_async_copy(block(att_hbm, me), att_at(me), local_sem.at[0])
    own_att.start()
    cot_copies = {
        r: remote(row_slots(cot_hbm)(r), row_slots(cots)(4 + r), cot_sent.at[r], cot_land.at[r], across) for r in range(4)
    }
    for r in (0, 1, 3):
        cot_copies[r].start()
    waits.extend(cot_copies.values())
    loads[0].wait()
    loads[1].wait()
    own_att.wait()

    @pl.loop(1, 16)
    def _(k):
        att_copy(lax.rem(me + k, 16), lax.rem(me + k, 16)).wait_recv()

    def scattered(base, got_base, relay_at, sent, landed):
        slots = row_slots(parts, base)

        def halves(ref, first):
            return lambda r, h: row_slots(ref, first)(r, h)

        def relay_half(h):
            return relay.at[pl.ds(relay_at * ROWS + h * (ROWS // 2), ROWS // 2), :]

        return scatter_ring(slots, relay_half, halves(got, got_base), along, sent, landed, waits)

    def summed(base, got_base):
        value = parts[base * ROWS : (base + 1) * ROWS, :].astype(F32)
        for i in range(2):
            value += got[(got_base + i) * ROWS : (got_base + i + 1) * ROWS, :].astype(F32)
        return value

    @pl.loop(0, model // WIDE)
    def _(n):
        cols = pl.ds(pl.multiple_of(n * WIDE, WIDE), WIDE)
        value = dot(att[:, :side], o_own[:, cols]) + dot(att[:, side:], o_par[:, cols])
        parts[pl.ds(0, half), cols] = value.astype(BF16)

    o_waits = []
    o_pass, o_finish = scatter_ring(
        row_slots(parts),
        lambda h: relay.at[pl.ds(h * (ROWS // 2), ROWS // 2), :],
        lambda r, h: row_slots(o_got)(r, h),
        along, o_sent, o_land, o_waits,
    )

    def grads_of_cot(first, count):
        rows = pl.ds(first, count)

        @pl.loop(0, width // WIDE)
        def _(n):
            cols = pl.ds(pl.multiple_of(n * WIDE, WIDE), WIDE)
            act_grad[rows, cols] = dot(cots[rows, :], down_w[cols, :], ((1,), (1,))).astype(BF16)

    loads[2].wait()
    loads[3].wait()
    grads_of_cot(0, half)
    o_pass()
    o_finish()
    value = tokens[...].astype(F32) + parts[:ROWS, :].astype(F32)
    for i in range(2):
        value += o_got[i * ROWS : (i + 1) * ROWS, :].astype(F32)
    middle[...] = value
    hid[:ROWS, :] = (value * inverse_rms(value) * gain[...]).astype(BF16)

    hid_pass, hid_finish = gather_ring(row_slots(hid), along, hid_sent, hid_land, waits)
    hid_across = remote(row_slots(hid)(0), row_slots(hid)(4), across_sent.at[0], across_land.at[0], across)
    hid_across.start()
    waits.append(hid_across)
    loads[4].wait()
    loads[5].wait()
    for copy in o_waits:
        copy.wait_send()
    hid_pass()
    hid_across.wait_recv()
    far_pass, far_finish = gather_ring(row_slots(hid, 4), along, far_sent, far_land, waits)
    cot_copies[2].start()

    def forward(first, count):
        rows = pl.ds(first, count)

        @pl.loop(0, width // WIDE)
        def _(n):
            cols = pl.ds(pl.multiple_of(n * WIDE, WIDE), WIDE)
            gate = dot(hid[rows, :], gate_w[:, cols])
            up = dot(hid[rows, :], up_w[:, cols])
            sig = jax.nn.sigmoid(gate)
            silu = gate * sig
            grad = act_grad[rows, cols].astype(F32)
            act[rows, cols] = (silu * up).astype(BF16)
            gu_grad[rows, cols] = (grad * up * sig * (1.0 + gate * (1.0 - sig))).astype(BF16)
            gu_grad[rows, pl.ds(pl.multiple_of(width + n * WIDE, WIDE), WIDE)] = (grad * silu).astype(BF16)

    def backward(first, count):
        rows = pl.ds(first, count)

        @pl.loop(0, model // WIDE)
        def _(n):
            cols = pl.ds(pl.multiple_of(n * WIDE, WIDE), WIDE)
            value = dot(gu_grad[rows, :width], gate_w[cols, :], ((1,), (1,)))
            value += dot(gu_grad[rows, width:], up_w[cols, :], ((1,), (1,)))
            parts[rows, cols] = value.astype(BF16)

    forward(0, 2 * ROWS)
    forward(3 * ROWS, ROWS)
    hid_finish()
    forward(2 * ROWS, ROWS)
    cot_copies[0].wait_recv()
    cot_copies[1].wait_recv()
    grads_of_cot(half, 2 * ROWS)
    cot_copies[3].wait_recv()
    grads_of_cot(7 * ROWS, ROWS)
    far_pass()
    backward(0, half)
    forward(half, 2 * ROWS)
    forward(7 * ROWS, ROWS)
    backward(half, 2 * ROWS)
    backward(7 * ROWS, ROWS)
    cot_copies[2].wait_recv()
    grads_of_cot(6 * ROWS, ROWS)
    far_finish()
    forward(6 * ROWS, ROWS)
    backward(6 * ROWS, ROWS)
    far_back_pass, far_back_finish = scattered(4, 2, 0, far_back_sent, far_back_land)
    near_back_pass, near_back_finish = scattered(0, 0, 1, near_back_sent, near_back_land)

    def tile_pair(p, which):
        def columns(ref):
            return jnp.concatenate(
                [ref[:, pl.ds(pl.multiple_of(((2 * p + i) * 2 + which) * ROWS, ROWS), ROWS)] for i in range(2)], axis=1
            )

        return dot(columns(hid), gu_grad[...], ((0,), (0,))), dot(columns(cots), act[...], ((0,), (0,)))

    def pair_copy(b, p):
        return remote(stage.at[b], tiles.at[pl.ds(2 * p, 2)], core_sent.at[p], core_land.at[p], other_core)

    @pl.loop(0, 2)
    def _(m):
        for b in range(2):
            p = m * 2 + b

            @pl.when(m > 0)
            def _():
                pair_copy(b, p - 2).wait_send()

            gate_up, down = tile_pair(p, 1 - core)
            for i in range(2):
                stage[b, i, :, : 2 * width] = gate_up[i * ROWS : (i + 1) * ROWS].astype(BF16)
                stage[b, i, :, 2 * width :] = down[i * ROWS : (i + 1) * ROWS].astype(BF16)
            pair_copy(b, p).start()

    far_back_pass()

    @pl.loop(0, 2)
    def _(m):
        for b in range(2):
            p = m * 2 + b
            gate_up, down = tile_pair(p, core)
            pair_copy(b, p).wait_recv()
            for i in range(2):
                at = 2 * p + i
                near = tiles[at]
                value = gate_up[i * ROWS : (i + 1) * ROWS] + near[:, : 2 * width].astype(F32)
                tiles[at, :, : 2 * width] = value.astype(BF16)
                value = down[i * ROWS : (i + 1) * ROWS] + near[:, 2 * width :].astype(F32)
                tiles[at, :, 2 * width :] = value.astype(BF16)

    tile_pass, tile_finish = scatter_ring(
        lambda k, h: tiles.at[h * 4 + lax.rem(x + k, 4)],
        lambda h: tile_relay.at[h],
        lambda r, h: tile_got.at[r, h],
        along_x, x_sent, x_land, waits,
    )
    near_back_pass()
    far_back_finish()
    z_out[...] = summed(4, 2).astype(BF16)
    z_copy = remote(z_out, z_got, across_sent.at[1], across_land.at[1], across)
    z_copy.start()
    waits.append(z_copy)

    def down_part(first):
        rows = pl.ds(first, half)

        @pl.loop(0, model // WIDE)
        def _(n):
            cols = pl.ds(pl.multiple_of(n * WIDE, WIDE), WIDE)
            part[rows, cols] = dot(act[rows, :], down_w[:, cols]).astype(BF16)

    down_part(half)
    down_part(0)
    outs = [
        pltpu.make_async_copy(part.at[pl.ds(half, half), :], part_hbm, out_sem.at[0]),
        pltpu.make_async_copy(att, att_out, out_sem.at[1]),
    ]
    for copy in outs:
        copy.start()
    tile_pass()
    near_back_finish()
    z_copy.wait_recv()

    rows_back, gain_sum = rms_back(summed(0, 0) + z_got[...].astype(F32), middle[...], gain[...])
    gain_grad[...] = gain_sum
    value = cot[...].astype(F32) + rows_back
    middle_grad[...] = value
    branch_all[:ROWS, :] = value.astype(BF16)

    branch_pass, branch_finish = gather_ring(row_slots(branch_all), along, branch_sent, branch_land, waits)

    def unit_of(unit):
        return att_grad.at[
            pl.ds(pl.multiple_of(unit // 4 * ROWS, ROWS), ROWS), pl.ds(pl.multiple_of(lax.rem(unit, 4) * HD, HD), HD)
        ]

    def grad_copy(dest, source):
        return remote(unit_of(dest), block(grad_got, source), grad_sent.at[dest], grad_land.at[source], ctx_at(dest))

    def to_units(s):
        rows = slice(s * ROWS, (s + 1) * ROWS)
        att_grad[rows, :side] = dot(branch_all[rows, :], o_own[...], ((1,), (1,))).astype(BF16)
        att_grad[rows, side:] = dot(branch_all[rows, :], o_par[...], ((1,), (1,))).astype(BF16)

        @pl.loop(0, 4)
        def _(j):
            dest = s * 4 + lax.rem(me + j, 4)

            @pl.when(dest != me)
            def _():
                grad_copy(dest, me).start()

    to_units(0)
    branch_pass()
    to_units(1)
    to_units(3)
    branch_finish()
    to_units(2)
    own_grad = pltpu.make_async_copy(unit_of(me), block(grad_got, me), local_sem.at[1])
    own_grad.start()
    part_pass, part_finish = scatter_ring(
        row_slots(part),
        lambda h: relay.at[pl.ds(h * (ROWS // 2), ROWS // 2), :],
        lambda r, h: row_slots(o_got)(r, h),
        along, part_sent, part_land, waits,
    )
    branch_copy = pltpu.make_async_copy(branch_all, branch_out, out_sem.at[2])
    branch_copy.start()
    outs.append(branch_copy)

    tile_finish()

    def tile_sum(a):
        value = tiles[a * 4 + x].astype(F32)
        for i in range(2):
            value += tile_got[i, a].astype(F32)
        return value

    for b in range(2):
        pair_copy(b, 2 + b).wait_send()
    stage[0, 0] = tile_sum(1 - zl).astype(BF16)
    tile_copy = remote(stage.at[0, 0], tile_z, zl_sent, zl_land, {"zl": 1 - zl})
    tile_copy.start()
    waits.append(tile_copy)
    value = tile_sum(zl)
    gate_wgrad[...] = value[:, :width]
    up_wgrad[...] = value[:, width : 2 * width]
    down_sum[...] = value[:, 2 * width :]
    part_pass()

    @pl.loop(1, 16)
    def _(k):
        peer = lax.rem(me + k, 16)
        grad_copy(peer, peer).wait_recv()
        grad_copy(peer, peer).wait_send()
        att_copy(peer, peer).wait_send()

    tile_copy.wait_recv()
    gate_wgrad[...] += tile_z[:, :width].astype(F32)
    up_wgrad[...] += tile_z[:, width : 2 * width].astype(F32)
    down = down_sum[...] + tile_z[:, 2 * width :].astype(F32)
    for i in range(width // HD):
        down_wgrad[i * HD : (i + 1) * HD, :] = down[:, i * HD : (i + 1) * HD].T
    own_grad.wait()
    part_finish()
    value = middle[...] + part[:ROWS, :].astype(F32)
    for i in range(2):
        value += o_got[i * ROWS : (i + 1) * ROWS, :].astype(F32)
    middle[...] = value
    for copy in waits:
        copy.wait_send()
    for copy in outs:
        copy.wait()


def middle_part(tokens, cot, gain, att, o_own, o_par, cot_half, gate_w, up_w, down_w):
    rows, model = tokens.shape
    width = gate_w.shape[1]
    anywhere = pl.BlockSpec(memory_space=pl.ANY)
    vmem = pl.BlockSpec(memory_space=pltpu.VMEM)
    dma = pltpu.SemaphoreType.DMA
    half = jax.ShapeDtypeStruct((4 * rows, model), BF16)
    low = functools.partial(pltpu.VMEM, dtype=BF16)
    return pl.pallas_call(
        middle_kernel,
        out_shape=(
            jax.ShapeDtypeStruct((rows, model), F32),
            jax.ShapeDtypeStruct((rows, model), F32),
            jax.ShapeDtypeStruct((1, model), F32),
            jax.ShapeDtypeStruct((rows, width), F32),
            jax.ShapeDtypeStruct((rows, width), F32),
            jax.ShapeDtypeStruct((width, rows), F32),
            jax.ShapeDtypeStruct((16 * rows, HD), BF16),
            jax.ShapeDtypeStruct((4 * rows, 4 * HD), BF16),
            half,
            half,
        ),
        in_specs=[vmem] * 3 + [anywhere] * 7,
        out_specs=(vmem,) * 6 + (anywhere,) * 4,
        scratch_shapes=[
            low((4 * rows, 4 * HD)),
            low((2 * HD, model)),
            low((2 * HD, model)),
            low((2 * rows, model)),
            low((2 * rows, model)),
            low((8 * rows, model)),
            low((8 * rows, model)),
            low((model, width)),
            low((model, width)),
            low((width, model)),
            low((8 * rows, width)),
            low((8 * rows, 2 * width)),
            low((8 * rows, width)),
            low((8 * rows, model)),
            low((4 * rows, model)),
            low((rows, model)),
            low((rows, model)),
            low((8 * rows, model)),
            low((2, 2, rows, 3 * width)),
            low((8, rows, 3 * width)),
            low((2, rows, 3 * width)),
            low((2, 2, rows, 3 * width)),
            low((rows, 3 * width)),
            pltpu.VMEM((rows, width), F32),
            low((4 * rows, model)),
            low((4 * rows, 4 * HD)),
            dma((6,)),
            dma((16,)),
            dma((16,)),
            dma((6,)),
            dma((6,)),
            dma((4,)),
            dma((4,)),
            dma((4,)),
            dma((4,)),
            dma((2,)),
            dma((2,)),
            dma((6,)),
            dma((6,)),
            dma((6,)),
            dma((6,)),
            dma((4,)),
            dma((4,)),
            dma((6,)),
            dma((6,)),
            dma((4,)),
            dma((4,)),
            dma((16,)),
            dma((16,)),
            dma((4,)),
            dma((4,)),
            dma((6,)),
            dma((6,)),
            dma,
            dma,
            dma((3,)),
            dma((2,)),
        ],
        compiler_params=pltpu.CompilerParams(
            collective_id=1, has_side_effects=True, vmem_limit_bytes=63 * 2**20
        ),
        cost_estimate=pl.CostEstimate(
            flops=2 * 9 * 8 * rows * model * width, bytes_accessed=40 * 2**20, transcendentals=8 * rows * width
        ),
        name="middle",
    )(tokens, cot, gain, att, o_own, o_par, cot_half, gate_w, up_w, down_w)


def back_kernel(
    q_grad, keep, send, raw, cos, sin, q_gain, k_gain, tokens, middle_grad, attn_gain, mlp_gain_grad,
    middle, normed_hbm, own_hbm, par_hbm, branch_hbm, att_hbm, part_hbm,
    tokens_grad, out_rows, q_wgrad, k_wgrad, v_wgrad, o_wgrad, attn_total, mlp_total, q_total, k_total,
    normed, w_own, w_par, branch_all, att, part, out_got, relay, out_across, swap_got, kv_out, q_got, kv_got, low, parts, y_got,
    core_out, core_got, red, x_relay, x_got, z_out, z_low, z_got, o_core_out, o_core_got, o_red, o_x_relay, o_x_got, o_z_out, o_z_low, o_z_got,
    g_out, g_got,
    load_sem, swap_sem, across_sem, q_sent, q_land, kv_sent, kv_land, y_sent, y_land, out_sent, out_land,
    core_sent, core_land, x_sent, x_land, z_sent, z_land, g_sent, g_land,
):
    zl, x, core = (lax.axis_index(a) for a in CTX)
    zh, y = (lax.axis_index(a) for a in FSDP)
    me = zl * 8 + x * 2 + core
    half = 4 * HD

    def along_y(k):
        return {"y": lax.rem(y + k, 4)}

    def along_x(k):
        return {"x": lax.rem(x + k, 4)}

    def along_ctx(k):
        return ctx_at(lax.rem(me + k, 16))

    other_core = {"core": 1 - core}
    zs = {1: {"zl": 1 - zl}, 2: {"zh": 1 - zh}, 3: {"zl": 1 - zl, "zh": 1 - zh}}

    loads = [
        pltpu.make_async_copy(src, dst, load_sem.at[i])
        for i, (src, dst) in enumerate(
            (
                (part_hbm, part),
                (branch_hbm, branch_all),
                (att_hbm, att),
                (normed_hbm, normed),
                (own_hbm, w_own),
                (par_hbm, w_par),
            )
        )
    ]
    for load in loads:
        load.start()
    peers([along_ctx(k) for k in range(1, 16)] + [along_y(k) for k in (1, 2, 3)] + [zs[2], zs[3]])

    swap = remote(send, swap_got, swap_sem.at[0], swap_sem.at[1], other_core)
    swap.start()

    waits = [swap]

    def to_rows(src, dst, sent, landed):
        copies = []
        for k in range(1, 16):
            copy = remote(block(src, lax.rem(me + k, 16)), block(dst, 16 - k), sent.at[k], landed.at[16 - k], along_ctx(k))
            copy.start()
            copies.append(copy)
        waits.extend(copies)
        return copies

    q_copies = to_rows(q_grad, q_got, q_sent, q_land)
    mine = pl.ds(pl.multiple_of(me * ROWS, ROWS), ROWS)
    q_got[:ROWS, :] = q_grad[mine, :]
    swap.wait_recv()
    kv_out[...] = (keep[...] + swap_got[...].astype(F32)).astype(BF16)
    kv_copies = to_rows(kv_out, kv_got, kv_sent, kv_land)
    kv_got[:ROWS, :] = kv_out[mine, :]

    loads[0].wait()
    out_pass, out_finish = scatter_ring(
        row_slots(part),
        lambda h: relay.at[pl.ds(h * (ROWS // 2), ROWS // 2), :],
        lambda r, h: row_slots(out_got)(r, h),
        along_y, out_sent, out_land, waits,
    )

    def grad_stages(first, tile, to_other, from_other, summed, x_relay, from_x, total, total_low, from_z):
        n = total.shape[2] // 2

        def over_cores():
            @pl.loop(0, 8)
            def _(t):
                to_other[t] = tile(t * 2 + 1 - core).astype(BF16)

            copy = remote(to_other, from_other, core_sent.at[first], core_land.at[first], other_core)
            copy.start()
            waits.append(copy)
            return copy

        def over_x(core_copy):
            core_copy.wait_recv()

            @pl.loop(0, 8)
            def _(t):
                summed[t] = (tile(t * 2 + core) + from_other[t].astype(F32)).astype(BF16)

            return scatter_ring(
                lambda k, h: summed.at[h * 4 + lax.rem(x + k, 4)],
                lambda h: x_relay.at[h],
                lambda r, h: from_x.at[r, h],
                along_x, x_sent.at[first], x_land.at[first], waits,
            )

        def over_z(x_finish):
            x_finish()
            for a in range(2):
                value = summed[a * 4 + x].astype(F32)
                for i in range(2):
                    value += from_x[i, a].astype(F32)
                total[a] = value
                total_low[a] = value.astype(BF16)
            copies = []
            for d in (1, 2, 3):
                rows_of = 1 - zl if d % 2 else zl
                copy = remote(
                    total_low.at[rows_of, :, pl.ds(n if d >= 2 else 0, n)], from_z.at[d - 1],
                    z_sent.at[first * 3 + d - 1], z_land.at[first * 3 + d - 1], zs[d],
                )
                copy.start()
                copies.append(copy)
            waits.extend(copies)
            return copies

        def finish(z_copies):
            for copy in z_copies:
                copy.wait_recv()
            value = total[zl, :, :n]
            for d in range(3):
                value = value + from_z[d].astype(F32)
            return value

        return over_cores, over_x, over_z, finish

    def tile_of(left, right):
        def tile(t):
            cols = pl.ds(pl.multiple_of(t * ROWS, ROWS), ROWS)
            return dot(left[:, cols], right[...], ((0,), (0,)))

        return tile

    qkv_cores, qkv_x, qkv_z, qkv_finish = grad_stages(
        0, tile_of(normed, low), core_out, core_got, red, x_relay, x_got, z_out, z_low, z_got
    )
    o_cores, o_x, o_z, o_finish = grad_stages(
        1, tile_of(branch_all, att), o_core_out, o_core_got, o_red, o_x_relay, o_x_got, o_z_out, o_z_low, o_z_got
    )
    loads[1].wait()
    loads[2].wait()
    o_x_pass, o_x_finish = o_x(o_cores())
    out_pass()
    for load in loads[3:]:
        load.wait()
    for copy in q_copies:
        copy.wait_recv()
    for copy in kv_copies:
        copy.wait_recv()

    g_out[0] = jnp.zeros_like(g_out[0])

    def from_unit(ref, unit):
        return ref[pl.ds(pl.multiple_of(lax.rem(unit - me + 16, 16) * ROWS, ROWS), ROWS), :]

    def head_back(grad, value, gain):
        turned = grad * sin[...]
        turned = jnp.concatenate([turned[:, HD // 2 :], -turned[:, : HD // 2]], axis=1)
        back, gain_sum = rms_back(grad * cos[...] + turned, value, gain)
        return back.astype(BF16), gain_sum

    @pl.loop(0, 4)
    def _(s):
        rows = pl.ds(pl.multiple_of(s * ROWS, ROWS), ROWS)
        for h in range(4):
            at = (h // 2) * half + (h % 2) * HD
            cols = slice(at, at + HD)
            grad = from_unit(q_got, s * 4 + h).astype(F32)
            back, gain_sum = head_back(grad, raw[rows, cols], q_gain[...])
            low[rows, cols] = back
            g_out[0, 32:33, :] += gain_sum
        for kv in range(2):
            at = kv * half + 2 * HD
            cols = slice(at, at + HD)
            grad = from_unit(kv_got, s * 4 + kv * 2).astype(F32)
            back, gain_sum = head_back(grad, raw[rows, cols], k_gain[...])
            low[rows, cols] = back
            g_out[0, 33:34, :] += gain_sum
            low[rows, at + HD : at + 2 * HD] = from_unit(kv_got, s * 4 + kv * 2 + 1)

    core_copy = qkv_cores()
    out_finish()
    value = part[:ROWS, :].astype(F32)
    for i in range(2):
        value += out_got[i * ROWS : (i + 1) * ROWS, :].astype(F32)
    part[:ROWS, :] = value.astype(BF16)
    across_copy = remote(part.at[pl.ds(0, ROWS), :], out_across, across_sem.at[0], across_sem.at[1], zs[2])
    across_copy.start()
    waits.append(across_copy)

    @pl.loop(0, parts.shape[1] // WIDE)
    def _(n):
        cols = pl.ds(pl.multiple_of(n * WIDE, WIDE), WIDE)
        total = dot(low[:, :half], w_own[cols, :], ((1,), (1,)))
        total += dot(low[:, half:], w_par[cols, :], ((1,), (1,)))
        parts[:, cols] = total.astype(BF16)

    o_x_pass()
    y_pass, y_finish = scatter_ring(
        row_slots(parts),
        lambda h: relay.at[pl.ds(ROWS + h * (ROWS // 2), ROWS // 2), :],
        lambda r, h: row_slots(y_got)(r, h),
        along_y, y_sent, y_land, waits,
    )

    x_pass, x_finish = qkv_x(core_copy)
    y_pass()
    x_pass()
    o_z_copies = o_z(o_x_finish)

    across_copy.wait_recv()
    out_rows[...] = (middle[...] + out_across[...].astype(F32)).astype(BF16)
    y_finish()
    grad = parts[:ROWS, :].astype(F32)
    for i in range(2):
        grad += y_got[i * ROWS : (i + 1) * ROWS, :].astype(F32)
    rows_back, gain_sum = rms_back(grad, tokens[...].astype(F32), attn_gain[...])
    tokens_grad[...] = (middle_grad[...] + rows_back).astype(BF16)
    for i in range(16):
        g_out[0, i : i + 1, :] = gain_sum[:, i * HD : (i + 1) * HD]
        g_out[0, 16 + i : 17 + i, :] = mlp_gain_grad[:, i * HD : (i + 1) * HD]

    def gain_stage(stage, places):
        copies = []
        for i, (place, back_slot) in enumerate(places):
            copy = remote(
                g_out.at[stage], g_got.at[stage, back_slot], g_sent.at[stage * 3 + i],
                g_land.at[stage * 3 + back_slot], place,
            )
            copy.start()
            copies.append(copy)
        waits.extend(copies)
        return copies

    def gain_sum_of(stage, copies):
        for copy in copies:
            copy.wait_recv()
        total = g_out[stage]
        for i in range(len(copies)):
            total = total + g_got[stage, i]
        return total

    copies = gain_stage(0, [(along_y(k), 3 - k) for k in (1, 2, 3)])

    z_copies = qkv_z(x_finish)
    value = o_finish(o_z_copies)
    for i in range(2):
        o_wgrad[i * HD : (i + 1) * HD, :] = value[:, i * HD : (i + 1) * HD].T
    g_out[1] = gain_sum_of(0, copies)
    copies = gain_stage(1, [(along_x(k), 3 - k) for k in (1, 2, 3)])
    g_out[2] = gain_sum_of(1, copies)
    copies = gain_stage(2, [(zs[d], d - 1) for d in (1, 2, 3)])
    value = qkv_finish(z_copies)
    q_wgrad[...] = value[:, : 2 * HD]
    k_wgrad[...] = value[:, 2 * HD : 3 * HD]
    v_wgrad[...] = value[:, 3 * HD :]
    g_out[3] = gain_sum_of(2, copies)
    copies = gain_stage(3, [(other_core, 0)])
    gains = gain_sum_of(3, copies)
    for i in range(16):
        attn_total[:, i * HD : (i + 1) * HD] = gains[i : i + 1, :]
        mlp_total[:, i * HD : (i + 1) * HD] = gains[16 + i : 17 + i, :]
    q_total[...] = gains[32:33, :]
    k_total[...] = gains[33:34, :]
    for copy in waits:
        copy.wait_send()


def back(q_grad, keep, send, raw, cos, sin, q_gain, k_gain, tokens, middle_grad, attn_gain, mlp_gain_grad,
         middle, normed, w_own, w_par, branch_all, att, part):
    rows, model = tokens.shape
    wide = raw.shape[1]
    anywhere = pl.BlockSpec(memory_space=pl.ANY)
    vmem = pl.BlockSpec(memory_space=pltpu.VMEM)
    dma = pltpu.SemaphoreType.DMA
    return pl.pallas_call(
        back_kernel,
        out_shape=(
            jax.ShapeDtypeStruct((rows, model), BF16),
            jax.ShapeDtypeStruct((rows, model), BF16),
            jax.ShapeDtypeStruct((rows, 2 * HD), F32),
            jax.ShapeDtypeStruct((rows, HD), F32),
            jax.ShapeDtypeStruct((rows, HD), F32),
            jax.ShapeDtypeStruct((2 * HD, rows), F32),
            jax.ShapeDtypeStruct((1, model), F32),
            jax.ShapeDtypeStruct((1, model), F32),
            jax.ShapeDtypeStruct((1, HD), F32),
            jax.ShapeDtypeStruct((1, HD), F32),
        ),
        in_specs=[vmem] * 13 + [anywhere] * 6,
        out_specs=(vmem,) * 10,
        scratch_shapes=[
            pltpu.VMEM((4 * rows, model), BF16),
            pltpu.VMEM((model, wide // 2), BF16),
            pltpu.VMEM((model, wide // 2), BF16),
            pltpu.VMEM((4 * rows, model), BF16),
            pltpu.VMEM((4 * rows, 4 * HD), BF16),
            pltpu.VMEM((4 * rows, model), BF16),
            pltpu.VMEM((2 * rows, model), BF16),
            pltpu.VMEM((2 * rows, model), BF16),
            pltpu.VMEM((rows, model), BF16),
            pltpu.VMEM((16 * rows, HD), BF16),
            pltpu.VMEM((16 * rows, HD), BF16),
            pltpu.VMEM((16 * rows, HD), BF16),
            pltpu.VMEM((16 * rows, HD), BF16),
            pltpu.VMEM((4 * rows, wide), BF16),
            pltpu.VMEM((4 * rows, model), BF16),
            pltpu.VMEM((2 * rows, model), BF16),
            pltpu.VMEM((8, rows, wide), BF16),
            pltpu.VMEM((8, rows, wide), BF16),
            pltpu.VMEM((8, rows, wide), BF16),
            pltpu.VMEM((2, rows, wide), BF16),
            pltpu.VMEM((2, 2, rows, wide), BF16),
            pltpu.VMEM((2, rows, wide), F32),
            pltpu.VMEM((2, rows, wide), BF16),
            pltpu.VMEM((3, rows, wide // 2), BF16),
            pltpu.VMEM((8, rows, 4 * HD), BF16),
            pltpu.VMEM((8, rows, 4 * HD), BF16),
            pltpu.VMEM((8, rows, 4 * HD), BF16),
            pltpu.VMEM((2, rows, 4 * HD), BF16),
            pltpu.VMEM((2, 2, rows, 4 * HD), BF16),
            pltpu.VMEM((2, rows, 4 * HD), F32),
            pltpu.VMEM((2, rows, 4 * HD), BF16),
            pltpu.VMEM((3, rows, 2 * HD), BF16),
            pltpu.VMEM((4, 40, HD), F32),
            pltpu.VMEM((4, 3, 40, HD), F32),
            dma((6,)),
            dma((2,)),
            dma((2,)),
            dma((16,)),
            dma((16,)),
            dma((16,)),
            dma((16,)),
            dma((6,)),
            dma((6,)),
            dma((6,)),
            dma((6,)),
            dma((2,)),
            dma((2,)),
            dma((2, 6)),
            dma((2, 6)),
            dma((6,)),
            dma((6,)),
            dma((12,)),
            dma((12,)),
        ],
        compiler_params=pltpu.CompilerParams(
            collective_id=2, has_side_effects=True, vmem_limit_bytes=58 * 2**20
        ),
        cost_estimate=pl.CostEstimate(
            flops=4 * 4 * rows * model * wide, bytes_accessed=24 * 2**20, transcendentals=0
        ),
        name="back",
    )(
        q_grad, keep, send, raw, cos, sin, q_gain, k_gain, tokens, middle_grad, attn_gain, mlp_gain_grad,
        middle, normed, w_own, w_par, branch_all, att, part,
    )


def per_device(
    tokens,
    cotangent,
    attn_gain,
    q_weight,
    k_weight,
    v_weight,
    q_gain,
    k_gain,
    o_weight,
    mlp_gain,
    gate_weight,
    up_weight,
    down_weight,
    doc_lengths,
    block_place,
):
    rows = tokens.shape[1]
    zl, x, core = (lax.axis_index(a) for a in CTX)
    zh, y = (lax.axis_index(a) for a in FSDP)
    ctx_place = zl * 8 + x * 2 + core
    sequence = zh * 4 + lax.rem(y + ctx_place // 4, 4)
    ends = jnp.cumsum(lax.dynamic_index_in_dim(doc_lengths, sequence, 0, keepdims=False))
    ends = ends.astype(jnp.int32)
    core_flag = core.astype(jnp.int32).reshape(1)
    own_blocks = lax.dynamic_slice_in_dim(block_place, ctx_place * (rows // BLK), rows // BLK)
    own_positions = (own_blocks[:, None] * BLK + jnp.arange(BLK, dtype=jnp.int32)[None, :]).reshape(-1)
    cos_rows, sin_rows = tables(own_positions, HD)
    q_gain, k_gain = q_gain.reshape(1, HD), k_gain.reshape(1, HD)
    attn_gain, mlp_gain = attn_gain.reshape(1, -1), mlp_gain.reshape(1, -1)
    cot = cotangent[0]

    q_in, mine, other, raw, normed, w_own, w_par, o_par, cot_half = pre(
        tokens[0], cos_rows, sin_rows, attn_gain, q_gain, k_gain, cot, q_weight, k_weight, v_weight, o_weight
    )
    out, q_pos, k_pos, v_pos, log_total = attend(block_place, ends, core_flag, q_in, mine, other)
    (
        middle, middle_grad, mlp_gain_grad, gate_wgrad, up_wgrad, down_wgrad, grad_in, att, branch_all, part,
    ) = middle_part(tokens[0], cot, mlp_gain, out, o_weight, o_par, cot_half, gate_weight, up_weight, down_weight)
    q_grad, keep_grad, send_grad = attend_back(
        block_place, ends, core_flag, grad_in, q_pos, k_pos, v_pos, log_total
    )
    (
        tokens_grad, out_rows, q_wgrad, k_wgrad, v_wgrad, o_wgrad, attn_gain_grad, mlp_gain_grad, q_gain_grad, k_gain_grad,
    ) = back(
        q_grad, keep_grad, send_grad, raw, cos_rows, sin_rows, q_gain, k_gain, tokens[0], middle_grad, attn_gain,
        mlp_gain_grad, middle, normed, w_own, w_par, branch_all, att, part,
    )
    return (
        out_rows[None],
        tokens_grad[None],
        attn_gain_grad[0],
        q_wgrad,
        k_wgrad,
        v_wgrad,
        q_gain_grad[0],
        k_gain_grad[0],
        o_wgrad,
        mlp_gain_grad[0],
        gate_wgrad,
        up_wgrad,
        down_wgrad,
    )


def solution(mesh):
    fine = Mesh(mesh.devices.reshape(SIZES), AXES)
    rows = P(FSDP, CTX, None)
    in_specs = (
        rows,
        rows,
        P(),
        P(None, FSDP),
        P(None, FSDP),
        P(None, FSDP),
        P(),
        P(),
        P(FSDP, None),
        P(),
        P(None, FSDP),
        P(None, FSDP),
        P(FSDP, None),
        P(),
        P(),
    )
    out_specs = (
        rows,
        rows,
        P(),
        P(CTX, FSDP),
        P(CTX, FSDP),
        P(CTX, FSDP),
        P(),
        P(),
        P(FSDP, CTX),
        P(),
        P(CTX, FSDP),
        P(CTX, FSDP),
        P(FSDP, CTX),
    )
    return jax.shard_map(
        per_device, mesh=fine, in_specs=in_specs, out_specs=out_specs, check_vma=False
    )
```

```python
import functools

import jax
import jax.numpy as jnp
from jax import lax
from jax.experimental import pallas as pl
from jax.experimental.pallas import tpu as pltpu
from jax.sharding import Mesh, PartitionSpec as P

EPSILON = 1e-06
ROPE_BASE = 1000000.0
MASKED_SCORE = -1e30
HD = 128
BLK = 64
AXES = ("zl", "x", "core", "zh", "y")
SIZES = (2, 4, 2, 2, 4)
CTX = ("zl", "x", "core")
FSDP = ("zh", "y")
F32 = jnp.float32
BF16 = jnp.bfloat16


def tables(positions, head_dim):
    exponent_steps = jnp.arange(head_dim // 2, dtype=jnp.int32).astype(F32) * (2.0 / head_dim)
    frequency = ROPE_BASE ** (-exponent_steps)
    phases = positions.astype(F32)[:, None] * frequency[None, :]
    phases = jnp.concatenate([phases, phases], axis=-1)
    return (jnp.cos(phases), jnp.sin(phases))


def dot(left, right, contract=((1,), (0,))):
    return lax.dot_general(left, right, (contract, ((), ())), preferred_element_type=F32)


TILE = 256


def keep_mask(ends, first_row, rows, cols):
    place = first_row + lax.broadcasted_iota(jnp.int32, (rows, 1), 0)
    start = jnp.zeros((rows, 1), jnp.int32)
    for end in ends:
        start = jnp.where(place >= end, end, start)
    key = lax.broadcasted_iota(jnp.int32, (rows, cols), 1)
    return (key >= start) & (key <= place)


def ordered(order, blocks, pairs):
    @pl.loop(0, blocks)
    def _(b):
        rows = pl.ds(pl.multiple_of(b * BLK, BLK), BLK)
        for src, dst in pairs:
            dst[rows, :] = src[order[b]]


def attend(ends, q_pos, k_pos, v_pos, out_pos, log_total):
    for i in range(q_pos.shape[0] // TILE):
        span = pl.ds(i * TILE, TILE)
        n = (i + 1) * TILE
        scores = dot(q_pos[span, :], k_pos[:n, :], ((1,), (1,))) * HD ** (-0.5)
        scores = jnp.where(keep_mask(ends, i * TILE, TILE, n), scores, MASKED_SCORE)
        top = jnp.max(scores, axis=-1, keepdims=True)
        weights = jnp.exp(scores - top)
        total = jnp.sum(weights, axis=-1, keepdims=True)
        log_total[span, :] = top + jnp.log(total)
        probs = (weights * (1.0 / total)).astype(BF16)
        out_pos[i * TILE // BLK : n // BLK] = dot(probs, v_pos[:n, :]).astype(BF16).reshape(TILE // BLK, BLK, HD)


def attend_back(ends, q_pos, k_pos, v_pos, log_total, grad_pos, q_acc, k_acc, v_acc):
    scale = HD ** (-0.5)
    k_acc[...] = jnp.zeros_like(k_acc)
    v_acc[...] = jnp.zeros_like(v_acc)
    for i in range(q_pos.shape[0] // TILE):
        span = pl.ds(i * TILE, TILE)
        n = (i + 1) * TILE
        queries = q_pos[span, :]
        grads = grad_pos[span, :]
        scores = dot(queries, k_pos[:n, :], ((1,), (1,))) * scale
        kept = keep_mask(ends, i * TILE, TILE, n)
        probs = jnp.where(kept, jnp.exp(scores - log_total[span, :]), 0.0)
        prob_grad = dot(grads, v_pos[:n, :], ((1,), (1,)))
        row_dot = jnp.sum(prob_grad * probs, axis=-1, keepdims=True)
        score_grad = (probs * (prob_grad - row_dot)).astype(BF16)
        q_rows = (dot(score_grad, k_pos[:n, :]) * scale).astype(BF16)
        q_acc[i * TILE // BLK : n // BLK] = q_rows.reshape(TILE // BLK, BLK, HD)
        k_acc[: n // BLK] += dot(score_grad, queries, ((0,), (0,))).reshape(n // BLK, BLK, HD)
        v_acc[: n // BLK] += dot(probs.astype(BF16), grads, ((0,), (0,))).reshape(n // BLK, BLK, HD)


def document_ends(doc_lengths, sequence):
    ends = [doc_lengths[sequence, 0]]
    for j in range(1, doc_lengths.shape[1]):
        ends.append(ends[-1] + doc_lengths[sequence, j])
    return ends


def peers(pairs):
    barrier = pltpu.get_barrier_semaphore()
    for place in pairs:
        pl.semaphore_signal(barrier, inc=1, device_id=place, device_id_type=pl.DeviceIdType.MESH)
    pl.semaphore_wait(barrier, len(pairs))


def remote(src, dst, sent, landed, place):
    return pltpu.make_async_remote_copy(
        src_ref=src, dst_ref=dst, send_sem=sent, recv_sem=landed, device_id=place,
        device_id_type=pl.DeviceIdType.MESH,
    )


ROWS = 128
WIDE = 256


def ctx_at(index):
    return {"zl": index // 8, "x": lax.rem(index // 2, 4), "core": lax.rem(index, 2)}


def block(ref, index):
    return ref.at[pl.ds(pl.multiple_of(index * ROWS, ROWS), ROWS), :]


def pair(ref, index):
    return ref.at[pl.ds(index * 2, 2)]


def inverse_rms(values):
    return lax.rsqrt(jnp.mean(values * values, axis=-1, keepdims=True) + EPSILON)


def rms_back(grad, values, gain):
    inverse = inverse_rms(values)
    scaled = grad * gain
    inner = jnp.mean(values * scaled, axis=-1, keepdims=True)
    back = inverse * scaled - values * (inverse * inverse * inverse * inner)
    return back, jnp.sum(grad * values * inverse, axis=0, keepdims=True)


def gather_ring(slot, along, sent, landed, waits, own=None):
    def move(src, dst, i, k):
        copy = remote(src, dst, sent.at[i], landed.at[i], along(k))
        copy.start()
        waits.append(copy)
        return copy

    own = slot(0) if own is None else own
    near = [move(own, slot(1), 0, 3), move(own, slot(3), 1, 1)]
    far = []

    def pass_on():
        for h, k in ((0, 3), (1, 1)):
            near[h].wait_recv()
            far.append(move(slot(1 + 2 * h, h), slot(2, h), 2 + h, k))

    def finish():
        for copy in far:
            copy.wait_recv()

    return pass_on, finish


def scatter_ring(part, relay, got, along, sent, landed, waits):
    def move(src, dst, i, k):
        copy = remote(src, dst, sent.at[i], landed.at[i], along(k))
        copy.start()
        waits.append(copy)
        return copy

    first = [move(part(2, 0), relay(0), 0, 1), move(part(2, 1), relay(1), 1, 3)]
    last = [move(part(1, 1), got(0, 1), 2, 1), move(part(3, 0), got(1, 0), 3, 3)]

    def pass_on():
        for h, k in ((0, 1), (1, 3)):
            first[h].wait_recv()
            ref = part(k, h)
            ref[...] = (ref[...].astype(F32) + relay(h)[...].astype(F32)).astype(BF16)
            last.append(move(ref, got(h, h), 4 + h, k))

    def finish():
        for copy in last:
            copy.wait_recv()

    return pass_on, finish


def row_slots(ref, base=0):
    def slot(r, h=None):
        if h is None:
            return ref.at[pl.ds((base + r) * ROWS, ROWS), :]
        return ref.at[pl.ds((base + r) * ROWS + h * (ROWS // 2), ROWS // 2), :]

    return slot


def pre_kernel(
    place, stored, doc_lengths, tokens, cos, sin, attn_gain, q_gain, k_gain, cot_hbm, q_hbm, k_hbm, v_hbm, o_hbm,
    log_total, out_hbm, q_hbm_out, k_hbm_out, v_hbm_out, raw_hbm, normed_hbm, own_hbm, par_hbm, o_par_hbm, cot_got,
    q_got, mine, other, q_pos, k_pos, v_pos, out_pos, out, normed, w_own, w_par, o_own, o_par, raw, q_out, kv_out,
    load_sem, y_sent, y_land, cot_sent, cot_land, z_sent, z_land, x_sent, x_land, core_sent, core_land,
    q_sent, q_land, kv_sent, kv_land, swap_sem, local_sem, out_sem,
):
    zl, x, core = (lax.axis_index(a) for a in CTX)
    zh, y = (lax.axis_index(a) for a in FSDP)
    me = zl * 8 + x * 2 + core
    half = 4 * HD
    waits = []

    def along_y(k):
        return {"y": lax.rem(y + k, 4)}

    def along_x(k):
        return {"x": lax.rem(x + k, 4)}

    other_core = {"core": 1 - core}
    cross = {"zl": 1 - zl, "zh": 1 - zh}
    q_width, k_width = q_hbm.shape[1], k_hbm.shape[1]
    pieces = (
        (q_hbm, w_own.at[:, pl.ds(0, q_width)]),
        (k_hbm, w_own.at[:, pl.ds(q_width, k_width)]),
        (v_hbm, w_own.at[:, pl.ds(q_width + k_width, k_width)]),
        (o_hbm, o_own),
    )
    loads = [pltpu.make_async_copy(src, dst, load_sem.at[i]) for i, (src, dst) in enumerate(pieces)]
    for load in loads:
        load.start()
    own_cot = pltpu.make_async_copy(cot_hbm, cot_got.at[pl.ds(0, ROWS), :], local_sem.at[0])
    own_cot.start()
    rows_in = tokens[...].astype(F32)
    normed[:ROWS, :] = (rows_in * inverse_rms(rows_in) * attn_gain[...]).astype(BF16)
    peers([ctx_at(lax.rem(me + k, 16)) for k in range(1, 16)] + [along_y(k) for k in (1, 2, 3)] + [cross])

    normed_pass, normed_finish = gather_ring(row_slots(normed), along_y, y_sent, y_land, waits)
    for load in loads:
        load.wait()

    def shard_stage(src, dst, first):
        eighth = src.shape[0] // 8

        def piece(ref, at_x, at_core):
            return ref.at[pl.ds(pl.multiple_of((at_x * 2 + at_core) * eighth, eighth), eighth), :]

        over_z = remote(piece(src, x, core), piece(dst, x, core), z_sent.at[first], z_land.at[first], cross)
        over_z.start()
        waits.append(over_z)

        def to_core(k):
            at_x = lax.rem(x + k, 4)
            copy = remote(
                piece(dst, at_x, core), piece(dst, at_x, core), core_sent.at[first * 4 + k],
                core_land.at[first * 4 + k], other_core,
            )
            copy.start()
            waits.append(copy)
            return copy

        def next_stage():
            over_z.wait_recv()
            copies = []
            for k in (1, 3, 2):
                copy = remote(
                    piece(dst, x, core), piece(dst, x, core), x_sent.at[first * 4 + k],
                    x_land.at[first * 4 + 4 - k], along_x(k),
                )
                copy.start()
                copies.append((4 - k, copy))
            waits.extend(copy for _, copy in copies)
            cores = [to_core(0)]

            def last_stage():
                for k, copy in copies:
                    copy.wait_recv()
                    cores.append(to_core(k))

                def finish():
                    for copy in cores:
                        copy.wait_recv()

                return finish

            return last_stage

        return next_stage

    def prepared(value, gain):
        scaled = value * inverse_rms(value) * gain
        turned = jnp.concatenate([-scaled[:, HD // 2 :], scaled[:, : HD // 2]], axis=1)
        return (scaled * cos[...] + turned * sin[...]).astype(BF16)

    def unit_copy(src, dst, sent, landed, dest):
        return remote(pair(src, dest), pair(dst, me), sent.at[dest], landed.at[me], ctx_at(dest))

    def put(ref, unit, value):
        ref[unit * 2 : unit * 2 + 2] = value.reshape(2, BLK, HD)

    def units(s, side):
        rows = slice(s * ROWS, (s + 1) * ROWS)
        unit = s * 4 + side * 2
        for g in range(2):
            at = side * half + g * HD
            put(q_out, unit + g, prepared(raw[rows, at : at + HD], q_gain[...]))
        at = side * half + 2 * HD
        put(kv_out, unit, prepared(raw[rows, at : at + HD], k_gain[...]))
        put(kv_out, unit + 1, raw[rows, at + HD : at + 2 * HD].astype(BF16))
        for g in range(2):
            dest = unit + lax.rem(me + g, 2)

            @pl.when(dest != me)
            def _():
                unit_copy(kv_out, mine, kv_sent, kv_land, dest).start()
                unit_copy(q_out, q_got, q_sent, q_land, dest).start()

    def own_side(s):
        rows = slice(s * ROWS, (s + 1) * ROWS)
        raw[rows, :half] = dot(normed[rows, :], w_own[...])
        units(s, 0)

    qkv_stage = shard_stage(w_own, w_par, 0)
    o_stage = shard_stage(o_own, o_par, 1)
    own_side(0)
    qkv_stage = qkv_stage()
    o_stage = o_stage()
    normed_pass()
    cot_pass, cot_finish = gather_ring(row_slots(cot_got), along_y, cot_sent, cot_land, waits, cot_hbm)
    own_side(1)
    own_side(3)
    qkv_finish = qkv_stage()
    normed_finish()
    own_side(2)
    qkv_finish()
    raw[:, half:] = dot(normed[...], w_par[...])
    for s in (2, 3, 1, 0):
        units(s, 1)
    o_finish = o_stage()
    local = [
        pltpu.make_async_copy(pair(q_out, me), pair(q_got, me), local_sem.at[1]),
        pltpu.make_async_copy(pair(kv_out, me), pair(mine, me), local_sem.at[2]),
    ]
    for copy in local:
        copy.start()
    o_finish()
    outs = [
        pltpu.make_async_copy(src, dst, out_sem.at[i])
        for i, (src, dst) in enumerate(
            ((raw, raw_hbm), (normed, normed_hbm), (w_own, own_hbm), (w_par, par_hbm), (o_par, o_par_hbm))
        )
    ]
    for copy in outs:
        copy.start()

    def from_unit(src, dst, sent, landed, source):
        return remote(pair(src, source), pair(dst, source), sent.at[source], landed.at[source], ctx_at(source))

    local[1].wait()

    @pl.loop(0, 16)
    def _(source):
        @pl.when(source != me)
        def _():
            from_unit(kv_out, mine, kv_sent, kv_land, source).wait_recv()

    swap = remote(mine, other, swap_sem.at[0], swap_sem.at[1], other_core)
    swap.start()

    @pl.loop(0, 16)
    def _(source):
        @pl.when(source != me)
        def _():
            from_unit(q_out, q_got, q_sent, q_land, source).wait_recv()
            from_unit(q_out, q_got, q_sent, q_land, source).wait_send()
            from_unit(kv_out, mine, kv_sent, kv_land, source).wait_send()

    swap.wait()
    local[0].wait()
    cot_pass()

    blocks = q_pos.shape[0] // BLK

    @pl.when(core == 0)
    def _():
        ordered(stored, blocks, ((q_got, q_pos), (mine, k_pos), (other, v_pos)))

    @pl.when(core == 1)
    def _():
        ordered(stored, blocks, ((q_got, q_pos), (other, k_pos), (mine, v_pos)))

    more = [
        pltpu.make_async_copy(src, dst, out_sem.at[5 + i])
        for i, (src, dst) in enumerate(((q_pos, q_hbm_out), (k_pos, k_hbm_out), (v_pos, v_hbm_out)))
    ]
    for copy in more:
        copy.start()
    outs.extend(more)
    ends = document_ends(doc_lengths, zh * 4 + lax.rem(y + me // 4, 4))
    attend(ends, q_pos, k_pos, v_pos, out_pos, log_total)
    ordered(place, blocks, ((out_pos, out),))
    out_copy = pltpu.make_async_copy(out, out_hbm, out_sem.at[8])
    out_copy.start()
    outs.append(out_copy)
    cot_finish()
    own_cot.wait()
    for copy in outs:
        copy.wait()
    for copy in waits:
        copy.wait_send()


def pre(place, stored, doc_lengths, tokens, cos, sin, attn_gain, q_gain, k_gain, cot, q_w, k_w, v_w, o_w):
    rows, model = tokens.shape
    wide = q_w.shape[1] + k_w.shape[1] + v_w.shape[1]
    anywhere = pl.BlockSpec(memory_space=pl.ANY)
    vmem = pl.BlockSpec(memory_space=pltpu.VMEM)
    dma = pltpu.SemaphoreType.DMA
    unit = jax.ShapeDtypeStruct((16 * rows, HD), BF16)
    return pl.pallas_call(
        pre_kernel,
        out_shape=(
            jax.ShapeDtypeStruct((16 * rows, 1), F32),
            unit,
            unit,
            unit,
            unit,
            jax.ShapeDtypeStruct((4 * rows, 2 * wide), F32),
            jax.ShapeDtypeStruct((4 * rows, model), BF16),
            jax.ShapeDtypeStruct((model, wide), BF16),
            jax.ShapeDtypeStruct((model, wide), BF16),
            jax.ShapeDtypeStruct(o_w.shape, BF16),
            jax.ShapeDtypeStruct((4 * rows, model), BF16),
        ),
        in_specs=[pl.BlockSpec(memory_space=pltpu.SMEM)] * 3 + [vmem] * 6 + [anywhere] * 5,
        out_specs=(vmem,) + (anywhere,) * 10,
        scratch_shapes=[pltpu.VMEM((16 * rows // BLK, BLK, HD), BF16)] * 3
        + [pltpu.VMEM((16 * rows, HD), BF16)] * 3
        + [pltpu.VMEM((16 * rows // BLK, BLK, HD), BF16), pltpu.VMEM((16 * rows, HD), BF16)]
        + [
            pltpu.VMEM((4 * rows, model), BF16),
            pltpu.VMEM((model, wide), BF16),
            pltpu.VMEM((model, wide), BF16),
            pltpu.VMEM(o_w.shape, BF16),
            pltpu.VMEM(o_w.shape, BF16),
            pltpu.VMEM((4 * rows, 2 * wide), F32),
            pltpu.VMEM((16 * rows // BLK, BLK, HD), BF16),
            pltpu.VMEM((16 * rows // BLK, BLK, HD), BF16),
            dma((4,)),
            dma((4,)),
            dma((4,)),
            dma((4,)),
            dma((4,)),
            dma((2,)),
            dma((2,)),
            dma((8,)),
            dma((8,)),
            dma((8,)),
            dma((8,)),
            dma((16,)),
            dma((16,)),
            dma((16,)),
            dma((16,)),
            dma((2,)),
            dma((3,)),
            dma((9,)),
        ],
        compiler_params=pltpu.CompilerParams(
            collective_id=3, has_side_effects=True, vmem_limit_bytes=58 * 2**20
        ),
        cost_estimate=pl.CostEstimate(
            flops=2 * 4 * rows * model * 2 * wide, bytes_accessed=24 * 2**20, transcendentals=0
        ),
        name="pre",
    )(place, stored, doc_lengths, tokens, cos, sin, attn_gain, q_gain, k_gain, cot, q_w, k_w, v_w, o_w)


def middle_kernel(
    tokens, cot, gain, att_hbm, o_own_hbm, o_par_hbm, cot_hbm, gate_hbm, up_hbm, down_hbm,
    middle, middle_grad, gain_grad, gate_wgrad, up_wgrad, down_wgrad, grad_got, att_out, branch, part_hbm, o_full,
    att, o_own, o_par, relay, o_got, hid, cots, gate_w, up_w, down_w, act_grad, gu_grad, act, parts, got, z_out, z_got,
    part, stage, tiles, tile_relay, tile_got, tile_z, down_sum, att_grad,
    load_sem, att_sent, att_land, o_sent, o_land, hid_sent, hid_land, far_sent, far_land, across_sent, across_land,
    near_back_sent, near_back_land, far_back_sent, far_back_land, cot_sent, cot_land, part_sent, part_land,
    oy_sent, oy_land, ox_sent, ox_land, oc_sent, oc_land, grad_sent, grad_land, core_sent, core_land, x_sent, x_land, zl_sent, zl_land,
    out_sem, local_sem, oload_sem,
):
    zl, x, core = (lax.axis_index(a) for a in CTX)
    zh, y = (lax.axis_index(a) for a in FSDP)
    me = zl * 8 + x * 2 + core
    half = 4 * ROWS
    width = gate_w.shape[1]
    model = hid.shape[1]
    side = 2 * HD
    waits = []

    def along(k):
        return {"y": lax.rem(y + k, 4)}

    def along_x(k):
        return {"x": lax.rem(x + k, 4)}

    across = {"zh": 1 - zh}
    other_core = {"core": 1 - core}
    loads = [
        pltpu.make_async_copy(src, dst, load_sem.at[i])
        for i, (src, dst) in enumerate(
            (
                (o_own_hbm, o_own),
                (o_par_hbm, o_par),
                (cot_hbm, cots.at[pl.ds(0, half), :]),
                (down_hbm, down_w),
                (gate_hbm, gate_w),
                (up_hbm, up_w),
            )
        )
    ]
    for load in loads:
        load.start()
    barrier = pltpu.get_barrier_semaphore()
    places = [ctx_at(lax.rem(me + k, 16)) for k in range(1, 16)] + [along(1), along(2), along(3), across]
    for place in places:
        pl.semaphore_signal(barrier, inc=1, device_id=place, device_id_type=pl.DeviceIdType.MESH)

    @pl.when(me >= 4)
    def _():
        @pl.loop(0, 16)
        def _(k):
            place = dict(ctx_at(lax.rem(me + k, 16)), **along(me // 4))
            pl.semaphore_signal(barrier, inc=1, device_id=place, device_id_type=pl.DeviceIdType.MESH)

    pl.semaphore_wait(barrier, len(places) + 12)

    def att_at(unit):
        return att.at[
            pl.ds(pl.multiple_of(unit // 4 * ROWS, ROWS), ROWS), pl.ds(pl.multiple_of(lax.rem(unit, 4) * HD, HD), HD)
        ]

    def att_copy(dest, source):
        return remote(block(att_hbm, dest), att_at(source), att_sent.at[dest], att_land.at[source], ctx_at(dest))

    @pl.loop(1, 16)
    def _(k):
        att_copy(lax.rem(me + k, 16), me).start()

    own_att = pltpu.make_async_copy(block(att_hbm, me), att_at(me), local_sem.at[0])
    own_att.start()
    cot_copies = [
        remote(row_slots(cot_hbm)(r), row_slots(cots)(4 + r), cot_sent.at[r], cot_land.at[r], across) for r in range(4)
    ]
    cot_copies[0].start()
    cot_copies[1].start()
    waits.extend(cot_copies)

    def o_rows(k, h, at, count):
        return o_full.at[pl.ds(pl.multiple_of(k * half + h * side + at, 16), count), :]

    piece = core * HD + x * (ROWS // 4)
    oy_rings = []
    for h, src in ((0, o_own_hbm), (1, o_par_hbm)):

        def slot(k, part_of=None, h=h):
            if part_of is None:
                return o_rows(k, h, piece, ROWS // 4)
            return o_rows(k, h, piece + part_of * (ROWS // 8), ROWS // 8)

        own_piece = src.at[pl.ds(pl.multiple_of(piece, ROWS // 4), ROWS // 4), :]
        oy_rings.append(gather_ring(slot, along, oy_sent.at[h], oy_land.at[h], waits, own_piece))

    def ox_move(k, h, at_x, i, to):
        ref = o_rows(k, h, core * HD + at_x * (ROWS // 4), ROWS // 4)
        copy = remote(ref, ref, ox_sent.at[i, k - 1, h], ox_land.at[i, k - 1, h], along_x(to))
        copy.start()
        waits.append(copy)
        return copy

    def ox_start():
        return [ox_move(k, h, x, i, to) for k in (1, 2, 3) for h in (0, 1) for i, to in ((0, 3), (1, 1))]

    def ox_pass(near):
        for copy in near:
            copy.wait_recv()
        far = [ox_move(k, 0, lax.rem(x + 1, 4), 2, 3) for k in (1, 2, 3)]
        return far + [ox_move(k, 1, lax.rem(x + 3, 4), 2, 1) for k in (1, 2, 3)]

    def o_cores(far):
        for copy in far:
            copy.wait_recv()
        copies = []
        for k in (1, 2, 3):
            for h in (0, 1):
                ref = o_rows(k, h, core * HD, HD)
                copy = remote(ref, ref, oc_sent.at[k - 1, h], oc_land.at[k - 1, h], other_core)
                copy.start()
                copies.append(copy)
        waits.extend(copies)
        return copies

    loads[0].wait()
    loads[1].wait()
    own_att.wait()

    @pl.loop(1, 16)
    def _(k):
        att_copy(lax.rem(me + k, 16), lax.rem(me + k, 16)).wait_recv()

    for ring_pass, _ in oy_rings:
        ring_pass()

    def scattered(base, got_base, relay_at, sent, landed):
        slots = row_slots(parts, base)

        def halves(ref, first):
            return lambda r, h: row_slots(ref, first)(r, h)

        def relay_half(h):
            return relay.at[pl.ds(relay_at * ROWS + h * (ROWS // 2), ROWS // 2), :]

        return scatter_ring(slots, relay_half, halves(got, got_base), along, sent, landed, waits)

    def summed(base, got_base):
        value = parts[base * ROWS : (base + 1) * ROWS, :].astype(F32)
        for i in range(2):
            value += got[(got_base + i) * ROWS : (got_base + i + 1) * ROWS, :].astype(F32)
        return value

    @pl.loop(0, model // WIDE)
    def _(n):
        cols = pl.ds(pl.multiple_of(n * WIDE, WIDE), WIDE)
        value = dot(att[:, :side], o_own[:, cols]) + dot(att[:, side:], o_par[:, cols])
        parts[pl.ds(0, half), cols] = value.astype(BF16)

    o_waits = []
    o_pass, o_finish = scatter_ring(
        row_slots(parts),
        lambda h: relay.at[pl.ds(h * (ROWS // 2), ROWS // 2), :],
        lambda r, h: row_slots(o_got)(r, h),
        along, o_sent, o_land, o_waits,
    )

    def grads_of_cot(first, count):
        rows = pl.ds(first, count)

        @pl.loop(0, width // WIDE)
        def _(n):
            cols = pl.ds(pl.multiple_of(n * WIDE, WIDE), WIDE)
            act_grad[rows, cols] = dot(cots[rows, :], down_w[cols, :], ((1,), (1,))).astype(BF16)

    for _, ring_finish in oy_rings:
        ring_finish()
    o_near = ox_start()
    loads[2].wait()
    loads[3].wait()
    grads_of_cot(0, half)
    o_pass()
    o_finish()
    value = tokens[...].astype(F32) + parts[:ROWS, :].astype(F32)
    for i in range(2):
        value += o_got[i * ROWS : (i + 1) * ROWS, :].astype(F32)
    middle[...] = value
    hid[:ROWS, :] = (value * inverse_rms(value) * gain[...]).astype(BF16)

    hid_waits = []
    hid_pass, hid_finish = gather_ring(row_slots(hid), along, hid_sent, hid_land, hid_waits)
    hid_across = remote(row_slots(hid)(0), row_slots(hid)(4), across_sent.at[0], across_land.at[0], across)
    hid_across.start()
    hid_waits.append(hid_across)
    loads[4].wait()
    loads[5].wait()
    for copy in o_waits:
        copy.wait_send()
    hid_pass()
    hid_across.wait_recv()
    far_pass, far_finish = gather_ring(row_slots(hid, 4), along, far_sent, far_land, hid_waits)
    cot_copies[3].start()
    cot_copies[2].start()

    def forward(first, count):
        rows = pl.ds(first, count)

        @pl.loop(0, width // WIDE)
        def _(n):
            cols = pl.ds(pl.multiple_of(n * WIDE, WIDE), WIDE)
            gate = dot(hid[rows, :], gate_w[:, cols])
            up = dot(hid[rows, :], up_w[:, cols])
            sig = jax.nn.sigmoid(gate)
            silu = gate * sig
            grad = act_grad[rows, cols].astype(F32)
            act[rows, cols] = (silu * up).astype(BF16)
            gu_grad[rows, cols] = (grad * up * sig * (1.0 + gate * (1.0 - sig))).astype(BF16)
            gu_grad[rows, pl.ds(pl.multiple_of(width + n * WIDE, WIDE), WIDE)] = (grad * silu).astype(BF16)

    def backward(first, count):
        rows = pl.ds(first, count)

        @pl.loop(0, model // WIDE)
        def _(n):
            cols = pl.ds(pl.multiple_of(n * WIDE, WIDE), WIDE)
            value = dot(gu_grad[rows, :width], gate_w[cols, :], ((1,), (1,)))
            value += dot(gu_grad[rows, width:], up_w[cols, :], ((1,), (1,)))
            parts[rows, cols] = value.astype(BF16)

    forward(0, 2 * ROWS)
    forward(3 * ROWS, ROWS)
    hid_finish()
    forward(2 * ROWS, ROWS)
    o_far = ox_pass(o_near)
    cot_copies[0].wait_recv()
    cot_copies[1].wait_recv()
    grads_of_cot(half, 2 * ROWS)
    far_pass()
    backward(0, half)
    forward(half, 2 * ROWS)
    cot_copies[3].wait_recv()
    grads_of_cot(7 * ROWS, ROWS)
    forward(7 * ROWS, ROWS)
    backward(half, 2 * ROWS)
    backward(7 * ROWS, ROWS)
    o_core_copies = o_cores(o_far)
    cot_copies[2].wait_recv()
    grads_of_cot(6 * ROWS, ROWS)
    far_finish()
    forward(6 * ROWS, ROWS)
    backward(6 * ROWS, ROWS)
    far_back_pass, far_back_finish = scattered(4, 2, 0, far_back_sent, far_back_land)
    near_back_pass, near_back_finish = scattered(0, 0, 1, near_back_sent, near_back_land)

    def tile_pair(p, which):
        def columns(ref):
            return jnp.concatenate(
                [ref[:, pl.ds(pl.multiple_of(((2 * p + i) * 2 + which) * ROWS, ROWS), ROWS)] for i in range(2)], axis=1
            )

        return dot(columns(hid), gu_grad[...], ((0,), (0,))), dot(columns(cots), act[...], ((0,), (0,)))

    def pair_copy(b, p):
        return remote(stage.at[b], tiles.at[pl.ds(2 * p, 2)], core_sent.at[p], core_land.at[p], other_core)

    @pl.loop(0, 2)
    def _(m):
        for b in range(2):
            p = m * 2 + b

            @pl.when(m > 0)
            def _():
                pair_copy(b, p - 2).wait_send()

            gate_up, down = tile_pair(p, 1 - core)
            for i in range(2):
                stage[b, i, :, : 2 * width] = gate_up[i * ROWS : (i + 1) * ROWS].astype(BF16)
                stage[b, i, :, 2 * width :] = down[i * ROWS : (i + 1) * ROWS].astype(BF16)
            pair_copy(b, p).start()

    far_back_pass()

    @pl.loop(0, 2)
    def _(m):
        for b in range(2):
            p = m * 2 + b
            gate_up, down = tile_pair(p, core)
            pair_copy(b, p).wait_recv()
            for i in range(2):
                at = 2 * p + i
                near = tiles[at]
                value = gate_up[i * ROWS : (i + 1) * ROWS] + near[:, : 2 * width].astype(F32)
                tiles[at, :, : 2 * width] = value.astype(BF16)
                value = down[i * ROWS : (i + 1) * ROWS] + near[:, 2 * width :].astype(F32)
                tiles[at, :, 2 * width :] = value.astype(BF16)

    tile_pass, tile_finish = scatter_ring(
        lambda k, h: tiles.at[h * 4 + lax.rem(x + k, 4)],
        lambda h: tile_relay.at[h],
        lambda r, h: tile_got.at[r, h],
        along_x, x_sent, x_land, waits,
    )
    near_back_pass()
    far_back_finish()
    z_out[...] = summed(4, 2).astype(BF16)
    z_copy = remote(z_out, z_got, across_sent.at[1], across_land.at[1], across)
    z_copy.start()
    waits.append(z_copy)

    def down_part(first):
        rows = pl.ds(first, half)

        @pl.loop(0, model // WIDE)
        def _(n):
            cols = pl.ds(pl.multiple_of(n * WIDE, WIDE), WIDE)
            part[rows, cols] = dot(act[rows, :], down_w[:, cols]).astype(BF16)

    for copy in o_core_copies:
        copy.wait_recv()
    for copy in hid_waits:
        copy.wait_send()
    o_loads = [
        pltpu.make_async_copy(o_full.at[pl.ds(k * half, half), :], ref.at[pl.ds(first, half), :], oload_sem.at[k - 1])
        for k, ref, first in ((1, cots, 0), (2, cots, half), (3, hid, 0))
    ]
    for load in o_loads:
        load.start()
    down_part(0)
    down_part(half)
    outs = [
        pltpu.make_async_copy(part.at[pl.ds(half, half), :], part_hbm, out_sem.at[0]),
        pltpu.make_async_copy(att, att_out, out_sem.at[1]),
    ]
    for copy in outs:
        copy.start()
    part_pass, part_finish = scatter_ring(
        row_slots(part),
        lambda h: relay.at[pl.ds(2 * ROWS + h * (ROWS // 2), ROWS // 2), :],
        lambda r, h: row_slots(o_got)(r, h),
        along, part_sent, part_land, waits,
    )
    tile_pass()
    near_back_finish()
    z_copy.wait_recv()

    rows_back, gain_sum = rms_back(summed(0, 0) + z_got[...].astype(F32), middle[...], gain[...])
    gain_grad[...] = gain_sum
    value = cot[...].astype(F32) + rows_back
    middle_grad[...] = value
    branch[...] = value.astype(BF16)

    def unit_copy(k, h):
        unit = (4 - k) % 4 * 4 + h
        place = dict(ctx_at(unit), **along(k))
        cols = pl.ds(pl.multiple_of((k * 4 + h) * HD, HD), HD)
        return remote(att_grad.at[:, cols], block(grad_got, me), grad_sent.at[k * 4 + h], grad_land.at[me], place)

    for k in range(4):
        at = k * 4 * HD
        if k == 0:
            att_grad[:, :side] = dot(branch[...], o_own[...], ((1,), (1,))).astype(BF16)
            att_grad[:, side : 2 * side] = dot(branch[...], o_par[...], ((1,), (1,))).astype(BF16)
        else:
            o_loads[k - 1].wait()
            rows_of = (cots[:half, :], cots[half:, :], hid[:half, :])[k - 1]
            att_grad[:, at : at + 4 * HD] = dot(branch[...], rows_of, ((1,), (1,))).astype(BF16)

        @pl.loop(0, 4)
        def _(j):
            h = lax.rem(me + j, 4)

            @pl.when((k > 0) | (h != me))
            def _():
                unit_copy(k, h).start()

    def own_grad():
        cols = pl.ds(pl.multiple_of(lax.rem(me, 4) * HD, HD), HD)
        return pltpu.make_async_copy(att_grad.at[:, cols], block(grad_got, me), local_sem.at[1])

    @pl.when(me < 4)
    def _():
        own_grad().start()

    tile_finish()

    def tile_sum(a):
        value = tiles[a * 4 + x].astype(F32)
        for i in range(2):
            value += tile_got[i, a].astype(F32)
        return value

    for b in range(2):
        pair_copy(b, 2 + b).wait_send()
    stage[0, 0] = tile_sum(1 - zl).astype(BF16)
    tile_copy = remote(stage.at[0, 0], tile_z, zl_sent, zl_land, {"zl": 1 - zl})
    tile_copy.start()
    waits.append(tile_copy)
    value = tile_sum(zl)
    gate_wgrad[...] = value[:, :width]
    up_wgrad[...] = value[:, width : 2 * width]
    down_sum[...] = value[:, 2 * width :]
    part_pass()

    @pl.loop(1, 16)
    def _(k):
        peer = lax.rem(me + k, 16)
        att_copy(peer, peer).wait_send()

    @pl.loop(0, 16)
    def _(source):
        @pl.when((me >= 4) | (source != me))
        def _():
            remote(
                att_grad.at[:, pl.ds(0, HD)], block(grad_got, source), grad_sent.at[0], grad_land.at[source], other_core
            ).wait_recv()

    for k in range(4):

        @pl.loop(0, 4)
        def _(h):
            @pl.when((k > 0) | (h != me))
            def _():
                unit_copy(k, h).wait_send()

    @pl.when(me < 4)
    def _():
        own_grad().wait()


    tile_copy.wait_recv()
    gate_wgrad[...] += tile_z[:, :width].astype(F32)
    up_wgrad[...] += tile_z[:, width : 2 * width].astype(F32)
    down = down_sum[...] + tile_z[:, 2 * width :].astype(F32)
    for i in range(width // HD):
        down_wgrad[i * HD : (i + 1) * HD, :] = down[:, i * HD : (i + 1) * HD].T
    part_finish()
    value = middle[...] + part[:ROWS, :].astype(F32)
    for i in range(2):
        value += o_got[i * ROWS : (i + 1) * ROWS, :].astype(F32)
    middle[...] = value
    for copy in waits:
        copy.wait_send()
    for copy in outs:
        copy.wait()


def middle_part(tokens, cot, gain, att, o_own, o_par, cot_half, gate_w, up_w, down_w):
    rows, model = tokens.shape
    width = gate_w.shape[1]
    anywhere = pl.BlockSpec(memory_space=pl.ANY)
    vmem = pl.BlockSpec(memory_space=pltpu.VMEM)
    dma = pltpu.SemaphoreType.DMA
    half = jax.ShapeDtypeStruct((4 * rows, model), BF16)
    low = functools.partial(pltpu.VMEM, dtype=BF16)
    return pl.pallas_call(
        middle_kernel,
        out_shape=(
            jax.ShapeDtypeStruct((rows, model), F32),
            jax.ShapeDtypeStruct((rows, model), F32),
            jax.ShapeDtypeStruct((1, model), F32),
            jax.ShapeDtypeStruct((rows, width), F32),
            jax.ShapeDtypeStruct((rows, width), F32),
            jax.ShapeDtypeStruct((width, rows), F32),
            jax.ShapeDtypeStruct((16 * rows, HD), BF16),
            jax.ShapeDtypeStruct((4 * rows, 4 * HD), BF16),
            jax.ShapeDtypeStruct((rows, model), BF16),
            half,
            jax.ShapeDtypeStruct((16 * HD, model), BF16),
        ),
        in_specs=[vmem] * 3 + [anywhere] * 7,
        out_specs=(vmem,) * 6 + (anywhere,) * 2 + (vmem,) + (anywhere,) * 2,
        scratch_shapes=[
            low((4 * rows, 4 * HD)),
            low((2 * HD, model)),
            low((2 * HD, model)),
            low((3 * rows, model)),
            low((2 * rows, model)),
            low((8 * rows, model)),
            low((8 * rows, model)),
            low((model, width)),
            low((model, width)),
            low((width, model)),
            low((8 * rows, width)),
            low((8 * rows, 2 * width)),
            low((8 * rows, width)),
            low((8 * rows, model)),
            low((4 * rows, model)),
            low((rows, model)),
            low((rows, model)),
            low((8 * rows, model)),
            low((2, 2, rows, 3 * width)),
            low((8, rows, 3 * width)),
            low((2, rows, 3 * width)),
            low((2, 2, rows, 3 * width)),
            low((rows, 3 * width)),
            pltpu.VMEM((rows, width), F32),
            low((rows, 16 * HD)),
            dma((6,)),
            dma((16,)),
            dma((16,)),
            dma((6,)),
            dma((6,)),
            dma((4,)),
            dma((4,)),
            dma((4,)),
            dma((4,)),
            dma((2,)),
            dma((2,)),
            dma((6,)),
            dma((6,)),
            dma((6,)),
            dma((6,)),
            dma((4,)),
            dma((4,)),
            dma((6,)),
            dma((6,)),
            dma((2, 4)),
            dma((2, 4)),
            dma((3, 3, 2)),
            dma((3, 3, 2)),
            dma((3, 2)),
            dma((3, 2)),
            dma((16,)),
            dma((16,)),
            dma((4,)),
            dma((4,)),
            dma((6,)),
            dma((6,)),
            dma,
            dma,
            dma((3,)),
            dma((2,)),
            dma((3,)),
        ],
        compiler_params=pltpu.CompilerParams(
            collective_id=1, has_side_effects=True, vmem_limit_bytes=63 * 2**20
        ),
        cost_estimate=pl.CostEstimate(
            flops=2 * 9 * 8 * rows * model * width, bytes_accessed=40 * 2**20, transcendentals=8 * rows * width
        ),
        name="middle",
    )(tokens, cot, gain, att, o_own, o_par, cot_half, gate_w, up_w, down_w)


def back_kernel(
    place, stored, doc_lengths, log_total, cos, sin, q_gain, k_gain, attn_gain, mlp_gain_grad,
    grad_hbm, q_pos_hbm, k_pos_hbm, v_pos_hbm, part_hbm, branch_hbm, att_hbm, raw_hbm, normed_hbm, own_hbm, par_hbm,
    middle_hbm, tokens_hbm, middle_grad_hbm,
    tokens_grad, out_rows, q_wgrad, k_wgrad, v_wgrad, o_wgrad, attn_total, mlp_total, q_total, k_total,
    grad_in, q_pos, k_pos, v_pos, grad_pos, q_acc, q_grad, send, k_acc, v_acc, keep, raw, middle, tokens, middle_grad,
    normed, w_own, w_par, branch_all, att, part, out_got, relay, out_across, swap_got, kv_out, q_got, kv_got, low, parts, y_got,
    core_out, core_got, red, x_relay, x_got, z_out, z_low, z_got, o_core_out, o_core_got, o_red, o_x_relay, o_x_got, o_z_out, o_z_low, o_z_got,
    g_out, g_got, by_gain,
    load_sem, swap_sem, across_sem, q_sent, q_land, kv_sent, kv_land, y_sent, y_land, out_sent, out_land, branch_sent, branch_land,
    core_sent, core_land, x_sent, x_land, z_sent, z_land, g_sent, g_land,
):
    zl, x, core = (lax.axis_index(a) for a in CTX)
    zh, y = (lax.axis_index(a) for a in FSDP)
    me = zl * 8 + x * 2 + core
    half = 4 * HD

    def along_y(k):
        return {"y": lax.rem(y + k, 4)}

    def along_x(k):
        return {"x": lax.rem(x + k, 4)}

    def along_ctx(k):
        return ctx_at(lax.rem(me + k, 16))

    other_core = {"core": 1 - core}
    zs = {1: {"zl": 1 - zl}, 2: {"zh": 1 - zh}, 3: {"zl": 1 - zl, "zh": 1 - zh}}

    loads = [
        pltpu.make_async_copy(src, dst, load_sem.at[i])
        for i, (src, dst) in enumerate(
            (
                (part_hbm, part),
                (grad_hbm, grad_in),
                (q_pos_hbm, q_pos),
                (k_pos_hbm, k_pos),
                (v_pos_hbm, v_pos),
                (branch_hbm, branch_all.at[pl.ds(0, ROWS), :]),
                (att_hbm, att),
                (normed_hbm, normed),
                (raw_hbm, raw),
                (own_hbm, w_own),
                (par_hbm, w_par),
                (middle_hbm, middle),
                (tokens_hbm, tokens),
                (middle_grad_hbm, middle_grad),
            )
        )
    ]
    for load in loads:
        load.start()
    peers([along_ctx(k) for k in range(1, 16)] + [along_y(k) for k in (1, 2, 3)] + [zs[2], zs[3]])
    waits = []

    loads[5].wait()
    branch_pass, branch_finish = gather_ring(row_slots(branch_all), along_y, branch_sent, branch_land, waits)

    def grad_stages(first, tile, to_other, from_other, summed, x_relay, from_x, total, total_low, from_z):
        n = total.shape[2] // 2

        def over_cores():
            @pl.loop(0, 8)
            def _(t):
                to_other[t] = tile(t * 2 + 1 - core).astype(BF16)

            copy = remote(to_other, from_other, core_sent.at[first], core_land.at[first], other_core)
            copy.start()
            waits.append(copy)
            return copy

        def over_x(core_copy):
            core_copy.wait_recv()

            @pl.loop(0, 8)
            def _(t):
                summed[t] = (tile(t * 2 + core) + from_other[t].astype(F32)).astype(BF16)

            return scatter_ring(
                lambda k, h: summed.at[h * 4 + lax.rem(x + k, 4)],
                lambda h: x_relay.at[h],
                lambda r, h: from_x.at[r, h],
                along_x, x_sent.at[first], x_land.at[first], waits,
            )

        def over_z(x_finish):
            x_finish()
            for a in range(2):
                value = summed[a * 4 + x].astype(F32)
                for i in range(2):
                    value += from_x[i, a].astype(F32)
                total[a] = value
                total_low[a] = value.astype(BF16)
            copies = []
            for d in (1, 2, 3):
                rows_of = 1 - zl if d % 2 else zl
                copy = remote(
                    total_low.at[rows_of, :, pl.ds(n if d >= 2 else 0, n)], from_z.at[d - 1],
                    z_sent.at[first * 3 + d - 1], z_land.at[first * 3 + d - 1], zs[d],
                )
                copy.start()
                copies.append(copy)
            waits.extend(copies)
            return copies

        def finish(z_copies):
            for copy in z_copies:
                copy.wait_recv()
            value = total[zl, :, :n]
            for d in range(3):
                value = value + from_z[d].astype(F32)
            return value

        return over_cores, over_x, over_z, finish

    def tile_of(left, right):
        def tile(t):
            cols = pl.ds(pl.multiple_of(t * ROWS, ROWS), ROWS)
            return dot(left[:, cols], right[...], ((0,), (0,)))

        return tile

    qkv_cores, qkv_x, qkv_z, qkv_finish = grad_stages(
        0, tile_of(normed, low), core_out, core_got, red, x_relay, x_got, z_out, z_low, z_got
    )
    o_cores, o_x, o_z, o_finish = grad_stages(
        1, tile_of(branch_all, att), o_core_out, o_core_got, o_red, o_x_relay, o_x_got, o_z_out, o_z_low, o_z_got
    )
    for load in loads[:5] + loads[6:7]:
        load.wait()

    blocks = q_pos.shape[0] // BLK
    ordered(stored, blocks, ((grad_in, grad_pos),))
    ends = document_ends(doc_lengths, zh * 4 + lax.rem(y + me // 4, 4))
    attend_back(ends, q_pos, k_pos, v_pos, log_total, grad_pos, q_acc, k_acc, v_acc)
    ordered(place, blocks, ((q_acc, q_grad),))

    @pl.loop(0, blocks)
    def _(b):
        dst_rows = pl.ds(pl.multiple_of(b * BLK, BLK), BLK)
        k_rows = k_acc[place[b]] * HD ** (-0.5)
        v_rows = v_acc[place[b]]
        keep[dst_rows, :] = jnp.where(core == 0, k_rows, v_rows)
        send[dst_rows, :] = jnp.where(core == 0, v_rows, k_rows).astype(BF16)

    swap = remote(send, swap_got, swap_sem.at[0], swap_sem.at[1], other_core)
    swap.start()

    waits.append(swap)

    def to_rows(src, dst, sent, landed):
        copies = []
        for k in range(1, 16):
            copy = remote(block(src, lax.rem(me + k, 16)), block(dst, 16 - k), sent.at[k], landed.at[16 - k], along_ctx(k))
            copy.start()
            copies.append(copy)
        waits.extend(copies)
        return copies

    q_copies = to_rows(q_grad, q_got, q_sent, q_land)
    mine = pl.ds(pl.multiple_of(me * ROWS, ROWS), ROWS)
    q_got[:ROWS, :] = q_grad[mine, :]
    branch_pass()
    out_pass, out_finish = scatter_ring(
        row_slots(part),
        lambda h: relay.at[pl.ds(h * (ROWS // 2), ROWS // 2), :],
        lambda r, h: row_slots(out_got)(r, h),
        along_y, out_sent, out_land, waits,
    )
    swap.wait_recv()
    kv_out[...] = (keep[...] + swap_got[...].astype(F32)).astype(BF16)
    kv_copies = to_rows(kv_out, kv_got, kv_sent, kv_land)
    kv_got[:ROWS, :] = kv_out[mine, :]

    branch_finish()
    o_x_pass, o_x_finish = o_x(o_cores())
    for load in loads[7:]:
        load.wait()
    for copy in q_copies:
        copy.wait_recv()
    for copy in kv_copies:
        copy.wait_recv()
    out_pass()

    g_out[0] = jnp.zeros_like(g_out[0])

    def from_unit(ref, unit):
        return ref[pl.ds(pl.multiple_of(lax.rem(unit - me + 16, 16) * ROWS, ROWS), ROWS), :]

    def head_back(grad, value, gain):
        turned = grad * sin[...]
        turned = jnp.concatenate([turned[:, HD // 2 :], -turned[:, : HD // 2]], axis=1)
        back, gain_sum = rms_back(grad * cos[...] + turned, value, gain)
        return back.astype(BF16), gain_sum

    @pl.loop(0, 4)
    def _(s):
        rows = pl.ds(pl.multiple_of(s * ROWS, ROWS), ROWS)
        for h in range(4):
            at = (h // 2) * half + (h % 2) * HD
            cols = slice(at, at + HD)
            grad = from_unit(q_got, s * 4 + h).astype(F32)
            back, gain_sum = head_back(grad, raw[rows, cols], q_gain[...])
            low[rows, cols] = back
            g_out[0, 32:33, :] += gain_sum
        for kv in range(2):
            at = kv * half + 2 * HD
            cols = slice(at, at + HD)
            grad = from_unit(kv_got, s * 4 + kv * 2).astype(F32)
            back, gain_sum = head_back(grad, raw[rows, cols], k_gain[...])
            low[rows, cols] = back
            g_out[0, 33:34, :] += gain_sum
            low[rows, at + HD : at + 2 * HD] = from_unit(kv_got, s * 4 + kv * 2 + 1)

    core_copy = qkv_cores()
    out_finish()
    value = part[:ROWS, :].astype(F32)
    for i in range(2):
        value += out_got[i * ROWS : (i + 1) * ROWS, :].astype(F32)
    part[:ROWS, :] = value.astype(BF16)
    across_copy = remote(part.at[pl.ds(0, ROWS), :], out_across, across_sem.at[0], across_sem.at[1], zs[2])
    across_copy.start()
    waits.append(across_copy)

    @pl.loop(0, parts.shape[1] // WIDE)
    def _(n):
        cols = pl.ds(pl.multiple_of(n * WIDE, WIDE), WIDE)
        total = dot(low[:, :half], w_own[cols, :], ((1,), (1,)))
        total += dot(low[:, half:], w_par[cols, :], ((1,), (1,)))
        parts[:, cols] = total.astype(BF16)
        by_gain[:, cols] = jnp.sum(total * normed[:, cols].astype(F32), axis=0, keepdims=True) / attn_gain[:, cols]

    for i in range(16):
        g_out[0, i : i + 1, :] = by_gain[:, i * HD : (i + 1) * HD]
        g_out[0, 16 + i : 17 + i, :] = mlp_gain_grad[:, i * HD : (i + 1) * HD]
    o_x_pass()
    y_pass, y_finish = scatter_ring(
        row_slots(parts),
        lambda h: relay.at[pl.ds(ROWS + h * (ROWS // 2), ROWS // 2), :],
        lambda r, h: row_slots(y_got)(r, h),
        along_y, y_sent, y_land, waits,
    )

    def gain_stage(stage, places):
        copies = []
        for i, (place, back_slot) in enumerate(places):
            copy = remote(
                g_out.at[stage], g_got.at[stage, back_slot], g_sent.at[stage * 3 + i],
                g_land.at[stage * 3 + back_slot], place,
            )
            copy.start()
            copies.append(copy)
        waits.extend(copies)
        return copies

    def gain_sum_of(stage, copies):
        for copy in copies:
            copy.wait_recv()
        total = g_out[stage]
        for i in range(len(copies)):
            total = total + g_got[stage, i]
        return total

    copies = gain_stage(0, [(along_y(k), 3 - k) for k in (1, 2, 3)])
    x_pass, x_finish = qkv_x(core_copy)
    g_out[1] = gain_sum_of(0, copies)
    copies = gain_stage(1, [(along_x(k), 3 - k) for k in (1, 2, 3)])
    y_pass()
    x_pass()
    g_out[2] = gain_sum_of(1, copies)
    copies = gain_stage(2, [(zs[d], d - 1) for d in (1, 2, 3)])
    o_z_copies = o_z(o_x_finish)
    across_copy.wait_recv()
    out_rows[...] = (middle[...] + out_across[...].astype(F32)).astype(BF16)
    g_out[3] = gain_sum_of(2, copies)
    copies = gain_stage(3, [(other_core, 0)])
    z_copies = qkv_z(x_finish)
    gains = gain_sum_of(3, copies)
    for i in range(16):
        attn_total[:, i * HD : (i + 1) * HD] = gains[i : i + 1, :]
        mlp_total[:, i * HD : (i + 1) * HD] = gains[16 + i : 17 + i, :]
    q_total[...] = gains[32:33, :]
    k_total[...] = gains[33:34, :]

    y_finish()
    grad = parts[:ROWS, :].astype(F32)
    for i in range(2):
        grad += y_got[i * ROWS : (i + 1) * ROWS, :].astype(F32)
    rows_back, _ = rms_back(grad, tokens[...].astype(F32), attn_gain[...])
    tokens_grad[...] = (middle_grad[...] + rows_back).astype(BF16)
    value = qkv_finish(z_copies)
    q_wgrad[...] = value[:, : 2 * HD]
    k_wgrad[...] = value[:, 2 * HD : 3 * HD]
    v_wgrad[...] = value[:, 3 * HD :]
    value = o_finish(o_z_copies)
    for i in range(2):
        o_wgrad[i * HD : (i + 1) * HD, :] = value[:, i * HD : (i + 1) * HD].T
    for copy in waits:
        copy.wait_send()


def back(place, stored, doc_lengths, log_total, cos, sin, q_gain, k_gain, attn_gain, mlp_gain_grad, grad_in, q_pos, k_pos,
         v_pos, part, branch, att, raw, normed, w_own, w_par, middle, tokens, middle_grad):
    rows, model = tokens.shape
    wide = raw.shape[1]
    anywhere = pl.BlockSpec(memory_space=pl.ANY)
    vmem = pl.BlockSpec(memory_space=pltpu.VMEM)
    dma = pltpu.SemaphoreType.DMA
    return pl.pallas_call(
        back_kernel,
        out_shape=(
            jax.ShapeDtypeStruct((rows, model), BF16),
            jax.ShapeDtypeStruct((rows, model), BF16),
            jax.ShapeDtypeStruct((rows, 2 * HD), F32),
            jax.ShapeDtypeStruct((rows, HD), F32),
            jax.ShapeDtypeStruct((rows, HD), F32),
            jax.ShapeDtypeStruct((2 * HD, rows), F32),
            jax.ShapeDtypeStruct((1, model), F32),
            jax.ShapeDtypeStruct((1, model), F32),
            jax.ShapeDtypeStruct((1, HD), F32),
            jax.ShapeDtypeStruct((1, HD), F32),
        ),
        in_specs=[pl.BlockSpec(memory_space=pltpu.SMEM)] * 3 + [vmem] * 7 + [anywhere] * 14,
        out_specs=(vmem,) * 10,
        scratch_shapes=[pltpu.VMEM((16 * rows // BLK, BLK, HD), BF16)]
        + [pltpu.VMEM((16 * rows, HD), BF16)] * 4
        + [pltpu.VMEM((16 * rows // BLK, BLK, HD), BF16)]
        + [pltpu.VMEM((16 * rows, HD), BF16)] * 2
        + [pltpu.VMEM((16 * rows // BLK, BLK, HD), F32)] * 2
        + [pltpu.VMEM((16 * rows, HD), F32)]
        + [
            pltpu.VMEM((4 * rows, wide), F32),
            pltpu.VMEM((rows, model), F32),
            pltpu.VMEM((rows, model), BF16),
            pltpu.VMEM((rows, model), F32),
            pltpu.VMEM((4 * rows, model), BF16),
            pltpu.VMEM((model, wide // 2), BF16),
            pltpu.VMEM((model, wide // 2), BF16),
            pltpu.VMEM((4 * rows, model), BF16),
            pltpu.VMEM((4 * rows, 4 * HD), BF16),
            pltpu.VMEM((4 * rows, model), BF16),
            pltpu.VMEM((2 * rows, model), BF16),
            pltpu.VMEM((2 * rows, model), BF16),
            pltpu.VMEM((rows, model), BF16),
            pltpu.VMEM((16 * rows, HD), BF16),
            pltpu.VMEM((16 * rows, HD), BF16),
            pltpu.VMEM((16 * rows, HD), BF16),
            pltpu.VMEM((16 * rows, HD), BF16),
            pltpu.VMEM((4 * rows, wide), BF16),
            pltpu.VMEM((4 * rows, model), BF16),
            pltpu.VMEM((2 * rows, model), BF16),
            pltpu.VMEM((8, rows, wide), BF16),
            pltpu.VMEM((8, rows, wide), BF16),
            pltpu.VMEM((8, rows, wide), BF16),
            pltpu.VMEM((2, rows, wide), BF16),
            pltpu.VMEM((2, 2, rows, wide), BF16),
            pltpu.VMEM((2, rows, wide), F32),
            pltpu.VMEM((2, rows, wide), BF16),
            pltpu.VMEM((3, rows, wide // 2), BF16),
            pltpu.VMEM((8, rows, 4 * HD), BF16),
            pltpu.VMEM((8, rows, 4 * HD), BF16),
            pltpu.VMEM((8, rows, 4 * HD), BF16),
            pltpu.VMEM((2, rows, 4 * HD), BF16),
            pltpu.VMEM((2, 2, rows, 4 * HD), BF16),
            pltpu.VMEM((2, rows, 4 * HD), F32),
            pltpu.VMEM((2, rows, 4 * HD), BF16),
            pltpu.VMEM((3, rows, 2 * HD), BF16),
            pltpu.VMEM((4, 40, HD), F32),
            pltpu.VMEM((4, 3, 40, HD), F32),
            pltpu.VMEM((1, model), F32),
            dma((14,)),
            dma((2,)),
            dma((2,)),
            dma((16,)),
            dma((16,)),
            dma((16,)),
            dma((16,)),
            dma((6,)),
            dma((6,)),
            dma((6,)),
            dma((6,)),
            dma((4,)),
            dma((4,)),
            dma((2,)),
            dma((2,)),
            dma((2, 6)),
            dma((2, 6)),
            dma((6,)),
            dma((6,)),
            dma((12,)),
            dma((12,)),
        ],
        compiler_params=pltpu.CompilerParams(
            collective_id=2, has_side_effects=True, vmem_limit_bytes=62 * 2**20
        ),
        cost_estimate=pl.CostEstimate(
            flops=4 * 4 * rows * model * wide, bytes_accessed=24 * 2**20, transcendentals=0
        ),
        name="back",
    )(
        place, stored, doc_lengths, log_total, cos, sin, q_gain, k_gain, attn_gain, mlp_gain_grad,
        grad_in.reshape(-1, BLK, HD), q_pos, k_pos, v_pos, part, branch, att, raw, normed, w_own, w_par, middle, tokens, middle_grad,
    )


def per_device(
    tokens,
    cotangent,
    attn_gain,
    q_weight,
    k_weight,
    v_weight,
    q_gain,
    k_gain,
    o_weight,
    mlp_gain,
    gate_weight,
    up_weight,
    down_weight,
    doc_lengths,
    block_place,
):
    rows = tokens.shape[1]
    zl, x, core = (lax.axis_index(a) for a in CTX)
    ctx_place = zl * 8 + x * 2 + core
    numbers = jnp.arange(block_place.shape[0], dtype=jnp.int32)
    stored = jnp.sum(jnp.where(block_place[None, :] == numbers[:, None], numbers[None, :], 0), axis=1, dtype=jnp.int32)
    own_blocks = lax.dynamic_slice_in_dim(block_place, ctx_place * (rows // BLK), rows // BLK)
    own_positions = (own_blocks[:, None] * BLK + jnp.arange(BLK, dtype=jnp.int32)[None, :]).reshape(-1)
    cos_rows, sin_rows = tables(own_positions, HD)
    q_gain, k_gain = q_gain.reshape(1, HD), k_gain.reshape(1, HD)
    attn_gain, mlp_gain = attn_gain.reshape(1, -1), mlp_gain.reshape(1, -1)
    cot = cotangent[0]

    log_total, out, q_pos, k_pos, v_pos, raw, normed, w_own, w_par, o_par, cot_half = pre(
        block_place, stored, doc_lengths, tokens[0], cos_rows, sin_rows, attn_gain, q_gain, k_gain, cot, q_weight, k_weight,
        v_weight, o_weight,
    )
    (
        middle, middle_grad, mlp_gain_grad, gate_wgrad, up_wgrad, down_wgrad, grad_in, att, branch, part, _,
    ) = middle_part(tokens[0], cot, mlp_gain, out, o_weight, o_par, cot_half, gate_weight, up_weight, down_weight)
    (
        tokens_grad, out_rows, q_wgrad, k_wgrad, v_wgrad, o_wgrad, attn_gain_grad, mlp_gain_grad, q_gain_grad, k_gain_grad,
    ) = back(
        block_place, stored, doc_lengths, log_total, cos_rows, sin_rows, q_gain, k_gain, attn_gain, mlp_gain_grad, grad_in,
        q_pos, k_pos, v_pos, part, branch, att, raw, normed, w_own, w_par, middle, tokens[0], middle_grad,
    )
    return (
        out_rows[None],
        tokens_grad[None],
        attn_gain_grad[0],
        q_wgrad,
        k_wgrad,
        v_wgrad,
        q_gain_grad[0],
        k_gain_grad[0],
        o_wgrad,
        mlp_gain_grad[0],
        gate_wgrad,
        up_wgrad,
        down_wgrad,
    )


def solution(mesh):
    fine = Mesh(mesh.devices.reshape(SIZES), AXES)
    rows = P(FSDP, CTX, None)
    in_specs = (
        rows,
        rows,
        P(),
        P(None, FSDP),
        P(None, FSDP),
        P(None, FSDP),
        P(),
        P(),
        P(FSDP, None),
        P(),
        P(None, FSDP),
        P(None, FSDP),
        P(FSDP, None),
        P(),
        P(),
    )
    out_specs = (
        rows,
        rows,
        P(),
        P(CTX, FSDP),
        P(CTX, FSDP),
        P(CTX, FSDP),
        P(),
        P(),
        P(FSDP, CTX),
        P(),
        P(CTX, FSDP),
        P(CTX, FSDP),
        P(FSDP, CTX),
    )
    return jax.shard_map(
        per_device, mesh=fine, in_specs=in_specs, out_specs=out_specs, check_vma=False
    )
```

```python
import functools

import jax
import jax.numpy as jnp
from jax import lax
from jax.experimental import pallas as pl
from jax.experimental.pallas import tpu as pltpu
from jax.sharding import Mesh, PartitionSpec as P

EPSILON = 1e-06
ROPE_BASE = 1000000.0
MASKED_SCORE = -1e30
HD = 128
BLK = 64
AXES = ("zl", "x", "core", "zh", "y")
SIZES = (2, 4, 2, 2, 4)
CTX = ("zl", "x", "core")
FSDP = ("zh", "y")
F32 = jnp.float32
BF16 = jnp.bfloat16


def tables(positions, head_dim):
    exponent_steps = jnp.arange(head_dim // 2, dtype=jnp.int32).astype(F32) * (2.0 / head_dim)
    frequency = ROPE_BASE ** (-exponent_steps)
    phases = positions.astype(F32)[:, None] * frequency[None, :]
    phases = jnp.concatenate([phases, phases], axis=-1)
    return (jnp.cos(phases), jnp.sin(phases))


def dot(left, right, contract=((1,), (0,))):
    return lax.dot_general(left, right, (contract, ((), ())), preferred_element_type=F32)


TILE = 256


def keep_mask(ends, first_row, rows, cols):
    place = first_row + lax.broadcasted_iota(jnp.int32, (rows, 1), 0)
    start = jnp.zeros((rows, 1), jnp.int32)
    for end in ends:
        start = jnp.where(place >= end, end, start)
    key = lax.broadcasted_iota(jnp.int32, (rows, cols), 1)
    return (key >= start) & (key <= place)


def ordered(order, blocks, pairs):
    @pl.loop(0, blocks)
    def _(b):
        rows = pl.ds(pl.multiple_of(b * BLK, BLK), BLK)
        for src, dst in pairs:
            dst[rows, :] = src[order[b]]


def attend(ends, q_pos, k_pos, v_pos, out_pos, log_total):
    for i in range(q_pos.shape[0] // TILE):
        span = pl.ds(i * TILE, TILE)
        n = (i + 1) * TILE
        scores = dot(q_pos[span, :], k_pos[:n, :], ((1,), (1,))) * HD ** (-0.5)
        scores = jnp.where(keep_mask(ends, i * TILE, TILE, n), scores, MASKED_SCORE)
        top = jnp.max(scores, axis=-1, keepdims=True)
        weights = jnp.exp(scores - top)
        total = jnp.sum(weights, axis=-1, keepdims=True)
        log_total[span, :] = top + jnp.log(total)
        probs = (weights * (1.0 / total)).astype(BF16)
        out_pos[i * TILE // BLK : n // BLK] = dot(probs, v_pos[:n, :]).astype(BF16).reshape(TILE // BLK, BLK, HD)


def attend_back(ends, q_pos, k_pos, v_pos, log_total, grad_pos, q_acc, k_acc, v_acc):
    scale = HD ** (-0.5)
    k_acc[...] = jnp.zeros_like(k_acc)
    v_acc[...] = jnp.zeros_like(v_acc)
    for i in range(q_pos.shape[0] // TILE):
        span = pl.ds(i * TILE, TILE)
        n = (i + 1) * TILE
        queries = q_pos[span, :]
        grads = grad_pos[span, :]
        scores = dot(queries, k_pos[:n, :], ((1,), (1,))) * scale
        kept = keep_mask(ends, i * TILE, TILE, n)
        probs = jnp.where(kept, jnp.exp(scores - log_total[span, :]), 0.0)
        prob_grad = dot(grads, v_pos[:n, :], ((1,), (1,)))
        row_dot = jnp.sum(prob_grad * probs, axis=-1, keepdims=True)
        score_grad = (probs * (prob_grad - row_dot)).astype(BF16)
        q_rows = (dot(score_grad, k_pos[:n, :]) * scale).astype(BF16)
        q_acc[i * TILE // BLK : n // BLK] = q_rows.reshape(TILE // BLK, BLK, HD)
        k_acc[: n // BLK] += dot(score_grad, queries, ((0,), (0,))).reshape(n // BLK, BLK, HD)
        v_acc[: n // BLK] += dot(probs.astype(BF16), grads, ((0,), (0,))).reshape(n // BLK, BLK, HD)


def document_ends(doc_lengths, sequence):
    ends = [doc_lengths[sequence, 0]]
    for j in range(1, doc_lengths.shape[1]):
        ends.append(ends[-1] + doc_lengths[sequence, j])
    return ends


def peers(pairs):
    barrier = pltpu.get_barrier_semaphore()
    for place in pairs:
        pl.semaphore_signal(barrier, inc=1, device_id=place, device_id_type=pl.DeviceIdType.MESH)
    pl.semaphore_wait(barrier, len(pairs))


def remote(src, dst, sent, landed, place):
    return pltpu.make_async_remote_copy(
        src_ref=src, dst_ref=dst, send_sem=sent, recv_sem=landed, device_id=place,
        device_id_type=pl.DeviceIdType.MESH,
    )


ROWS = 128
WIDE = 256


def ctx_at(index):
    return {"zl": index // 8, "x": lax.rem(index // 2, 4), "core": lax.rem(index, 2)}


def block(ref, index):
    return ref.at[pl.ds(pl.multiple_of(index * ROWS, ROWS), ROWS), :]


def pair(ref, index):
    return ref.at[pl.ds(index * 2, 2)]


def inverse_rms(values):
    return lax.rsqrt(jnp.mean(values * values, axis=-1, keepdims=True) + EPSILON)


def rms_back(grad, values, gain):
    inverse = inverse_rms(values)
    scaled = grad * gain
    inner = jnp.mean(values * scaled, axis=-1, keepdims=True)
    back = inverse * scaled - values * (inverse * inverse * inverse * inner)
    return back, jnp.sum(grad * values * inverse, axis=0, keepdims=True)


def gather_ring(slot, along, sent, landed, waits, own=None):
    def move(src, dst, i, k):
        copy = remote(src, dst, sent.at[i], landed.at[i], along(k))
        copy.start()
        waits.append(copy)
        return copy

    own = slot(0) if own is None else own
    near = [move(own, slot(1), 0, 3), move(own, slot(3), 1, 1)]
    far = []

    def pass_on():
        for h, k in ((0, 3), (1, 1)):
            near[h].wait_recv()
            far.append(move(slot(1 + 2 * h, h), slot(2, h), 2 + h, k))

    def finish():
        for copy in far:
            copy.wait_recv()

    return pass_on, finish


def scatter_ring(part, relay, got, along, sent, landed, waits):
    def move(src, dst, i, k):
        copy = remote(src, dst, sent.at[i], landed.at[i], along(k))
        copy.start()
        waits.append(copy)
        return copy

    first = [move(part(2, 0), relay(0), 0, 1), move(part(2, 1), relay(1), 1, 3)]
    last = [move(part(1, 1), got(0, 1), 2, 1), move(part(3, 0), got(1, 0), 3, 3)]

    def pass_on():
        for h, k in ((0, 1), (1, 3)):
            first[h].wait_recv()
            ref = part(k, h)
            ref[...] = (ref[...].astype(F32) + relay(h)[...].astype(F32)).astype(BF16)
            last.append(move(ref, got(h, h), 4 + h, k))

    def finish():
        for copy in last:
            copy.wait_recv()

    return pass_on, finish


def row_slots(ref, base=0):
    def slot(r, h=None):
        if h is None:
            return ref.at[pl.ds((base + r) * ROWS, ROWS), :]
        return ref.at[pl.ds((base + r) * ROWS + h * (ROWS // 2), ROWS // 2), :]

    return slot


def pre_kernel(
    place, stored, doc_lengths, tokens, cos, sin, attn_gain, q_gain, k_gain, cot_hbm, q_hbm, k_hbm, v_hbm, o_hbm,
    log_total, out_hbm, q_hbm_out, k_hbm_out, v_hbm_out, raw_hbm, normed_hbm, own_hbm, par_hbm, o_par_hbm, cot_got,
    q_got, mine, other, q_pos, k_pos, v_pos, out_pos, out, normed, w_own, w_par, o_own, o_par, raw, q_out, kv_out,
    load_sem, y_sent, y_land, cot_sent, cot_land, z_sent, z_land, x_sent, x_land, core_sent, core_land,
    q_sent, q_land, kv_sent, kv_land, swap_sem, local_sem, out_sem,
):
    zl, x, core = (lax.axis_index(a) for a in CTX)
    zh, y = (lax.axis_index(a) for a in FSDP)
    me = zl * 8 + x * 2 + core
    half = 4 * HD
    waits = []

    def along_y(k):
        return {"y": lax.rem(y + k, 4)}

    def along_x(k):
        return {"x": lax.rem(x + k, 4)}

    other_core = {"core": 1 - core}
    cross = {"zl": 1 - zl, "zh": 1 - zh}
    q_width, k_width = q_hbm.shape[1], k_hbm.shape[1]
    pieces = (
        (q_hbm, w_own.at[:, pl.ds(0, q_width)]),
        (k_hbm, w_own.at[:, pl.ds(q_width, k_width)]),
        (v_hbm, w_own.at[:, pl.ds(q_width + k_width, k_width)]),
        (o_hbm, o_own),
    )
    loads = [pltpu.make_async_copy(src, dst, load_sem.at[i]) for i, (src, dst) in enumerate(pieces)]
    for load in loads:
        load.start()
    own_cot = pltpu.make_async_copy(cot_hbm, cot_got.at[pl.ds(0, ROWS), :], local_sem.at[0])
    own_cot.start()
    rows_in = tokens[...].astype(F32)
    normed[:ROWS, :] = (rows_in * inverse_rms(rows_in) * attn_gain[...]).astype(BF16)
    peers([ctx_at(lax.rem(me + k, 16)) for k in range(1, 16)] + [along_y(k) for k in (1, 2, 3)] + [cross])

    normed_pass, normed_finish = gather_ring(row_slots(normed), along_y, y_sent, y_land, waits)
    for load in loads:
        load.wait()

    def shard_stage(src, dst, first):
        eighth = src.shape[0] // 8

        def piece(ref, at_x, at_core):
            return ref.at[pl.ds(pl.multiple_of((at_x * 2 + at_core) * eighth, eighth), eighth), :]

        over_z = remote(piece(src, x, core), piece(dst, x, core), z_sent.at[first], z_land.at[first], cross)
        over_z.start()
        waits.append(over_z)

        def to_core(k):
            at_x = lax.rem(x + k, 4)
            copy = remote(
                piece(dst, at_x, core), piece(dst, at_x, core), core_sent.at[first * 4 + k],
                core_land.at[first * 4 + k], other_core,
            )
            copy.start()
            waits.append(copy)
            return copy

        def next_stage():
            over_z.wait_recv()
            copies = []
            for k in (1, 3, 2):
                copy = remote(
                    piece(dst, x, core), piece(dst, x, core), x_sent.at[first * 4 + k],
                    x_land.at[first * 4 + 4 - k], along_x(k),
                )
                copy.start()
                copies.append((4 - k, copy))
            waits.extend(copy for _, copy in copies)
            cores = [to_core(0)]

            def last_stage():
                for k, copy in copies:
                    copy.wait_recv()
                    cores.append(to_core(k))

                def finish():
                    for copy in cores:
                        copy.wait_recv()

                return finish

            return last_stage

        return next_stage

    def prepared(value, gain):
        scaled = value * inverse_rms(value) * gain
        turned = jnp.concatenate([-scaled[:, HD // 2 :], scaled[:, : HD // 2]], axis=1)
        return (scaled * cos[...] + turned * sin[...]).astype(BF16)

    def unit_copy(src, dst, sent, landed, dest):
        return remote(pair(src, dest), pair(dst, me), sent.at[dest], landed.at[me], ctx_at(dest))

    def put(ref, unit, value):
        ref[unit * 2 : unit * 2 + 2] = value.reshape(2, BLK, HD)

    def units(s, side):
        rows = slice(s * ROWS, (s + 1) * ROWS)
        unit = s * 4 + side * 2
        for g in range(2):
            at = side * half + g * HD
            put(q_out, unit + g, prepared(raw[rows, at : at + HD], q_gain[...]))
        at = side * half + 2 * HD
        put(kv_out, unit, prepared(raw[rows, at : at + HD], k_gain[...]))
        put(kv_out, unit + 1, raw[rows, at + HD : at + 2 * HD].astype(BF16))
        for g in range(2):
            dest = unit + lax.rem(me + g, 2)

            @pl.when(dest != me)
            def _():
                unit_copy(kv_out, mine, kv_sent, kv_land, dest).start()
                unit_copy(q_out, q_got, q_sent, q_land, dest).start()

    def own_side(s):
        rows = slice(s * ROWS, (s + 1) * ROWS)
        raw[rows, :half] = dot(normed[rows, :], w_own[...])
        units(s, 0)

    qkv_stage = shard_stage(w_own, w_par, 0)
    o_stage = shard_stage(o_own, o_par, 1)
    own_side(0)
    qkv_stage = qkv_stage()
    o_stage = o_stage()
    normed_pass()
    cot_pass, cot_finish = gather_ring(row_slots(cot_got), along_y, cot_sent, cot_land, waits, cot_hbm)
    own_side(1)
    own_side(3)
    qkv_finish = qkv_stage()
    normed_finish()
    own_side(2)
    qkv_finish()
    raw[:, half:] = dot(normed[...], w_par[...])
    for s in (2, 3, 1, 0):
        units(s, 1)
    o_finish = o_stage()
    local = [
        pltpu.make_async_copy(pair(q_out, me), pair(q_got, me), local_sem.at[1]),
        pltpu.make_async_copy(pair(kv_out, me), pair(mine, me), local_sem.at[2]),
    ]
    for copy in local:
        copy.start()
    o_finish()
    outs = [
        pltpu.make_async_copy(src, dst, out_sem.at[i])
        for i, (src, dst) in enumerate(
            ((raw, raw_hbm), (normed, normed_hbm), (w_own, own_hbm), (w_par, par_hbm), (o_par, o_par_hbm))
        )
    ]
    for copy in outs:
        copy.start()

    def from_unit(src, dst, sent, landed, source):
        return remote(pair(src, source), pair(dst, source), sent.at[source], landed.at[source], ctx_at(source))

    local[1].wait()

    @pl.loop(0, 16)
    def _(source):
        @pl.when(source != me)
        def _():
            from_unit(kv_out, mine, kv_sent, kv_land, source).wait_recv()

    swap = remote(mine, other, swap_sem.at[0], swap_sem.at[1], other_core)
    swap.start()

    @pl.loop(0, 16)
    def _(source):
        @pl.when(source != me)
        def _():
            from_unit(q_out, q_got, q_sent, q_land, source).wait_recv()
            from_unit(q_out, q_got, q_sent, q_land, source).wait_send()
            from_unit(kv_out, mine, kv_sent, kv_land, source).wait_send()

    swap.wait()
    local[0].wait()
    cot_pass()

    blocks = q_pos.shape[0] // BLK

    @pl.when(core == 0)
    def _():
        ordered(stored, blocks, ((q_got, q_pos), (mine, k_pos), (other, v_pos)))

    @pl.when(core == 1)
    def _():
        ordered(stored, blocks, ((q_got, q_pos), (other, k_pos), (mine, v_pos)))

    more = [
        pltpu.make_async_copy(src, dst, out_sem.at[5 + i])
        for i, (src, dst) in enumerate(((q_pos, q_hbm_out), (k_pos, k_hbm_out), (v_pos, v_hbm_out)))
    ]
    for copy in more:
        copy.start()
    outs.extend(more)
    ends = document_ends(doc_lengths, zh * 4 + lax.rem(y + me // 4, 4))
    attend(ends, q_pos, k_pos, v_pos, out_pos, log_total)
    ordered(place, blocks, ((out_pos, out),))
    out_copy = pltpu.make_async_copy(out, out_hbm, out_sem.at[8])
    out_copy.start()
    outs.append(out_copy)
    cot_finish()
    own_cot.wait()
    for copy in outs:
        copy.wait()
    for copy in waits:
        copy.wait_send()


def pre(place, stored, doc_lengths, tokens, cos, sin, attn_gain, q_gain, k_gain, cot, q_w, k_w, v_w, o_w):
    rows, model = tokens.shape
    wide = q_w.shape[1] + k_w.shape[1] + v_w.shape[1]
    anywhere = pl.BlockSpec(memory_space=pl.ANY)
    vmem = pl.BlockSpec(memory_space=pltpu.VMEM)
    dma = pltpu.SemaphoreType.DMA
    unit = jax.ShapeDtypeStruct((16 * rows, HD), BF16)
    return pl.pallas_call(
        pre_kernel,
        out_shape=(
            jax.ShapeDtypeStruct((16 * rows, 1), F32),
            unit,
            unit,
            unit,
            unit,
            jax.ShapeDtypeStruct((4 * rows, 2 * wide), F32),
            jax.ShapeDtypeStruct((4 * rows, model), BF16),
            jax.ShapeDtypeStruct((model, wide), BF16),
            jax.ShapeDtypeStruct((model, wide), BF16),
            jax.ShapeDtypeStruct(o_w.shape, BF16),
            jax.ShapeDtypeStruct((4 * rows, model), BF16),
        ),
        in_specs=[pl.BlockSpec(memory_space=pltpu.SMEM)] * 3 + [vmem] * 6 + [anywhere] * 5,
        out_specs=(vmem,) + (anywhere,) * 10,
        scratch_shapes=[pltpu.VMEM((16 * rows // BLK, BLK, HD), BF16)] * 3
        + [pltpu.VMEM((16 * rows, HD), BF16)] * 3
        + [pltpu.VMEM((16 * rows // BLK, BLK, HD), BF16), pltpu.VMEM((16 * rows, HD), BF16)]
        + [
            pltpu.VMEM((4 * rows, model), BF16),
            pltpu.VMEM((model, wide), BF16),
            pltpu.VMEM((model, wide), BF16),
            pltpu.VMEM(o_w.shape, BF16),
            pltpu.VMEM(o_w.shape, BF16),
            pltpu.VMEM((4 * rows, 2 * wide), F32),
            pltpu.VMEM((16 * rows // BLK, BLK, HD), BF16),
            pltpu.VMEM((16 * rows // BLK, BLK, HD), BF16),
            dma((4,)),
            dma((4,)),
            dma((4,)),
            dma((4,)),
            dma((4,)),
            dma((2,)),
            dma((2,)),
            dma((8,)),
            dma((8,)),
            dma((8,)),
            dma((8,)),
            dma((16,)),
            dma((16,)),
            dma((16,)),
            dma((16,)),
            dma((2,)),
            dma((3,)),
            dma((9,)),
        ],
        compiler_params=pltpu.CompilerParams(
            collective_id=3, has_side_effects=True, vmem_limit_bytes=58 * 2**20
        ),
        cost_estimate=pl.CostEstimate(
            flops=2 * 4 * rows * model * 2 * wide, bytes_accessed=24 * 2**20, transcendentals=0
        ),
        name="pre",
    )(place, stored, doc_lengths, tokens, cos, sin, attn_gain, q_gain, k_gain, cot, q_w, k_w, v_w, o_w)


def middle_kernel(
    tokens, cot, gain, att_hbm, o_own_hbm, o_par_hbm, cot_hbm, gate_hbm, up_hbm, down_hbm,
    middle, middle_grad, gain_grad, gate_wgrad, up_wgrad, down_wgrad, grad_got, att_out, branch, part_hbm, o_full,
    att, o_own, o_par, relay, o_got, hid, cots, gate_w, up_w, down_w, act_grad, gu_grad, act, parts, got, z_out, z_got,
    part, stage, tiles, tile_relay, tile_got, tile_z, down_sum, att_grad,
    load_sem, att_sent, att_land, o_sent, o_land, hid_sent, hid_land, far_sent, far_land, across_sent, across_land,
    near_back_sent, near_back_land, far_back_sent, far_back_land, cot_sent, cot_land, part_sent, part_land,
    oy_sent, oy_land, ox_sent, ox_land, oc_sent, oc_land, grad_sent, grad_land, core_sent, core_land, x_sent, x_land, zl_sent, zl_land,
    out_sem, local_sem, oload_sem,
):
    zl, x, core = (lax.axis_index(a) for a in CTX)
    zh, y = (lax.axis_index(a) for a in FSDP)
    me = zl * 8 + x * 2 + core
    half = 4 * ROWS
    width = gate_w.shape[1]
    model = hid.shape[1]
    side = 2 * HD
    waits = []

    def along(k):
        return {"y": lax.rem(y + k, 4)}

    def along_x(k):
        return {"x": lax.rem(x + k, 4)}

    across = {"zh": 1 - zh}
    other_core = {"core": 1 - core}
    loads = [
        pltpu.make_async_copy(src, dst, load_sem.at[i])
        for i, (src, dst) in enumerate(
            (
                (o_own_hbm, o_own),
                (o_par_hbm, o_par),
                (cot_hbm, cots.at[pl.ds(0, half), :]),
                (down_hbm, down_w),
                (gate_hbm, gate_w),
                (up_hbm, up_w),
            )
        )
    ]
    for load in loads:
        load.start()
    barrier = pltpu.get_barrier_semaphore()
    places = [ctx_at(lax.rem(me + k, 16)) for k in range(1, 16)] + [along(1), along(2), along(3), across]
    for place in places:
        pl.semaphore_signal(barrier, inc=1, device_id=place, device_id_type=pl.DeviceIdType.MESH)

    @pl.when(me >= 4)
    def _():
        @pl.loop(0, 16)
        def _(k):
            place = dict(ctx_at(lax.rem(me + k, 16)), **along(me // 4))
            pl.semaphore_signal(barrier, inc=1, device_id=place, device_id_type=pl.DeviceIdType.MESH)

    pl.semaphore_wait(barrier, len(places) + 12)

    def att_at(unit):
        return att.at[
            pl.ds(pl.multiple_of(unit // 4 * ROWS, ROWS), ROWS), pl.ds(pl.multiple_of(lax.rem(unit, 4) * HD, HD), HD)
        ]

    def att_copy(dest, source):
        return remote(block(att_hbm, dest), att_at(source), att_sent.at[dest], att_land.at[source], ctx_at(dest))

    @pl.loop(1, 16)
    def _(k):
        att_copy(lax.rem(me + k, 16), me).start()

    own_att = pltpu.make_async_copy(block(att_hbm, me), att_at(me), local_sem.at[0])
    own_att.start()
    cot_copies = [
        remote(row_slots(cot_hbm)(r), row_slots(cots)(4 + r), cot_sent.at[r], cot_land.at[r], across) for r in range(4)
    ]
    cot_copies[0].start()
    cot_copies[1].start()
    waits.extend(cot_copies)

    def o_rows(k, h, at, count):
        return o_full.at[pl.ds(pl.multiple_of(k * half + h * side + at, 16), count), :]

    piece = core * HD + x * (ROWS // 4)
    oy_rings = []
    for h, src in ((0, o_own_hbm), (1, o_par_hbm)):

        def slot(k, part_of=None, h=h):
            if part_of is None:
                return o_rows(k, h, piece, ROWS // 4)
            return o_rows(k, h, piece + part_of * (ROWS // 8), ROWS // 8)

        own_piece = src.at[pl.ds(pl.multiple_of(piece, ROWS // 4), ROWS // 4), :]
        oy_rings.append(gather_ring(slot, along, oy_sent.at[h], oy_land.at[h], waits, own_piece))

    def ox_move(k, h, at_x, i, to):
        ref = o_rows(k, h, core * HD + at_x * (ROWS // 4), ROWS // 4)
        copy = remote(ref, ref, ox_sent.at[i, k - 1, h], ox_land.at[i, k - 1, h], along_x(to))
        copy.start()
        waits.append(copy)
        return copy

    def ox_start():
        return [ox_move(k, h, x, i, to) for k in (1, 2, 3) for h in (0, 1) for i, to in ((0, 3), (1, 1))]

    def ox_pass(near):
        for copy in near:
            copy.wait_recv()
        far = [ox_move(k, 0, lax.rem(x + 1, 4), 2, 3) for k in (1, 2, 3)]
        return far + [ox_move(k, 1, lax.rem(x + 3, 4), 2, 1) for k in (1, 2, 3)]

    def o_cores(far):
        for copy in far:
            copy.wait_recv()
        copies = []
        for k in (1, 2, 3):
            for h in (0, 1):
                ref = o_rows(k, h, core * HD, HD)
                copy = remote(ref, ref, oc_sent.at[k - 1, h], oc_land.at[k - 1, h], other_core)
                copy.start()
                copies.append(copy)
        waits.extend(copies)
        return copies

    loads[0].wait()
    loads[1].wait()
    own_att.wait()

    @pl.loop(1, 16)
    def _(k):
        att_copy(lax.rem(me + k, 16), lax.rem(me + k, 16)).wait_recv()

    for ring_pass, _ in oy_rings:
        ring_pass()

    def scattered(base, got_base, relay_at, sent, landed):
        slots = row_slots(parts, base)

        def halves(ref, first):
            return lambda r, h: row_slots(ref, first)(r, h)

        def relay_half(h):
            return relay.at[pl.ds(relay_at * ROWS + h * (ROWS // 2), ROWS // 2), :]

        return scatter_ring(slots, relay_half, halves(got, got_base), along, sent, landed, waits)

    def summed(base, got_base):
        value = parts[base * ROWS : (base + 1) * ROWS, :].astype(F32)
        for i in range(2):
            value += got[(got_base + i) * ROWS : (got_base + i + 1) * ROWS, :].astype(F32)
        return value

    @pl.loop(0, model // WIDE)
    def _(n):
        cols = pl.ds(pl.multiple_of(n * WIDE, WIDE), WIDE)
        value = dot(att[:, :side], o_own[:, cols]) + dot(att[:, side:], o_par[:, cols])
        parts[pl.ds(0, half), cols] = value.astype(BF16)

    o_waits = []
    o_pass, o_finish = scatter_ring(
        row_slots(parts),
        lambda h: relay.at[pl.ds(h * (ROWS // 2), ROWS // 2), :],
        lambda r, h: row_slots(o_got)(r, h),
        along, o_sent, o_land, o_waits,
    )

    def grads_of_cot(first, count):
        rows = pl.ds(first, count)

        @pl.loop(0, width // WIDE)
        def _(n):
            cols = pl.ds(pl.multiple_of(n * WIDE, WIDE), WIDE)
            act_grad[rows, cols] = dot(cots[rows, :], down_w[cols, :], ((1,), (1,))).astype(BF16)

    for _, ring_finish in oy_rings:
        ring_finish()
    o_near = ox_start()
    loads[2].wait()
    loads[3].wait()
    grads_of_cot(0, half)
    o_pass()
    o_finish()
    value = tokens[...].astype(F32) + parts[:ROWS, :].astype(F32)
    for i in range(2):
        value += o_got[i * ROWS : (i + 1) * ROWS, :].astype(F32)
    middle[...] = value
    hid[:ROWS, :] = (value * inverse_rms(value) * gain[...]).astype(BF16)

    hid_waits = []
    hid_pass, hid_finish = gather_ring(row_slots(hid), along, hid_sent, hid_land, hid_waits)
    hid_across = remote(row_slots(hid)(0), row_slots(hid)(4), across_sent.at[0], across_land.at[0], across)
    hid_across.start()
    hid_waits.append(hid_across)
    loads[4].wait()
    loads[5].wait()
    for copy in o_waits:
        copy.wait_send()
    hid_pass()
    hid_across.wait_recv()
    far_pass, far_finish = gather_ring(row_slots(hid, 4), along, far_sent, far_land, hid_waits)
    cot_copies[3].start()
    cot_copies[2].start()

    def forward(first, count):
        rows = pl.ds(first, count)

        @pl.loop(0, width // WIDE)
        def _(n):
            cols = pl.ds(pl.multiple_of(n * WIDE, WIDE), WIDE)
            gate = dot(hid[rows, :], gate_w[:, cols])
            up = dot(hid[rows, :], up_w[:, cols])
            sig = jax.nn.sigmoid(gate)
            silu = gate * sig
            grad = act_grad[rows, cols].astype(F32)
            act[rows, cols] = (silu * up).astype(BF16)
            gu_grad[rows, cols] = (grad * up * sig * (1.0 + gate * (1.0 - sig))).astype(BF16)
            gu_grad[rows, pl.ds(pl.multiple_of(width + n * WIDE, WIDE), WIDE)] = (grad * silu).astype(BF16)

    def backward(first, count):
        rows = pl.ds(first, count)

        @pl.loop(0, model // WIDE)
        def _(n):
            cols = pl.ds(pl.multiple_of(n * WIDE, WIDE), WIDE)
            value = dot(gu_grad[rows, :width], gate_w[cols, :], ((1,), (1,)))
            value += dot(gu_grad[rows, width:], up_w[cols, :], ((1,), (1,)))
            parts[rows, cols] = value.astype(BF16)

    forward(0, 2 * ROWS)
    forward(3 * ROWS, ROWS)
    hid_finish()
    forward(2 * ROWS, ROWS)
    o_far = ox_pass(o_near)
    cot_copies[0].wait_recv()
    cot_copies[1].wait_recv()
    grads_of_cot(half, 2 * ROWS)
    far_pass()
    backward(0, half)
    forward(half, 2 * ROWS)
    cot_copies[3].wait_recv()
    grads_of_cot(7 * ROWS, ROWS)
    forward(7 * ROWS, ROWS)
    backward(half, 2 * ROWS)
    backward(7 * ROWS, ROWS)
    o_core_copies = o_cores(o_far)
    cot_copies[2].wait_recv()
    grads_of_cot(6 * ROWS, ROWS)
    far_finish()
    forward(6 * ROWS, ROWS)
    backward(6 * ROWS, ROWS)
    far_back_pass, far_back_finish = scattered(4, 2, 0, far_back_sent, far_back_land)
    near_back_pass, near_back_finish = scattered(0, 0, 1, near_back_sent, near_back_land)

    def tile_pair(p, which):
        def columns(ref):
            return jnp.concatenate(
                [ref[:, pl.ds(pl.multiple_of(((2 * p + i) * 2 + which) * ROWS, ROWS), ROWS)] for i in range(2)], axis=1
            )

        return dot(columns(hid), gu_grad[...], ((0,), (0,))), dot(columns(cots), act[...], ((0,), (0,)))

    def pair_copy(b, p):
        return remote(stage.at[b], tiles.at[pl.ds(2 * p, 2)], core_sent.at[p], core_land.at[p], other_core)

    @pl.loop(0, 2)
    def _(m):
        for b in range(2):
            p = m * 2 + b

            @pl.when(m > 0)
            def _():
                pair_copy(b, p - 2).wait_send()

            gate_up, down = tile_pair(p, 1 - core)
            for i in range(2):
                stage[b, i, :, : 2 * width] = gate_up[i * ROWS : (i + 1) * ROWS].astype(BF16)
                stage[b, i, :, 2 * width :] = down[i * ROWS : (i + 1) * ROWS].astype(BF16)
            pair_copy(b, p).start()

    far_back_pass()

    @pl.loop(0, 2)
    def _(m):
        for b in range(2):
            p = m * 2 + b
            gate_up, down = tile_pair(p, core)
            pair_copy(b, p).wait_recv()
            for i in range(2):
                at = 2 * p + i
                near = tiles[at]
                value = gate_up[i * ROWS : (i + 1) * ROWS] + near[:, : 2 * width].astype(F32)
                tiles[at, :, : 2 * width] = value.astype(BF16)
                value = down[i * ROWS : (i + 1) * ROWS] + near[:, 2 * width :].astype(F32)
                tiles[at, :, 2 * width :] = value.astype(BF16)

    tile_pass, tile_finish = scatter_ring(
        lambda k, h: tiles.at[h * 4 + lax.rem(x + k, 4)],
        lambda h: tile_relay.at[h],
        lambda r, h: tile_got.at[r, h],
        along_x, x_sent, x_land, waits,
    )
    near_back_pass()
    far_back_finish()
    z_out[...] = summed(4, 2).astype(BF16)
    z_copy = remote(z_out, z_got, across_sent.at[1], across_land.at[1], across)
    z_copy.start()
    waits.append(z_copy)

    def down_part(first):
        rows = pl.ds(first, half)

        @pl.loop(0, model // WIDE)
        def _(n):
            cols = pl.ds(pl.multiple_of(n * WIDE, WIDE), WIDE)
            part[rows, cols] = dot(act[rows, :], down_w[:, cols]).astype(BF16)

    for copy in o_core_copies:
        copy.wait_recv()
    for copy in hid_waits:
        copy.wait_send()
    o_loads = [
        pltpu.make_async_copy(o_full.at[pl.ds(k * half, half), :], ref.at[pl.ds(first, half), :], oload_sem.at[k - 1])
        for k, ref, first in ((1, cots, 0), (2, cots, half), (3, hid, 0))
    ]
    for load in o_loads:
        load.start()
    down_part(0)
    down_part(half)
    outs = [
        pltpu.make_async_copy(part.at[pl.ds(half, half), :], part_hbm, out_sem.at[0]),
        pltpu.make_async_copy(att, att_out, out_sem.at[1]),
    ]
    for copy in outs:
        copy.start()
    part_pass, part_finish = scatter_ring(
        row_slots(part),
        lambda h: relay.at[pl.ds(2 * ROWS + h * (ROWS // 2), ROWS // 2), :],
        lambda r, h: row_slots(o_got)(r, h),
        along, part_sent, part_land, waits,
    )
    tile_pass()
    near_back_finish()
    z_copy.wait_recv()

    rows_back, gain_sum = rms_back(summed(0, 0) + z_got[...].astype(F32), middle[...], gain[...])
    gain_grad[...] = gain_sum
    value = cot[...].astype(F32) + rows_back
    middle_grad[...] = value
    branch[...] = value.astype(BF16)

    def unit_copy(k, h):
        unit = (4 - k) % 4 * 4 + h
        place = dict(ctx_at(unit), **along(k))
        cols = pl.ds(pl.multiple_of((k * 4 + h) * HD, HD), HD)
        return remote(att_grad.at[:, cols], block(grad_got, me), grad_sent.at[k * 4 + h], grad_land.at[me], place)

    for k in range(4):
        at = k * 4 * HD
        if k == 0:
            att_grad[:, :side] = dot(branch[...], o_own[...], ((1,), (1,))).astype(BF16)
            att_grad[:, side : 2 * side] = dot(branch[...], o_par[...], ((1,), (1,))).astype(BF16)
        else:
            o_loads[k - 1].wait()
            rows_of = (cots[:half, :], cots[half:, :], hid[:half, :])[k - 1]
            att_grad[:, at : at + 4 * HD] = dot(branch[...], rows_of, ((1,), (1,))).astype(BF16)

        @pl.loop(0, 4)
        def _(j):
            h = lax.rem(me + j, 4)

            @pl.when((k > 0) | (h != me))
            def _():
                unit_copy(k, h).start()

    def own_grad():
        cols = pl.ds(pl.multiple_of(lax.rem(me, 4) * HD, HD), HD)
        return pltpu.make_async_copy(att_grad.at[:, cols], block(grad_got, me), local_sem.at[1])

    @pl.when(me < 4)
    def _():
        own_grad().start()

    tile_finish()

    def tile_sum(a):
        value = tiles[a * 4 + x].astype(F32)
        for i in range(2):
            value += tile_got[i, a].astype(F32)
        return value

    for b in range(2):
        pair_copy(b, 2 + b).wait_send()
    stage[0, 0] = tile_sum(1 - zl).astype(BF16)
    tile_copy = remote(stage.at[0, 0], tile_z, zl_sent, zl_land, {"zl": 1 - zl})
    tile_copy.start()
    waits.append(tile_copy)
    value = tile_sum(zl)
    gate_wgrad[...] = value[:, :width]
    up_wgrad[...] = value[:, width : 2 * width]
    down_sum[...] = value[:, 2 * width :]
    part_pass()

    @pl.loop(1, 16)
    def _(k):
        peer = lax.rem(me + k, 16)
        att_copy(peer, peer).wait_send()

    @pl.loop(0, 16)
    def _(source):
        @pl.when((me >= 4) | (source != me))
        def _():
            remote(
                att_grad.at[:, pl.ds(0, HD)], block(grad_got, source), grad_sent.at[0], grad_land.at[source], other_core
            ).wait_recv()

    for k in range(4):

        @pl.loop(0, 4)
        def _(h):
            @pl.when((k > 0) | (h != me))
            def _():
                unit_copy(k, h).wait_send()

    @pl.when(me < 4)
    def _():
        own_grad().wait()


    tile_copy.wait_recv()
    gate_wgrad[...] += tile_z[:, :width].astype(F32)
    up_wgrad[...] += tile_z[:, width : 2 * width].astype(F32)
    down = down_sum[...] + tile_z[:, 2 * width :].astype(F32)
    for i in range(width // HD):
        down_wgrad[i * HD : (i + 1) * HD, :] = down[:, i * HD : (i + 1) * HD].T
    part_finish()
    value = middle[...] + part[:ROWS, :].astype(F32)
    for i in range(2):
        value += o_got[i * ROWS : (i + 1) * ROWS, :].astype(F32)
    middle[...] = value
    for copy in waits:
        copy.wait_send()
    for copy in outs:
        copy.wait()


def middle_part(tokens, cot, gain, att, o_own, o_par, cot_half, gate_w, up_w, down_w):
    rows, model = tokens.shape
    width = gate_w.shape[1]
    anywhere = pl.BlockSpec(memory_space=pl.ANY)
    vmem = pl.BlockSpec(memory_space=pltpu.VMEM)
    dma = pltpu.SemaphoreType.DMA
    half = jax.ShapeDtypeStruct((4 * rows, model), BF16)
    low = functools.partial(pltpu.VMEM, dtype=BF16)
    return pl.pallas_call(
        middle_kernel,
        out_shape=(
            jax.ShapeDtypeStruct((rows, model), F32),
            jax.ShapeDtypeStruct((rows, model), F32),
            jax.ShapeDtypeStruct((1, model), F32),
            jax.ShapeDtypeStruct((rows, width), F32),
            jax.ShapeDtypeStruct((rows, width), F32),
            jax.ShapeDtypeStruct((width, rows), F32),
            jax.ShapeDtypeStruct((16 * rows, HD), BF16),
            jax.ShapeDtypeStruct((4 * rows, 4 * HD), BF16),
            jax.ShapeDtypeStruct((rows, model), BF16),
            half,
            jax.ShapeDtypeStruct((16 * HD, model), BF16),
        ),
        in_specs=[vmem] * 3 + [anywhere] * 7,
        out_specs=(vmem,) * 6 + (anywhere,) * 2 + (vmem,) + (anywhere,) * 2,
        scratch_shapes=[
            low((4 * rows, 4 * HD)),
            low((2 * HD, model)),
            low((2 * HD, model)),
            low((3 * rows, model)),
            low((2 * rows, model)),
            low((8 * rows, model)),
            low((8 * rows, model)),
            low((model, width)),
            low((model, width)),
            low((width, model)),
            low((8 * rows, width)),
            low((8 * rows, 2 * width)),
            low((8 * rows, width)),
            low((8 * rows, model)),
            low((4 * rows, model)),
            low((rows, model)),
            low((rows, model)),
            low((8 * rows, model)),
            low((2, 2, rows, 3 * width)),
            low((8, rows, 3 * width)),
            low((2, rows, 3 * width)),
            low((2, 2, rows, 3 * width)),
            low((rows, 3 * width)),
            pltpu.VMEM((rows, width), F32),
            low((rows, 16 * HD)),
            dma((6,)),
            dma((16,)),
            dma((16,)),
            dma((6,)),
            dma((6,)),
            dma((4,)),
            dma((4,)),
            dma((4,)),
            dma((4,)),
            dma((2,)),
            dma((2,)),
            dma((6,)),
            dma((6,)),
            dma((6,)),
            dma((6,)),
            dma((4,)),
            dma((4,)),
            dma((6,)),
            dma((6,)),
            dma((2, 4)),
            dma((2, 4)),
            dma((3, 3, 2)),
            dma((3, 3, 2)),
            dma((3, 2)),
            dma((3, 2)),
            dma((16,)),
            dma((16,)),
            dma((4,)),
            dma((4,)),
            dma((6,)),
            dma((6,)),
            dma,
            dma,
            dma((3,)),
            dma((2,)),
            dma((3,)),
        ],
        compiler_params=pltpu.CompilerParams(
            collective_id=1, has_side_effects=True, vmem_limit_bytes=63 * 2**20
        ),
        cost_estimate=pl.CostEstimate(
            flops=2 * 9 * 8 * rows * model * width, bytes_accessed=40 * 2**20, transcendentals=8 * rows * width
        ),
        name="middle",
    )(tokens, cot, gain, att, o_own, o_par, cot_half, gate_w, up_w, down_w)


def back_kernel(
    place, stored, doc_lengths, log_total, cos, sin, q_gain, k_gain, attn_gain, mlp_gain_grad,
    grad_hbm, q_pos_hbm, k_pos_hbm, v_pos_hbm, part_hbm, branch_hbm, att_hbm, raw_hbm, normed_hbm, own_hbm, par_hbm,
    middle_hbm, tokens_hbm, middle_grad_hbm,
    tokens_grad, out_rows, q_wgrad, k_wgrad, v_wgrad, o_wgrad, attn_total, mlp_total, q_total, k_total,
    grad_in, q_pos, k_pos, v_pos, grad_pos, q_acc, q_grad, send, k_acc, v_acc, keep, raw, middle, tokens, middle_grad,
    normed, w_own, w_par, branch_all, att, part, out_got, relay, out_across, swap_got, kv_out, q_got, kv_got, low_q, low_kv, parts, y_got,
    q_bufs, kv_bufs, o_bufs,
    g_out, g_got, by_gain,
    load_sem, swap_sem, across_sem, q_sent, q_land, kv_sent, kv_land, y_sent, y_land, out_sent, out_land, branch_sent, branch_land,
    core_sent, core_land, x_sent, x_land, z_sent, z_land, g_sent, g_land,
):
    zl, x, core = (lax.axis_index(a) for a in CTX)
    zh, y = (lax.axis_index(a) for a in FSDP)
    me = zl * 8 + x * 2 + core
    half = 4 * HD

    def along_y(k):
        return {"y": lax.rem(y + k, 4)}

    def along_x(k):
        return {"x": lax.rem(x + k, 4)}

    def along_ctx(k):
        return ctx_at(lax.rem(me + k, 16))

    other_core = {"core": 1 - core}
    zs = {1: {"zl": 1 - zl}, 2: {"zh": 1 - zh}, 3: {"zl": 1 - zl, "zh": 1 - zh}}

    loads = [
        pltpu.make_async_copy(src, dst, load_sem.at[i])
        for i, (src, dst) in enumerate(
            (
                (part_hbm, part),
                (grad_hbm, grad_in),
                (q_pos_hbm, q_pos),
                (k_pos_hbm, k_pos),
                (v_pos_hbm, v_pos),
                (branch_hbm, branch_all.at[pl.ds(0, ROWS), :]),
                (att_hbm, att),
                (normed_hbm, normed),
                (raw_hbm, raw),
                (own_hbm, w_own),
                (par_hbm, w_par),
                (middle_hbm, middle),
                (tokens_hbm, tokens),
                (middle_grad_hbm, middle_grad),
            )
        )
    ]
    for load in loads:
        load.start()
    peers([along_ctx(k) for k in range(1, 16)] + [along_y(k) for k in (1, 2, 3)] + [zs[2], zs[3]])
    waits = []

    loads[5].wait()
    branch_pass, branch_finish = gather_ring(row_slots(branch_all), along_y, branch_sent, branch_land, waits)

    def grad_stages(first, tile, to_other, from_other, summed, x_relay, from_x, total, total_low, from_z):
        n = total.shape[2] // 2

        def over_cores():
            @pl.loop(0, 8)
            def _(t):
                to_other[t] = tile(t * 2 + 1 - core).astype(BF16)

            copy = remote(to_other, from_other, core_sent.at[first], core_land.at[first], other_core)
            copy.start()
            waits.append(copy)
            return copy

        def over_x(core_copy):
            core_copy.wait_recv()

            @pl.loop(0, 8)
            def _(t):
                summed[t] = (tile(t * 2 + core) + from_other[t].astype(F32)).astype(BF16)

            return scatter_ring(
                lambda k, h: summed.at[h * 4 + lax.rem(x + k, 4)],
                lambda h: x_relay.at[h],
                lambda r, h: from_x.at[r, h],
                along_x, x_sent.at[first], x_land.at[first], waits,
            )

        def over_z(x_finish):
            x_finish()
            for a in range(2):
                value = summed[a * 4 + x].astype(F32)
                for i in range(2):
                    value += from_x[i, a].astype(F32)
                total[a] = value
                total_low[a] = value.astype(BF16)
            copies = []
            for d in (1, 2, 3):
                rows_of = 1 - zl if d % 2 else zl
                copy = remote(
                    total_low.at[rows_of, :, pl.ds(n if d >= 2 else 0, n)], from_z.at[d - 1],
                    z_sent.at[first * 3 + d - 1], z_land.at[first * 3 + d - 1], zs[d],
                )
                copy.start()
                copies.append(copy)
            waits.extend(copies)
            return copies

        def finish(z_copies):
            for copy in z_copies:
                copy.wait_recv()
            value = total[zl, :, :n]
            for d in range(3):
                value = value + from_z[d].astype(F32)
            return value

        return over_cores, over_x, over_z, finish

    def tile_of(left, right):
        def tile(t):
            cols = pl.ds(pl.multiple_of(t * ROWS, ROWS), ROWS)
            return dot(left[:, cols], right[...], ((0,), (0,)))

        return tile

    q_cores, q_x, q_z, q_finish = grad_stages(0, tile_of(normed, low_q), *q_bufs)
    kv_cores, kv_x, kv_z, kv_finish = grad_stages(1, tile_of(normed, low_kv), *kv_bufs)
    o_cores, o_x, o_z, o_finish = grad_stages(2, tile_of(branch_all, att), *o_bufs)
    for load in loads[:5] + loads[6:7]:
        load.wait()

    blocks = q_pos.shape[0] // BLK
    ordered(stored, blocks, ((grad_in, grad_pos),))
    ends = document_ends(doc_lengths, zh * 4 + lax.rem(y + me // 4, 4))
    attend_back(ends, q_pos, k_pos, v_pos, log_total, grad_pos, q_acc, k_acc, v_acc)
    ordered(place, blocks, ((q_acc, q_grad),))

    @pl.loop(0, blocks)
    def _(b):
        dst_rows = pl.ds(pl.multiple_of(b * BLK, BLK), BLK)
        k_rows = k_acc[place[b]] * HD ** (-0.5)
        v_rows = v_acc[place[b]]
        keep[dst_rows, :] = jnp.where(core == 0, k_rows, v_rows)
        send[dst_rows, :] = jnp.where(core == 0, v_rows, k_rows).astype(BF16)

    swap = remote(send, swap_got, swap_sem.at[0], swap_sem.at[1], other_core)
    swap.start()

    waits.append(swap)

    def to_rows(src, dst, sent, landed):
        copies = []
        for k in range(1, 16):
            copy = remote(block(src, lax.rem(me + k, 16)), block(dst, 16 - k), sent.at[k], landed.at[16 - k], along_ctx(k))
            copy.start()
            copies.append(copy)
        waits.extend(copies)
        return copies

    q_copies = to_rows(q_grad, q_got, q_sent, q_land)
    mine = pl.ds(pl.multiple_of(me * ROWS, ROWS), ROWS)
    q_got[:ROWS, :] = q_grad[mine, :]
    branch_pass()
    out_pass, out_finish = scatter_ring(
        row_slots(part),
        lambda h: relay.at[pl.ds(h * (ROWS // 2), ROWS // 2), :],
        lambda r, h: row_slots(out_got)(r, h),
        along_y, out_sent, out_land, waits,
    )
    swap.wait_recv()
    kv_out[...] = (keep[...] + swap_got[...].astype(F32)).astype(BF16)
    kv_copies = to_rows(kv_out, kv_got, kv_sent, kv_land)
    kv_got[:ROWS, :] = kv_out[mine, :]

    for load in loads[7:]:
        load.wait()
    for copy in q_copies:
        copy.wait_recv()

    g_out[0] = jnp.zeros_like(g_out[0])

    def from_unit(ref, unit):
        return ref[pl.ds(pl.multiple_of(lax.rem(unit - me + 16, 16) * ROWS, ROWS), ROWS), :]

    def head_back(grad, value, gain):
        turned = grad * sin[...]
        turned = jnp.concatenate([turned[:, HD // 2 :], -turned[:, : HD // 2]], axis=1)
        back, gain_sum = rms_back(grad * cos[...] + turned, value, gain)
        return back.astype(BF16), gain_sum

    @pl.loop(0, 4)
    def _(s):
        rows = pl.ds(pl.multiple_of(s * ROWS, ROWS), ROWS)
        for h in range(4):
            at = (h // 2) * half + (h % 2) * HD
            grad = from_unit(q_got, s * 4 + h).astype(F32)
            back, gain_sum = head_back(grad, raw[rows, at : at + HD], q_gain[...])
            low_q[rows, h * HD : (h + 1) * HD] = back
            g_out[0, 32:33, :] += gain_sum

    q_core_copy = q_cores()
    branch_finish()
    o_core_copy = o_cores()
    for copy in kv_copies:
        copy.wait_recv()

    @pl.loop(0, 4)
    def _(s):
        rows = pl.ds(pl.multiple_of(s * ROWS, ROWS), ROWS)
        for kv in range(2):
            at = kv * half + 2 * HD
            grad = from_unit(kv_got, s * 4 + kv * 2).astype(F32)
            back, gain_sum = head_back(grad, raw[rows, at : at + HD], k_gain[...])
            low_kv[rows, kv * 2 * HD : (kv * 2 + 1) * HD] = back
            g_out[0, 33:34, :] += gain_sum
            low_kv[rows, (kv * 2 + 1) * HD : (kv * 2 + 2) * HD] = from_unit(kv_got, s * 4 + kv * 2 + 1)

    kv_core_copy = kv_cores()
    out_pass()
    q_x_pass, q_x_finish = q_x(q_core_copy)
    @pl.loop(0, parts.shape[1] // WIDE)
    def _(n):
        cols = pl.ds(pl.multiple_of(n * WIDE, WIDE), WIDE)
        total = dot(low_q[:, : half // 2], w_own[cols, : half // 2], ((1,), (1,)))
        total += dot(low_q[:, half // 2 :], w_par[cols, : half // 2], ((1,), (1,)))
        total += dot(low_kv[:, : half // 2], w_own[cols, half // 2 :], ((1,), (1,)))
        total += dot(low_kv[:, half // 2 :], w_par[cols, half // 2 :], ((1,), (1,)))
        parts[:, cols] = total.astype(BF16)
        by_gain[:, cols] = jnp.sum(total * normed[:, cols].astype(F32), axis=0, keepdims=True) / attn_gain[:, cols]

    for i in range(16):
        g_out[0, i : i + 1, :] = by_gain[:, i * HD : (i + 1) * HD]
        g_out[0, 16 + i : 17 + i, :] = mlp_gain_grad[:, i * HD : (i + 1) * HD]
    y_pass, y_finish = scatter_ring(
        row_slots(parts),
        lambda h: relay.at[pl.ds(ROWS + h * (ROWS // 2), ROWS // 2), :],
        lambda r, h: row_slots(y_got)(r, h),
        along_y, y_sent, y_land, waits,
    )

    def gain_stage(stage, places):
        copies = []
        for i, (place, back_slot) in enumerate(places):
            copy = remote(
                g_out.at[stage], g_got.at[stage, back_slot], g_sent.at[stage * 3 + i],
                g_land.at[stage * 3 + back_slot], place,
            )
            copy.start()
            copies.append(copy)
        waits.extend(copies)
        return copies

    def gain_sum_of(stage, copies):
        for copy in copies:
            copy.wait_recv()
        total = g_out[stage]
        for i in range(len(copies)):
            total = total + g_got[stage, i]
        return total

    copies = gain_stage(0, [(along_y(k), 3 - k) for k in (1, 2, 3)])
    kv_x_pass, kv_x_finish = kv_x(kv_core_copy)
    q_x_pass()
    o_x_pass, o_x_finish = o_x(o_core_copy)
    out_finish()
    value = part[:ROWS, :].astype(F32)
    for i in range(2):
        value += out_got[i * ROWS : (i + 1) * ROWS, :].astype(F32)
    part[:ROWS, :] = value.astype(BF16)
    across_copy = remote(part.at[pl.ds(0, ROWS), :], out_across, across_sem.at[0], across_sem.at[1], zs[2])
    across_copy.start()
    waits.append(across_copy)
    y_pass()
    kv_x_pass()
    g_out[1] = gain_sum_of(0, copies)
    copies = gain_stage(1, [(along_x(k), 3 - k) for k in (1, 2, 3)])
    o_x_pass()
    q_z_copies = q_z(q_x_finish)
    g_out[2] = gain_sum_of(1, copies)
    copies = gain_stage(2, [(zs[d], d - 1) for d in (1, 2, 3)])
    across_copy.wait_recv()
    out_rows[...] = (middle[...] + out_across[...].astype(F32)).astype(BF16)
    kv_z_copies = kv_z(kv_x_finish)

    y_finish()
    grad = parts[:ROWS, :].astype(F32)
    for i in range(2):
        grad += y_got[i * ROWS : (i + 1) * ROWS, :].astype(F32)
    rows_back, _ = rms_back(grad, tokens[...].astype(F32), attn_gain[...])
    tokens_grad[...] = (middle_grad[...] + rows_back).astype(BF16)
    g_out[3] = gain_sum_of(2, copies)
    copies = gain_stage(3, [(other_core, 0)])
    o_z_copies = o_z(o_x_finish)
    q_wgrad[...] = q_finish(q_z_copies)
    value = kv_finish(kv_z_copies)
    k_wgrad[...] = value[:, :HD]
    v_wgrad[...] = value[:, HD:]
    value = o_finish(o_z_copies)
    for i in range(2):
        o_wgrad[i * HD : (i + 1) * HD, :] = value[:, i * HD : (i + 1) * HD].T
    gains = gain_sum_of(3, copies)
    for i in range(16):
        attn_total[:, i * HD : (i + 1) * HD] = gains[i : i + 1, :]
        mlp_total[:, i * HD : (i + 1) * HD] = gains[16 + i : 17 + i, :]
    q_total[...] = gains[32:33, :]
    k_total[...] = gains[33:34, :]
    for copy in waits:
        copy.wait_send()


def stage_buffers(rows):
    wide = 4 * HD
    low = functools.partial(pltpu.VMEM, dtype=BF16)
    return (
        low((8, rows, wide)),
        low((8, rows, wide)),
        low((8, rows, wide)),
        low((2, rows, wide)),
        low((2, 2, rows, wide)),
        pltpu.VMEM((2, rows, wide), F32),
        low((2, rows, wide)),
        low((3, rows, wide // 2)),
    )


def back(place, stored, doc_lengths, log_total, cos, sin, q_gain, k_gain, attn_gain, mlp_gain_grad, grad_in, q_pos, k_pos,
         v_pos, part, branch, att, raw, normed, w_own, w_par, middle, tokens, middle_grad):
    rows, model = tokens.shape
    wide = raw.shape[1]
    anywhere = pl.BlockSpec(memory_space=pl.ANY)
    vmem = pl.BlockSpec(memory_space=pltpu.VMEM)
    dma = pltpu.SemaphoreType.DMA
    return pl.pallas_call(
        back_kernel,
        out_shape=(
            jax.ShapeDtypeStruct((rows, model), BF16),
            jax.ShapeDtypeStruct((rows, model), BF16),
            jax.ShapeDtypeStruct((rows, 2 * HD), F32),
            jax.ShapeDtypeStruct((rows, HD), F32),
            jax.ShapeDtypeStruct((rows, HD), F32),
            jax.ShapeDtypeStruct((2 * HD, rows), F32),
            jax.ShapeDtypeStruct((1, model), F32),
            jax.ShapeDtypeStruct((1, model), F32),
            jax.ShapeDtypeStruct((1, HD), F32),
            jax.ShapeDtypeStruct((1, HD), F32),
        ),
        in_specs=[pl.BlockSpec(memory_space=pltpu.SMEM)] * 3 + [vmem] * 7 + [anywhere] * 14,
        out_specs=(vmem,) * 10,
        scratch_shapes=[pltpu.VMEM((16 * rows // BLK, BLK, HD), BF16)]
        + [pltpu.VMEM((16 * rows, HD), BF16)] * 4
        + [pltpu.VMEM((16 * rows // BLK, BLK, HD), BF16)]
        + [pltpu.VMEM((16 * rows, HD), BF16)] * 2
        + [pltpu.VMEM((16 * rows // BLK, BLK, HD), F32)] * 2
        + [pltpu.VMEM((16 * rows, HD), F32)]
        + [
            pltpu.VMEM((4 * rows, wide), F32),
            pltpu.VMEM((rows, model), F32),
            pltpu.VMEM((rows, model), BF16),
            pltpu.VMEM((rows, model), F32),
            pltpu.VMEM((4 * rows, model), BF16),
            pltpu.VMEM((model, wide // 2), BF16),
            pltpu.VMEM((model, wide // 2), BF16),
            pltpu.VMEM((4 * rows, model), BF16),
            pltpu.VMEM((4 * rows, 4 * HD), BF16),
            pltpu.VMEM((4 * rows, model), BF16),
            pltpu.VMEM((2 * rows, model), BF16),
            pltpu.VMEM((2 * rows, model), BF16),
            pltpu.VMEM((rows, model), BF16),
            pltpu.VMEM((16 * rows, HD), BF16),
            pltpu.VMEM((16 * rows, HD), BF16),
            pltpu.VMEM((16 * rows, HD), BF16),
            pltpu.VMEM((16 * rows, HD), BF16),
            pltpu.VMEM((4 * rows, wide // 2), BF16),
            pltpu.VMEM((4 * rows, wide // 2), BF16),
            pltpu.VMEM((4 * rows, model), BF16),
            pltpu.VMEM((2 * rows, model), BF16),
            stage_buffers(rows),
            stage_buffers(rows),
            stage_buffers(rows),
            pltpu.VMEM((4, 40, HD), F32),
            pltpu.VMEM((4, 3, 40, HD), F32),
            pltpu.VMEM((1, model), F32),
            dma((14,)),
            dma((2,)),
            dma((2,)),
            dma((16,)),
            dma((16,)),
            dma((16,)),
            dma((16,)),
            dma((6,)),
            dma((6,)),
            dma((6,)),
            dma((6,)),
            dma((4,)),
            dma((4,)),
            dma((3,)),
            dma((3,)),
            dma((3, 6)),
            dma((3, 6)),
            dma((9,)),
            dma((9,)),
            dma((12,)),
            dma((12,)),
        ],
        compiler_params=pltpu.CompilerParams(
            collective_id=2, has_side_effects=True, vmem_limit_bytes=62 * 2**20
        ),
        cost_estimate=pl.CostEstimate(
            flops=4 * 4 * rows * model * wide, bytes_accessed=24 * 2**20, transcendentals=0
        ),
        name="back",
    )(
        place, stored, doc_lengths, log_total, cos, sin, q_gain, k_gain, attn_gain, mlp_gain_grad,
        grad_in.reshape(-1, BLK, HD), q_pos, k_pos, v_pos, part, branch, att, raw, normed, w_own, w_par, middle, tokens, middle_grad,
    )


def results_kernel(*refs):
    count = (len(refs) - 2) // 3
    arrays, outs, held, (in_sem, out_sem) = refs[:count], refs[count : 2 * count], refs[2 * count : 3 * count], refs[-2:]
    copies = [pltpu.make_async_copy(arrays[i], held[i], in_sem.at[i]) for i in range(count)]
    for copy in copies:
        copy.start()
    for i in range(count):
        copies[i].wait()
        copies[i] = pltpu.make_async_copy(held[i], outs[i], out_sem.at[i])
        copies[i].start()
    for copy in copies:
        copy.wait()


def results(arrays):
    anywhere = pl.BlockSpec(memory_space=pl.ANY)
    return pl.pallas_call(
        results_kernel,
        out_shape=tuple(jax.ShapeDtypeStruct(a.shape, a.dtype) for a in arrays),
        in_specs=[anywhere] * len(arrays),
        out_specs=(anywhere,) * len(arrays),
        scratch_shapes=[pltpu.VMEM(a.shape, a.dtype) for a in arrays] + [pltpu.SemaphoreType.DMA((len(arrays),))] * 2,
        compiler_params=pltpu.CompilerParams(vmem_limit_bytes=62 * 2**20),
        name="results",
    )(*arrays)


def per_device(
    tokens,
    cotangent,
    attn_gain,
    q_weight,
    k_weight,
    v_weight,
    q_gain,
    k_gain,
    o_weight,
    mlp_gain,
    gate_weight,
    up_weight,
    down_weight,
    doc_lengths,
    block_place,
):
    rows = tokens.shape[1]
    zl, x, core = (lax.axis_index(a) for a in CTX)
    ctx_place = zl * 8 + x * 2 + core
    numbers = jnp.arange(block_place.shape[0], dtype=jnp.int32)
    stored = jnp.sum(jnp.where(block_place[None, :] == numbers[:, None], numbers[None, :], 0), axis=1, dtype=jnp.int32)
    own_blocks = lax.dynamic_slice_in_dim(block_place, ctx_place * (rows // BLK), rows // BLK)
    own_positions = (own_blocks[:, None] * BLK + jnp.arange(BLK, dtype=jnp.int32)[None, :]).reshape(-1)
    cos_rows, sin_rows = tables(own_positions, HD)
    q_gain, k_gain = q_gain.reshape(1, HD), k_gain.reshape(1, HD)
    attn_gain, mlp_gain = attn_gain.reshape(1, -1), mlp_gain.reshape(1, -1)
    cot = cotangent[0]

    log_total, out, q_pos, k_pos, v_pos, raw, normed, w_own, w_par, o_par, cot_half = pre(
        block_place, stored, doc_lengths, tokens[0], cos_rows, sin_rows, attn_gain, q_gain, k_gain, cot, q_weight, k_weight,
        v_weight, o_weight,
    )
    (
        middle, middle_grad, mlp_gain_grad, gate_wgrad, up_wgrad, down_wgrad, grad_in, att, branch, part, _,
    ) = middle_part(tokens[0], cot, mlp_gain, out, o_weight, o_par, cot_half, gate_weight, up_weight, down_weight)
    (
        tokens_grad, out_rows, q_wgrad, k_wgrad, v_wgrad, o_wgrad, attn_gain_grad, mlp_gain_grad, q_gain_grad, k_gain_grad,
    ) = back(
        block_place, stored, doc_lengths, log_total, cos_rows, sin_rows, q_gain, k_gain, attn_gain, mlp_gain_grad, grad_in,
        q_pos, k_pos, v_pos, part, branch, att, raw, normed, w_own, w_par, middle, tokens[0], middle_grad,
    )
    (
        out_rows, tokens_grad, attn_gain_grad, q_wgrad, k_wgrad, v_wgrad, q_gain_grad, k_gain_grad, o_wgrad, mlp_gain_grad,
        gate_wgrad, up_wgrad, down_wgrad,
    ) = results(
        (
            out_rows, tokens_grad, attn_gain_grad, q_wgrad, k_wgrad, v_wgrad, q_gain_grad, k_gain_grad, o_wgrad,
            mlp_gain_grad, gate_wgrad, up_wgrad, down_wgrad,
        )
    )
    return (
        out_rows[None],
        tokens_grad[None],
        attn_gain_grad[0],
        q_wgrad,
        k_wgrad,
        v_wgrad,
        q_gain_grad[0],
        k_gain_grad[0],
        o_wgrad,
        mlp_gain_grad[0],
        gate_wgrad,
        up_wgrad,
        down_wgrad,
    )


def solution(mesh):
    fine = Mesh(mesh.devices.reshape(SIZES), AXES)
    rows = P(FSDP, CTX, None)
    in_specs = (
        rows,
        rows,
        P(),
        P(None, FSDP),
        P(None, FSDP),
        P(None, FSDP),
        P(),
        P(),
        P(FSDP, None),
        P(),
        P(None, FSDP),
        P(None, FSDP),
        P(FSDP, None),
        P(),
        P(),
    )
    out_specs = (
        rows,
        rows,
        P(),
        P(CTX, FSDP),
        P(CTX, FSDP),
        P(CTX, FSDP),
        P(),
        P(),
        P(FSDP, CTX),
        P(),
        P(CTX, FSDP),
        P(CTX, FSDP),
        P(FSDP, CTX),
    )
    return jax.shard_map(
        per_device, mesh=fine, in_specs=in_specs, out_specs=out_specs, check_vma=False
    )
```

```python
import functools

import jax
import jax.numpy as jnp
from jax import lax
from jax.experimental import pallas as pl
from jax.experimental.pallas import tpu as pltpu
from jax.sharding import Mesh, PartitionSpec as P

EPSILON = 1e-06
ROPE_BASE = 1000000.0
MASKED_SCORE = -1e30
HD = 128
BLK = 64
AXES = ("zl", "x", "core", "zh", "y")
SIZES = (2, 4, 2, 2, 4)
CTX = ("zl", "x", "core")
FSDP = ("zh", "y")
F32 = jnp.float32
BF16 = jnp.bfloat16


def tables(positions, head_dim):
    exponent_steps = jnp.arange(head_dim // 2, dtype=jnp.int32).astype(F32) * (2.0 / head_dim)
    frequency = ROPE_BASE ** (-exponent_steps)
    phases = positions.astype(F32)[:, None] * frequency[None, :]
    phases = jnp.concatenate([phases, phases], axis=-1)
    return (jnp.cos(phases), jnp.sin(phases))


def dot(left, right, contract=((1,), (0,))):
    return lax.dot_general(left, right, (contract, ((), ())), preferred_element_type=F32)


TILE = 256


def keep_mask(ends, first_row, rows, cols):
    place = first_row + lax.broadcasted_iota(jnp.int32, (rows, 1), 0)
    start = jnp.zeros((rows, 1), jnp.int32)
    for end in ends:
        start = jnp.where(place >= end, end, start)
    key = lax.broadcasted_iota(jnp.int32, (rows, cols), 1)
    return (key >= start) & (key <= place)


def ordered(order, blocks, pairs):
    @pl.loop(0, blocks)
    def _(b):
        rows = pl.ds(pl.multiple_of(b * BLK, BLK), BLK)
        for src, dst in pairs:
            dst[rows, :] = src[order[b]]


def attend(ends, q_pos, k_pos, v_pos, out_pos, log_total):
    for i in range(q_pos.shape[0] // TILE):
        span = pl.ds(i * TILE, TILE)
        n = (i + 1) * TILE
        scores = dot(q_pos[span, :], k_pos[:n, :], ((1,), (1,))) * HD ** (-0.5)
        scores = jnp.where(keep_mask(ends, i * TILE, TILE, n), scores, MASKED_SCORE)
        top = jnp.max(scores, axis=-1, keepdims=True)
        weights = jnp.exp(scores - top)
        total = jnp.sum(weights, axis=-1, keepdims=True)
        log_total[span, :] = top + jnp.log(total)
        probs = (weights * (1.0 / total)).astype(BF16)
        out_pos[i * TILE // BLK : n // BLK] = dot(probs, v_pos[:n, :]).astype(BF16).reshape(TILE // BLK, BLK, HD)


def attend_back(ends, q_pos, k_pos, v_pos, log_total, grad_pos, q_acc, k_acc, v_acc):
    scale = HD ** (-0.5)
    k_acc[...] = jnp.zeros_like(k_acc)
    v_acc[...] = jnp.zeros_like(v_acc)
    for i in range(q_pos.shape[0] // TILE):
        span = pl.ds(i * TILE, TILE)
        n = (i + 1) * TILE
        queries = q_pos[span, :]
        grads = grad_pos[span, :]
        scores = dot(queries, k_pos[:n, :], ((1,), (1,))) * scale
        kept = keep_mask(ends, i * TILE, TILE, n)
        probs = jnp.where(kept, jnp.exp(scores - log_total[span, :]), 0.0)
        prob_grad = dot(grads, v_pos[:n, :], ((1,), (1,)))
        row_dot = jnp.sum(prob_grad * probs, axis=-1, keepdims=True)
        score_grad = (probs * (prob_grad - row_dot)).astype(BF16)
        q_rows = (dot(score_grad, k_pos[:n, :]) * scale).astype(BF16)
        q_acc[i * TILE // BLK : n // BLK] = q_rows.reshape(TILE // BLK, BLK, HD)
        k_acc[: n // BLK] += dot(score_grad, queries, ((0,), (0,))).reshape(n // BLK, BLK, HD)
        v_acc[: n // BLK] += dot(probs.astype(BF16), grads, ((0,), (0,))).reshape(n // BLK, BLK, HD)


def document_ends(doc_lengths, sequence):
    ends = [doc_lengths[sequence, 0]]
    for j in range(1, doc_lengths.shape[1]):
        ends.append(ends[-1] + doc_lengths[sequence, j])
    return ends


def peers(pairs):
    barrier = pltpu.get_barrier_semaphore()
    for place in pairs:
        pl.semaphore_signal(barrier, inc=1, device_id=place, device_id_type=pl.DeviceIdType.MESH)
    pl.semaphore_wait(barrier, len(pairs))


def remote(src, dst, sent, landed, place):
    return pltpu.make_async_remote_copy(
        src_ref=src, dst_ref=dst, send_sem=sent, recv_sem=landed, device_id=place,
        device_id_type=pl.DeviceIdType.MESH,
    )


ROWS = 128
WIDE = 256


def ctx_at(index):
    return {"zl": index // 8, "x": lax.rem(index // 2, 4), "core": lax.rem(index, 2)}


def block(ref, index):
    return ref.at[pl.ds(pl.multiple_of(index * ROWS, ROWS), ROWS), :]


def pair(ref, index):
    return ref.at[pl.ds(index * 2, 2)]


def inverse_rms(values):
    return lax.rsqrt(jnp.mean(values * values, axis=-1, keepdims=True) + EPSILON)


def rms_back(grad, values, gain):
    inverse = inverse_rms(values)
    scaled = grad * gain
    inner = jnp.mean(values * scaled, axis=-1, keepdims=True)
    back = inverse * scaled - values * (inverse * inverse * inverse * inner)
    return back, jnp.sum(grad * values * inverse, axis=0, keepdims=True)


def gather_ring(slot, along, sent, landed, waits, own=None):
    def move(src, dst, i, k):
        copy = remote(src, dst, sent.at[i], landed.at[i], along(k))
        copy.start()
        waits.append(copy)
        return copy

    own = slot(0) if own is None else own
    near = [move(own, slot(1), 0, 3), move(own, slot(3), 1, 1)]
    far = []

    def pass_on():
        for h, k in ((0, 3), (1, 1)):
            near[h].wait_recv()
            far.append(move(slot(1 + 2 * h, h), slot(2, h), 2 + h, k))

    def finish():
        for copy in far:
            copy.wait_recv()

    return pass_on, finish


def scatter_ring(part, relay, got, along, sent, landed, waits, wait_for_far=False):
    def move(src, dst, i, k):
        copy = remote(src, dst, sent.at[i], landed.at[i], along(k))
        copy.start()
        waits.append(copy)
        return copy

    first, last = [], []

    def send_far():
        first.extend([move(part(2, 0), relay(0), 0, 1), move(part(2, 1), relay(1), 1, 3)])

    if not wait_for_far:
        send_far()
    last.extend([move(part(1, 1), got(0, 1), 2, 1), move(part(3, 0), got(1, 0), 3, 3)])

    def pass_on():
        for h, k in ((0, 1), (1, 3)):
            first[h].wait_recv()
            ref = part(k, h)
            ref[...] = (ref[...].astype(F32) + relay(h)[...].astype(F32)).astype(BF16)
            last.append(move(ref, got(h, h), 4 + h, k))

    def finish():
        for copy in last:
            copy.wait_recv()

    return (pass_on, finish, send_far) if wait_for_far else (pass_on, finish)


def row_slots(ref, base=0):
    def slot(r, h=None):
        if h is None:
            return ref.at[pl.ds((base + r) * ROWS, ROWS), :]
        return ref.at[pl.ds((base + r) * ROWS + h * (ROWS // 2), ROWS // 2), :]

    return slot


def pre_kernel(
    place, stored, doc_lengths, tokens, cos, sin, attn_gain, q_gain, k_gain, cot_hbm, q_hbm, k_hbm, v_hbm, o_hbm,
    log_total, out_hbm, q_hbm_out, k_hbm_out, v_hbm_out, raw_hbm, normed_hbm, own_hbm, par_hbm, o_par_hbm, cot_got,
    q_got, mine, other, q_pos, k_pos, v_pos, out_pos, out, normed, w_own, w_par, o_own, o_par, raw, q_out, kv_out,
    load_sem, y_sent, y_land, cot_sent, cot_land, z_sent, z_land, x_sent, x_land, core_sent, core_land,
    q_sent, q_land, kv_sent, kv_land, swap_sem, local_sem, out_sem,
):
    zl, x, core = (lax.axis_index(a) for a in CTX)
    zh, y = (lax.axis_index(a) for a in FSDP)
    me = zl * 8 + x * 2 + core
    half = 4 * HD
    waits = []

    def along_y(k):
        return {"y": lax.rem(y + k, 4)}

    def along_x(k):
        return {"x": lax.rem(x + k, 4)}

    other_core = {"core": 1 - core}
    cross = {"zl": 1 - zl, "zh": 1 - zh}
    q_width, k_width = q_hbm.shape[1], k_hbm.shape[1]
    pieces = (
        (q_hbm, w_own.at[:, pl.ds(0, q_width)]),
        (k_hbm, w_own.at[:, pl.ds(q_width, k_width)]),
        (v_hbm, w_own.at[:, pl.ds(q_width + k_width, k_width)]),
        (o_hbm, o_own),
    )
    loads = [pltpu.make_async_copy(src, dst, load_sem.at[i]) for i, (src, dst) in enumerate(pieces)]
    for load in loads:
        load.start()
    own_cot = pltpu.make_async_copy(cot_hbm, cot_got.at[pl.ds(0, ROWS), :], local_sem.at[0])
    own_cot.start()
    rows_in = tokens[...].astype(F32)
    normed[:ROWS, :] = (rows_in * inverse_rms(rows_in) * attn_gain[...]).astype(BF16)
    peers([ctx_at(lax.rem(me + k, 16)) for k in range(1, 16)] + [along_y(k) for k in (1, 2, 3)] + [cross])

    normed_pass, normed_finish = gather_ring(row_slots(normed), along_y, y_sent, y_land, waits)
    for load in loads:
        load.wait()

    def shard_stage(src, dst, first):
        eighth = src.shape[0] // 8

        def piece(ref, at_x, at_core):
            return ref.at[pl.ds(pl.multiple_of((at_x * 2 + at_core) * eighth, eighth), eighth), :]

        over_z = remote(piece(src, x, core), piece(dst, x, core), z_sent.at[first], z_land.at[first], cross)
        over_z.start()
        waits.append(over_z)

        def to_core(k):
            at_x = lax.rem(x + k, 4)
            copy = remote(
                piece(dst, at_x, core), piece(dst, at_x, core), core_sent.at[first * 4 + k],
                core_land.at[first * 4 + k], other_core,
            )
            copy.start()
            waits.append(copy)
            return copy

        def next_stage():
            over_z.wait_recv()
            copies = []
            for k in (1, 3, 2):
                copy = remote(
                    piece(dst, x, core), piece(dst, x, core), x_sent.at[first * 4 + k],
                    x_land.at[first * 4 + 4 - k], along_x(k),
                )
                copy.start()
                copies.append((4 - k, copy))
            waits.extend(copy for _, copy in copies)
            cores = [to_core(0)]

            def last_stage():
                for k, copy in copies:
                    copy.wait_recv()
                    cores.append(to_core(k))

                def finish():
                    for copy in cores:
                        copy.wait_recv()

                return finish

            return last_stage

        return next_stage

    def prepared(value, gain):
        scaled = value * inverse_rms(value) * gain
        turned = jnp.concatenate([-scaled[:, HD // 2 :], scaled[:, : HD // 2]], axis=1)
        return (scaled * cos[...] + turned * sin[...]).astype(BF16)

    def unit_copy(src, dst, sent, landed, dest):
        return remote(pair(src, dest), pair(dst, me), sent.at[dest], landed.at[me], ctx_at(dest))

    def put(ref, unit, value):
        ref[unit * 2 : unit * 2 + 2] = value.reshape(2, BLK, HD)

    def units(s, side):
        rows = slice(s * ROWS, (s + 1) * ROWS)
        unit = s * 4 + side * 2
        for g in range(2):
            at = side * half + g * HD
            put(q_out, unit + g, prepared(raw[rows, at : at + HD], q_gain[...]))
        at = side * half + 2 * HD
        put(kv_out, unit, prepared(raw[rows, at : at + HD], k_gain[...]))
        put(kv_out, unit + 1, raw[rows, at + HD : at + 2 * HD].astype(BF16))
        for g in range(2):
            dest = unit + lax.rem(me + g, 2)

            @pl.when(dest != me)
            def _():
                unit_copy(kv_out, mine, kv_sent, kv_land, dest).start()
                unit_copy(q_out, q_got, q_sent, q_land, dest).start()

    def own_side(s):
        rows = slice(s * ROWS, (s + 1) * ROWS)
        raw[rows, :half] = dot(normed[rows, :], w_own[...])
        units(s, 0)

    qkv_stage = shard_stage(w_own, w_par, 0)
    o_stage = shard_stage(o_own, o_par, 1)
    own_side(0)
    qkv_stage = qkv_stage()
    o_stage = o_stage()
    normed_pass()
    cot_pass, cot_finish = gather_ring(row_slots(cot_got), along_y, cot_sent, cot_land, waits, cot_hbm)
    own_side(1)
    own_side(3)
    qkv_finish = qkv_stage()
    normed_finish()
    own_side(2)
    qkv_finish()
    raw[:, half:] = dot(normed[...], w_par[...])
    for s in (2, 3, 1, 0):
        units(s, 1)
    o_finish = o_stage()
    local = [
        pltpu.make_async_copy(pair(q_out, me), pair(q_got, me), local_sem.at[1]),
        pltpu.make_async_copy(pair(kv_out, me), pair(mine, me), local_sem.at[2]),
    ]
    for copy in local:
        copy.start()
    o_finish()
    outs = [
        pltpu.make_async_copy(src, dst, out_sem.at[i])
        for i, (src, dst) in enumerate(
            ((raw, raw_hbm), (normed, normed_hbm), (w_own, own_hbm), (w_par, par_hbm), (o_par, o_par_hbm))
        )
    ]
    for copy in outs:
        copy.start()

    def from_unit(src, dst, sent, landed, source):
        return remote(pair(src, source), pair(dst, source), sent.at[source], landed.at[source], ctx_at(source))

    local[1].wait()

    @pl.loop(0, 16)
    def _(source):
        @pl.when(source != me)
        def _():
            from_unit(kv_out, mine, kv_sent, kv_land, source).wait_recv()

    swap = remote(mine, other, swap_sem.at[0], swap_sem.at[1], other_core)
    swap.start()

    @pl.loop(0, 16)
    def _(source):
        @pl.when(source != me)
        def _():
            from_unit(q_out, q_got, q_sent, q_land, source).wait_recv()
            from_unit(q_out, q_got, q_sent, q_land, source).wait_send()
            from_unit(kv_out, mine, kv_sent, kv_land, source).wait_send()

    swap.wait()
    local[0].wait()
    cot_pass()

    blocks = q_pos.shape[0] // BLK

    @pl.when(core == 0)
    def _():
        ordered(stored, blocks, ((q_got, q_pos), (mine, k_pos), (other, v_pos)))

    @pl.when(core == 1)
    def _():
        ordered(stored, blocks, ((q_got, q_pos), (other, k_pos), (mine, v_pos)))

    more = [
        pltpu.make_async_copy(src, dst, out_sem.at[5 + i])
        for i, (src, dst) in enumerate(((q_pos, q_hbm_out), (k_pos, k_hbm_out), (v_pos, v_hbm_out)))
    ]
    for copy in more:
        copy.start()
    outs.extend(more)
    ends = document_ends(doc_lengths, zh * 4 + lax.rem(y + me // 4, 4))
    attend(ends, q_pos, k_pos, v_pos, out_pos, log_total)
    ordered(place, blocks, ((out_pos, out),))
    out_copy = pltpu.make_async_copy(out, out_hbm, out_sem.at[8])
    out_copy.start()
    outs.append(out_copy)
    cot_finish()
    own_cot.wait()
    for copy in outs:
        copy.wait()
    for copy in waits:
        copy.wait_send()


def pre(place, stored, doc_lengths, tokens, cos, sin, attn_gain, q_gain, k_gain, cot, q_w, k_w, v_w, o_w):
    rows, model = tokens.shape
    wide = q_w.shape[1] + k_w.shape[1] + v_w.shape[1]
    anywhere = pl.BlockSpec(memory_space=pl.ANY)
    vmem = pl.BlockSpec(memory_space=pltpu.VMEM)
    dma = pltpu.SemaphoreType.DMA
    unit = jax.ShapeDtypeStruct((16 * rows, HD), BF16)
    return pl.pallas_call(
        pre_kernel,
        out_shape=(
            jax.ShapeDtypeStruct((16 * rows, 1), F32),
            unit,
            unit,
            unit,
            unit,
            jax.ShapeDtypeStruct((4 * rows, 2 * wide), F32),
            jax.ShapeDtypeStruct((4 * rows, model), BF16),
            jax.ShapeDtypeStruct((model, wide), BF16),
            jax.ShapeDtypeStruct((model, wide), BF16),
            jax.ShapeDtypeStruct(o_w.shape, BF16),
            jax.ShapeDtypeStruct((4 * rows, model), BF16),
        ),
        in_specs=[pl.BlockSpec(memory_space=pltpu.SMEM)] * 3 + [vmem] * 6 + [anywhere] * 5,
        out_specs=(vmem,) + (anywhere,) * 10,
        scratch_shapes=[pltpu.VMEM((16 * rows // BLK, BLK, HD), BF16)] * 3
        + [pltpu.VMEM((16 * rows, HD), BF16)] * 3
        + [pltpu.VMEM((16 * rows // BLK, BLK, HD), BF16), pltpu.VMEM((16 * rows, HD), BF16)]
        + [
            pltpu.VMEM((4 * rows, model), BF16),
            pltpu.VMEM((model, wide), BF16),
            pltpu.VMEM((model, wide), BF16),
            pltpu.VMEM(o_w.shape, BF16),
            pltpu.VMEM(o_w.shape, BF16),
            pltpu.VMEM((4 * rows, 2 * wide), F32),
            pltpu.VMEM((16 * rows // BLK, BLK, HD), BF16),
            pltpu.VMEM((16 * rows // BLK, BLK, HD), BF16),
            dma((4,)),
            dma((4,)),
            dma((4,)),
            dma((4,)),
            dma((4,)),
            dma((2,)),
            dma((2,)),
            dma((8,)),
            dma((8,)),
            dma((8,)),
            dma((8,)),
            dma((16,)),
            dma((16,)),
            dma((16,)),
            dma((16,)),
            dma((2,)),
            dma((3,)),
            dma((9,)),
        ],
        compiler_params=pltpu.CompilerParams(
            collective_id=3, has_side_effects=True, vmem_limit_bytes=58 * 2**20
        ),
        cost_estimate=pl.CostEstimate(
            flops=2 * 4 * rows * model * 2 * wide, bytes_accessed=24 * 2**20, transcendentals=0
        ),
        name="pre",
    )(place, stored, doc_lengths, tokens, cos, sin, attn_gain, q_gain, k_gain, cot, q_w, k_w, v_w, o_w)


def middle_kernel(
    tokens, cot, gain, att_hbm, o_own_hbm, o_par_hbm, cot_hbm, gate_hbm, up_hbm, down_hbm,
    middle, middle_grad, gain_grad, mlp_total, mlp_low, grad_got, att_out, branch, part_hbm, o_full,
    att, o_own, o_par, relay, o_got, hid, cots, gate_w, up_w, down_w, act_grad, gu_grad, act, parts, got, z_out, z_got,
    part, stage, tiles, tile_relay, tile_got, att_grad,
    load_sem, att_sent, att_land, o_sent, o_land, hid_sent, hid_land, far_sent, far_land, across_sent, across_land,
    near_back_sent, near_back_land, far_back_sent, far_back_land, cot_sent, cot_land, part_sent, part_land,
    oy_sent, oy_land, ox_sent, ox_land, oc_sent, oc_land, grad_sent, grad_land, core_sent, core_land, x_sent, x_land,
    out_sem, local_sem, oload_sem,
):
    zl, x, core = (lax.axis_index(a) for a in CTX)
    zh, y = (lax.axis_index(a) for a in FSDP)
    me = zl * 8 + x * 2 + core
    half = 4 * ROWS
    width = gate_w.shape[1]
    model = hid.shape[1]
    side = 2 * HD
    waits = []

    def along(k):
        return {"y": lax.rem(y + k, 4)}

    def along_x(k):
        return {"x": lax.rem(x + k, 4)}

    across = {"zh": 1 - zh}
    other_core = {"core": 1 - core}
    loads = [
        pltpu.make_async_copy(src, dst, load_sem.at[i])
        for i, (src, dst) in enumerate(
            (
                (o_own_hbm, o_own),
                (o_par_hbm, o_par),
                (cot_hbm, cots.at[pl.ds(0, half), :]),
                (down_hbm, down_w),
                (gate_hbm, gate_w),
                (up_hbm, up_w),
            )
        )
    ]
    for load in loads:
        load.start()
    barrier = pltpu.get_barrier_semaphore()
    places = [ctx_at(lax.rem(me + k, 16)) for k in range(1, 16)] + [along(1), along(2), along(3), across]
    for place in places:
        pl.semaphore_signal(barrier, inc=1, device_id=place, device_id_type=pl.DeviceIdType.MESH)

    @pl.when(me >= 4)
    def _():
        @pl.loop(0, 16)
        def _(k):
            place = dict(ctx_at(lax.rem(me + k, 16)), **along(me // 4))
            pl.semaphore_signal(barrier, inc=1, device_id=place, device_id_type=pl.DeviceIdType.MESH)

    pl.semaphore_wait(barrier, len(places) + 12)

    def att_at(unit):
        return att.at[
            pl.ds(pl.multiple_of(unit // 4 * ROWS, ROWS), ROWS), pl.ds(pl.multiple_of(lax.rem(unit, 4) * HD, HD), HD)
        ]

    def att_copy(dest, source):
        return remote(block(att_hbm, dest), att_at(source), att_sent.at[dest], att_land.at[source], ctx_at(dest))

    @pl.loop(1, 16)
    def _(k):
        att_copy(lax.rem(me + k, 16), me).start()

    own_att = pltpu.make_async_copy(block(att_hbm, me), att_at(me), local_sem.at[0])
    own_att.start()
    cot_copies = [
        remote(row_slots(cot_hbm)(r), row_slots(cots)(4 + r), cot_sent.at[r], cot_land.at[r], across) for r in range(4)
    ]
    cot_copies[0].start()
    cot_copies[1].start()
    waits.extend(cot_copies)

    def o_rows(k, h, at, count):
        return o_full.at[pl.ds(pl.multiple_of(k * half + h * side + at, 16), count), :]

    piece = core * HD + x * (ROWS // 4)
    oy_rings = []
    for h, src in ((0, o_own_hbm), (1, o_par_hbm)):

        def slot(k, part_of=None, h=h):
            if part_of is None:
                return o_rows(k, h, piece, ROWS // 4)
            return o_rows(k, h, piece + part_of * (ROWS // 8), ROWS // 8)

        own_piece = src.at[pl.ds(pl.multiple_of(piece, ROWS // 4), ROWS // 4), :]
        oy_rings.append(gather_ring(slot, along, oy_sent.at[h], oy_land.at[h], waits, own_piece))

    def ox_move(k, h, at_x, i, to):
        ref = o_rows(k, h, core * HD + at_x * (ROWS // 4), ROWS // 4)
        copy = remote(ref, ref, ox_sent.at[i, k - 1, h], ox_land.at[i, k - 1, h], along_x(to))
        copy.start()
        waits.append(copy)
        return copy

    def ox_start():
        return [ox_move(k, h, x, i, to) for k in (1, 2, 3) for h in (0, 1) for i, to in ((0, 3), (1, 1))]

    def ox_pass(near):
        for copy in near:
            copy.wait_recv()
        far = [ox_move(k, 0, lax.rem(x + 1, 4), 2, 3) for k in (1, 2, 3)]
        return far + [ox_move(k, 1, lax.rem(x + 3, 4), 2, 1) for k in (1, 2, 3)]

    def o_cores(far):
        for copy in far:
            copy.wait_recv()
        copies = []
        for k in (1, 2, 3):
            for h in (0, 1):
                ref = o_rows(k, h, core * HD, HD)
                copy = remote(ref, ref, oc_sent.at[k - 1, h], oc_land.at[k - 1, h], other_core)
                copy.start()
                copies.append(copy)
        waits.extend(copies)
        return copies

    loads[0].wait()
    loads[1].wait()
    own_att.wait()

    @pl.loop(1, 16)
    def _(k):
        att_copy(lax.rem(me + k, 16), lax.rem(me + k, 16)).wait_recv()

    for ring_pass, _ in oy_rings:
        ring_pass()

    def scattered(base, got_base, relay_at, sent, landed, wait_for_far=False):
        slots = row_slots(parts, base)

        def halves(ref, first):
            return lambda r, h: row_slots(ref, first)(r, h)

        def relay_half(h):
            return relay.at[pl.ds(relay_at * ROWS + h * (ROWS // 2), ROWS // 2), :]

        return scatter_ring(slots, relay_half, halves(got, got_base), along, sent, landed, waits, wait_for_far)

    def summed(base, got_base):
        value = parts[base * ROWS : (base + 1) * ROWS, :].astype(F32)
        for i in range(2):
            value += got[(got_base + i) * ROWS : (got_base + i + 1) * ROWS, :].astype(F32)
        return value

    @pl.loop(0, model // WIDE)
    def _(n):
        cols = pl.ds(pl.multiple_of(n * WIDE, WIDE), WIDE)
        value = dot(att[:, :side], o_own[:, cols]) + dot(att[:, side:], o_par[:, cols])
        parts[pl.ds(0, half), cols] = value.astype(BF16)

    o_waits = []
    o_pass, o_finish = scatter_ring(
        row_slots(parts),
        lambda h: relay.at[pl.ds(h * (ROWS // 2), ROWS // 2), :],
        lambda r, h: row_slots(o_got)(r, h),
        along, o_sent, o_land, o_waits,
    )

    def grads_of_cot(first, count):
        rows = pl.ds(first, count)

        @pl.loop(0, width // WIDE)
        def _(n):
            cols = pl.ds(pl.multiple_of(n * WIDE, WIDE), WIDE)
            act_grad[rows, cols] = dot(cots[rows, :], down_w[cols, :], ((1,), (1,))).astype(BF16)

    for _, ring_finish in oy_rings:
        ring_finish()
    o_near = ox_start()
    loads[2].wait()
    loads[3].wait()
    grads_of_cot(0, half)
    o_pass()
    o_finish()
    value = tokens[...].astype(F32) + parts[:ROWS, :].astype(F32)
    for i in range(2):
        value += o_got[i * ROWS : (i + 1) * ROWS, :].astype(F32)
    middle[...] = value
    hid[:ROWS, :] = (value * inverse_rms(value) * gain[...]).astype(BF16)

    hid_waits = []
    hid_pass, hid_finish = gather_ring(row_slots(hid), along, hid_sent, hid_land, hid_waits)
    hid_across = remote(row_slots(hid)(0), row_slots(hid)(4), across_sent.at[0], across_land.at[0], across)
    hid_across.start()
    hid_waits.append(hid_across)
    loads[4].wait()
    loads[5].wait()
    for copy in o_waits:
        copy.wait_send()
    hid_pass()
    hid_across.wait_recv()
    far_pass, far_finish = gather_ring(row_slots(hid, 4), along, far_sent, far_land, hid_waits)
    cot_copies[3].start()
    cot_copies[2].start()

    def forward(first, count):
        rows = pl.ds(first, count)

        @pl.loop(0, width // WIDE)
        def _(n):
            cols = pl.ds(pl.multiple_of(n * WIDE, WIDE), WIDE)
            gate = dot(hid[rows, :], gate_w[:, cols])
            up = dot(hid[rows, :], up_w[:, cols])
            sig = jax.nn.sigmoid(gate)
            silu = gate * sig
            grad = act_grad[rows, cols].astype(F32)
            act[rows, cols] = (silu * up).astype(BF16)
            gu_grad[rows, cols] = (grad * up * sig * (1.0 + gate * (1.0 - sig))).astype(BF16)
            gu_grad[rows, pl.ds(pl.multiple_of(width + n * WIDE, WIDE), WIDE)] = (grad * silu).astype(BF16)

    def backward(first, count):
        rows = pl.ds(first, count)

        @pl.loop(0, model // WIDE)
        def _(n):
            cols = pl.ds(pl.multiple_of(n * WIDE, WIDE), WIDE)
            value = dot(gu_grad[rows, :width], gate_w[cols, :], ((1,), (1,)))
            value += dot(gu_grad[rows, width:], up_w[cols, :], ((1,), (1,)))
            parts[rows, cols] = value.astype(BF16)

    forward(0, 2 * ROWS)
    forward(3 * ROWS, ROWS)
    hid_finish()
    forward(2 * ROWS, ROWS)
    o_far = ox_pass(o_near)
    cot_copies[0].wait_recv()
    cot_copies[1].wait_recv()
    grads_of_cot(half, 2 * ROWS)
    far_pass()
    backward(0, half)
    forward(half, 2 * ROWS)
    cot_copies[3].wait_recv()
    grads_of_cot(7 * ROWS, ROWS)
    forward(7 * ROWS, ROWS)
    backward(half, 2 * ROWS)
    backward(7 * ROWS, ROWS)
    far_back_pass, far_back_finish, far_back_rest = scattered(4, 2, 0, far_back_sent, far_back_land, True)
    o_core_copies = o_cores(o_far)
    cot_copies[2].wait_recv()
    grads_of_cot(6 * ROWS, ROWS)
    far_finish()
    forward(6 * ROWS, ROWS)
    backward(6 * ROWS, ROWS)
    far_back_rest()
    near_back_pass, near_back_finish = scattered(0, 0, 1, near_back_sent, near_back_land)

    def tile_pair(p, which):
        def columns(ref):
            return jnp.concatenate(
                [ref[:, pl.ds(pl.multiple_of(((2 * p + i) * 2 + which) * ROWS, ROWS), ROWS)] for i in range(2)], axis=1
            )

        return dot(columns(hid), gu_grad[...], ((0,), (0,))), dot(columns(cots), act[...], ((0,), (0,)))

    def pair_copy(b, p):
        return remote(stage.at[b], tiles.at[pl.ds(2 * p, 2)], core_sent.at[p], core_land.at[p], other_core)

    @pl.loop(0, 2)
    def _(m):
        for b in range(2):
            p = m * 2 + b

            @pl.when(m > 0)
            def _():
                pair_copy(b, p - 2).wait_send()

            gate_up, down = tile_pair(p, 1 - core)
            for i in range(2):
                stage[b, i, :, : 2 * width] = gate_up[i * ROWS : (i + 1) * ROWS].astype(BF16)
                stage[b, i, :, 2 * width :] = down[i * ROWS : (i + 1) * ROWS].astype(BF16)
            pair_copy(b, p).start()

    far_back_pass()

    @pl.loop(0, 2)
    def _(m):
        for b in range(2):
            p = m * 2 + b
            gate_up, down = tile_pair(p, core)
            pair_copy(b, p).wait_recv()
            for i in range(2):
                at = 2 * p + i
                near = tiles[at]
                value = gate_up[i * ROWS : (i + 1) * ROWS] + near[:, : 2 * width].astype(F32)
                tiles[at, :, : 2 * width] = value.astype(BF16)
                value = down[i * ROWS : (i + 1) * ROWS] + near[:, 2 * width :].astype(F32)
                tiles[at, :, 2 * width :] = value.astype(BF16)

    tile_pass, tile_finish = scatter_ring(
        lambda k, h: tiles.at[h * 4 + lax.rem(x + k, 4)],
        lambda h: tile_relay.at[h],
        lambda r, h: tile_got.at[r, h],
        along_x, x_sent, x_land, waits,
    )
    near_back_pass()
    far_back_finish()
    z_out[...] = summed(4, 2).astype(BF16)
    z_copy = remote(z_out, z_got, across_sent.at[1], across_land.at[1], across)
    z_copy.start()
    waits.append(z_copy)

    def down_part(first):
        rows = pl.ds(first, half)

        @pl.loop(0, model // WIDE)
        def _(n):
            cols = pl.ds(pl.multiple_of(n * WIDE, WIDE), WIDE)
            part[rows, cols] = dot(act[rows, :], down_w[:, cols]).astype(BF16)

    for copy in o_core_copies:
        copy.wait_recv()
    for copy in hid_waits:
        copy.wait_send()
    o_loads = [
        pltpu.make_async_copy(o_full.at[pl.ds(k * half, half), :], ref.at[pl.ds(first, half), :], oload_sem.at[k - 1])
        for k, ref, first in ((1, cots, 0), (2, cots, half), (3, hid, 0))
    ]
    for load in o_loads:
        load.start()
    down_part(0)
    down_part(half)
    outs = [
        pltpu.make_async_copy(part.at[pl.ds(half, half), :], part_hbm, out_sem.at[0]),
        pltpu.make_async_copy(att, att_out, out_sem.at[1]),
    ]
    for copy in outs:
        copy.start()
    part_pass, part_finish = scatter_ring(
        row_slots(part),
        lambda h: relay.at[pl.ds(2 * ROWS + h * (ROWS // 2), ROWS // 2), :],
        lambda r, h: row_slots(o_got)(r, h),
        along, part_sent, part_land, waits,
    )
    tile_pass()
    near_back_finish()
    z_copy.wait_recv()

    rows_back, gain_sum = rms_back(summed(0, 0) + z_got[...].astype(F32), middle[...], gain[...])
    gain_grad[...] = gain_sum
    value = cot[...].astype(F32) + rows_back
    middle_grad[...] = value
    branch[...] = value.astype(BF16)

    def unit_copy(k, h):
        unit = (4 - k) % 4 * 4 + h
        place = dict(ctx_at(unit), **along(k))
        cols = pl.ds(pl.multiple_of((k * 4 + h) * HD, HD), HD)
        return remote(att_grad.at[:, cols], block(grad_got, me), grad_sent.at[k * 4 + h], grad_land.at[me], place)

    for k in range(4):
        at = k * 4 * HD
        if k == 0:
            att_grad[:, :side] = dot(branch[...], o_own[...], ((1,), (1,))).astype(BF16)
            att_grad[:, side : 2 * side] = dot(branch[...], o_par[...], ((1,), (1,))).astype(BF16)
        else:
            o_loads[k - 1].wait()
            rows_of = (cots[:half, :], cots[half:, :], hid[:half, :])[k - 1]
            att_grad[:, at : at + 4 * HD] = dot(branch[...], rows_of, ((1,), (1,))).astype(BF16)

        @pl.loop(0, 4)
        def _(j):
            h = lax.rem(me + j, 4)

            @pl.when((k > 0) | (h != me))
            def _():
                unit_copy(k, h).start()

    def own_grad():
        cols = pl.ds(pl.multiple_of(lax.rem(me, 4) * HD, HD), HD)
        return pltpu.make_async_copy(att_grad.at[:, cols], block(grad_got, me), local_sem.at[1])

    @pl.when(me < 4)
    def _():
        own_grad().start()

    tile_finish()

    def tile_sum(a):
        value = tiles[a * 4 + x].astype(F32)
        for i in range(2):
            value += tile_got[i, a].astype(F32)
        return value

    mlp_low[...] = tile_sum(1 - zl).astype(BF16)
    mlp_total[...] = tile_sum(zl)
    for b in range(2):
        pair_copy(b, 2 + b).wait_send()
    part_pass()

    @pl.loop(1, 16)
    def _(k):
        peer = lax.rem(me + k, 16)
        att_copy(peer, peer).wait_send()

    @pl.loop(0, 16)
    def _(source):
        @pl.when((me >= 4) | (source != me))
        def _():
            remote(
                att_grad.at[:, pl.ds(0, HD)], block(grad_got, source), grad_sent.at[0], grad_land.at[source], other_core
            ).wait_recv()

    for k in range(4):

        @pl.loop(0, 4)
        def _(h):
            @pl.when((k > 0) | (h != me))
            def _():
                unit_copy(k, h).wait_send()

    @pl.when(me < 4)
    def _():
        own_grad().wait()


    part_finish()
    value = middle[...] + part[:ROWS, :].astype(F32)
    for i in range(2):
        value += o_got[i * ROWS : (i + 1) * ROWS, :].astype(F32)
    middle[...] = value
    for copy in waits:
        copy.wait_send()
    for copy in outs:
        copy.wait()


def middle_part(tokens, cot, gain, att, o_own, o_par, cot_half, gate_w, up_w, down_w):
    rows, model = tokens.shape
    width = gate_w.shape[1]
    anywhere = pl.BlockSpec(memory_space=pl.ANY)
    vmem = pl.BlockSpec(memory_space=pltpu.VMEM)
    dma = pltpu.SemaphoreType.DMA
    half = jax.ShapeDtypeStruct((4 * rows, model), BF16)
    low = functools.partial(pltpu.VMEM, dtype=BF16)
    return pl.pallas_call(
        middle_kernel,
        out_shape=(
            jax.ShapeDtypeStruct((rows, model), F32),
            jax.ShapeDtypeStruct((rows, model), F32),
            jax.ShapeDtypeStruct((1, model), F32),
            jax.ShapeDtypeStruct((rows, 3 * width), F32),
            jax.ShapeDtypeStruct((rows, 3 * width), BF16),
            jax.ShapeDtypeStruct((16 * rows, HD), BF16),
            jax.ShapeDtypeStruct((4 * rows, 4 * HD), BF16),
            jax.ShapeDtypeStruct((rows, model), BF16),
            half,
            jax.ShapeDtypeStruct((16 * HD, model), BF16),
        ),
        in_specs=[vmem] * 3 + [anywhere] * 7,
        out_specs=(vmem,) * 5 + (anywhere,) * 2 + (vmem,) + (anywhere,) * 2,
        scratch_shapes=[
            low((4 * rows, 4 * HD)),
            low((2 * HD, model)),
            low((2 * HD, model)),
            low((3 * rows, model)),
            low((2 * rows, model)),
            low((8 * rows, model)),
            low((8 * rows, model)),
            low((model, width)),
            low((model, width)),
            low((width, model)),
            low((8 * rows, width)),
            low((8 * rows, 2 * width)),
            low((8 * rows, width)),
            low((8 * rows, model)),
            low((4 * rows, model)),
            low((rows, model)),
            low((rows, model)),
            low((8 * rows, model)),
            low((2, 2, rows, 3 * width)),
            low((8, rows, 3 * width)),
            low((2, rows, 3 * width)),
            low((2, 2, rows, 3 * width)),
            low((rows, 16 * HD)),
            dma((6,)),
            dma((16,)),
            dma((16,)),
            dma((6,)),
            dma((6,)),
            dma((4,)),
            dma((4,)),
            dma((4,)),
            dma((4,)),
            dma((2,)),
            dma((2,)),
            dma((6,)),
            dma((6,)),
            dma((6,)),
            dma((6,)),
            dma((4,)),
            dma((4,)),
            dma((6,)),
            dma((6,)),
            dma((2, 4)),
            dma((2, 4)),
            dma((3, 3, 2)),
            dma((3, 3, 2)),
            dma((3, 2)),
            dma((3, 2)),
            dma((16,)),
            dma((16,)),
            dma((4,)),
            dma((4,)),
            dma((6,)),
            dma((6,)),
            dma((3,)),
            dma((2,)),
            dma((3,)),
        ],
        compiler_params=pltpu.CompilerParams(
            collective_id=1, has_side_effects=True, vmem_limit_bytes=63 * 2**20
        ),
        cost_estimate=pl.CostEstimate(
            flops=2 * 9 * 8 * rows * model * width, bytes_accessed=40 * 2**20, transcendentals=8 * rows * width
        ),
        name="middle",
    )(tokens, cot, gain, att, o_own, o_par, cot_half, gate_w, up_w, down_w)


def back_kernel(
    place, stored, doc_lengths, log_total, cos, sin, q_gain, k_gain, attn_gain, mlp_gain_grad,
    grad_hbm, q_pos_hbm, k_pos_hbm, v_pos_hbm, part_hbm, branch_hbm, att_hbm, raw_hbm, normed_hbm, own_hbm, par_hbm,
    middle_hbm, tokens_hbm, middle_grad_hbm, mlp_hbm, mlp_low_hbm,
    tokens_grad, out_rows, q_wgrad, k_wgrad, v_wgrad, o_wgrad, attn_total, mlp_total, q_total, k_total, gate_wgrad, up_wgrad, down_wgrad,
    mlp_sum, mlp_got,
    grad_in, q_pos, k_pos, v_pos, grad_pos, q_acc, q_grad, send, k_acc, v_acc, keep, raw, middle, tokens, middle_grad,
    normed, w_own, w_par, branch_all, att, part, out_got, relay, out_across, swap_got, kv_out, q_got, kv_got, low_q, low_kv, parts, y_got,
    q_bufs, kv_bufs, o_bufs,
    g_out, g_got, by_gain,
    load_sem, mlp_sem, swap_sem, across_sem, q_sent, q_land, kv_sent, kv_land, y_sent, y_land, out_sent, out_land, branch_sent, branch_land,
    core_sent, core_land, x_sent, x_land, z_sent, z_land, g_sent, g_land,
):
    zl, x, core = (lax.axis_index(a) for a in CTX)
    zh, y = (lax.axis_index(a) for a in FSDP)
    me = zl * 8 + x * 2 + core
    half = 4 * HD

    def along_y(k):
        return {"y": lax.rem(y + k, 4)}

    def along_x(k):
        return {"x": lax.rem(x + k, 4)}

    def along_ctx(k):
        return ctx_at(lax.rem(me + k, 16))

    other_core = {"core": 1 - core}
    zs = {1: {"zl": 1 - zl}, 2: {"zh": 1 - zh}, 3: {"zl": 1 - zl, "zh": 1 - zh}}

    loads = [
        pltpu.make_async_copy(src, dst, load_sem.at[i])
        for i, (src, dst) in enumerate(
            (
                (part_hbm, part),
                (grad_hbm, grad_in),
                (q_pos_hbm, q_pos),
                (k_pos_hbm, k_pos),
                (v_pos_hbm, v_pos),
                (branch_hbm, branch_all.at[pl.ds(0, ROWS), :]),
                (att_hbm, att),
                (normed_hbm, normed),
                (raw_hbm, raw),
                (own_hbm, w_own),
                (par_hbm, w_par),
                (middle_hbm, middle),
                (tokens_hbm, tokens),
                (middle_grad_hbm, middle_grad),
                (mlp_hbm, mlp_sum),
            )
        )
    ]
    for load in loads:
        load.start()
    peers([along_ctx(k) for k in range(1, 16)] + [along_y(k) for k in (1, 2, 3)] + [zs[2], zs[3]])
    waits = []

    mlp_copy = remote(mlp_low_hbm, mlp_got, mlp_sem.at[0], mlp_sem.at[1], zs[1])
    loads[5].wait()
    branch_pass, branch_finish = gather_ring(row_slots(branch_all), along_y, branch_sent, branch_land, waits)

    def grad_stages(first, tile, to_other, from_other, summed, x_relay, from_x, total, total_low, from_z):
        n = total.shape[2] // 2

        def over_cores():
            @pl.loop(0, 8)
            def _(t):
                to_other[t] = tile(t * 2 + 1 - core).astype(BF16)

            copy = remote(to_other, from_other, core_sent.at[first], core_land.at[first], other_core)
            copy.start()
            waits.append(copy)
            return copy

        def over_x(core_copy):
            core_copy.wait_recv()

            @pl.loop(0, 8)
            def _(t):
                summed[t] = (tile(t * 2 + core) + from_other[t].astype(F32)).astype(BF16)

            return scatter_ring(
                lambda k, h: summed.at[h * 4 + lax.rem(x + k, 4)],
                lambda h: x_relay.at[h],
                lambda r, h: from_x.at[r, h],
                along_x, x_sent.at[first], x_land.at[first], waits,
            )

        def over_z(x_finish):
            x_finish()
            for a in range(2):
                value = summed[a * 4 + x].astype(F32)
                for i in range(2):
                    value += from_x[i, a].astype(F32)
                total[a] = value
                total_low[a] = value.astype(BF16)
            copies = []
            for d in (1, 2, 3):
                rows_of = 1 - zl if d % 2 else zl
                copy = remote(
                    total_low.at[rows_of, :, pl.ds(n if d >= 2 else 0, n)], from_z.at[d - 1],
                    z_sent.at[first * 3 + d - 1], z_land.at[first * 3 + d - 1], zs[d],
                )
                copy.start()
                copies.append(copy)
            waits.extend(copies)
            return copies

        def finish(z_copies):
            for copy in z_copies:
                copy.wait_recv()
            value = total[zl, :, :n]
            for d in range(3):
                value = value + from_z[d].astype(F32)
            return value

        return over_cores, over_x, over_z, finish

    def tile_of(left, right):
        def tile(t):
            cols = pl.ds(pl.multiple_of(t * ROWS, ROWS), ROWS)
            return dot(left[:, cols], right[...], ((0,), (0,)))

        return tile

    q_cores, q_x, q_z, q_finish = grad_stages(0, tile_of(normed, low_q), *q_bufs)
    kv_cores, kv_x, kv_z, kv_finish = grad_stages(1, tile_of(normed, low_kv), *kv_bufs)
    o_cores, o_x, o_z, o_finish = grad_stages(2, tile_of(branch_all, att), *o_bufs)
    for load in loads[:5] + loads[6:7]:
        load.wait()

    blocks = q_pos.shape[0] // BLK
    ordered(stored, blocks, ((grad_in, grad_pos),))
    ends = document_ends(doc_lengths, zh * 4 + lax.rem(y + me // 4, 4))
    attend_back(ends, q_pos, k_pos, v_pos, log_total, grad_pos, q_acc, k_acc, v_acc)
    ordered(place, blocks, ((q_acc, q_grad),))

    @pl.loop(0, blocks)
    def _(b):
        dst_rows = pl.ds(pl.multiple_of(b * BLK, BLK), BLK)
        k_rows = k_acc[place[b]] * HD ** (-0.5)
        v_rows = v_acc[place[b]]
        keep[dst_rows, :] = jnp.where(core == 0, k_rows, v_rows)
        send[dst_rows, :] = jnp.where(core == 0, v_rows, k_rows).astype(BF16)

    swap = remote(send, swap_got, swap_sem.at[0], swap_sem.at[1], other_core)
    swap.start()

    waits.append(swap)

    def to_rows(src, dst, sent, landed):
        copies = []
        for k in range(1, 16):
            copy = remote(block(src, lax.rem(me + k, 16)), block(dst, 16 - k), sent.at[k], landed.at[16 - k], along_ctx(k))
            copy.start()
            copies.append(copy)
        waits.extend(copies)
        return copies

    q_copies = to_rows(q_grad, q_got, q_sent, q_land)
    mine = pl.ds(pl.multiple_of(me * ROWS, ROWS), ROWS)
    q_got[:ROWS, :] = q_grad[mine, :]
    branch_pass()
    out_pass, out_finish = scatter_ring(
        row_slots(part),
        lambda h: relay.at[pl.ds(h * (ROWS // 2), ROWS // 2), :],
        lambda r, h: row_slots(out_got)(r, h),
        along_y, out_sent, out_land, waits,
    )
    swap.wait_recv()
    kv_out[...] = (keep[...] + swap_got[...].astype(F32)).astype(BF16)
    kv_copies = to_rows(kv_out, kv_got, kv_sent, kv_land)
    kv_got[:ROWS, :] = kv_out[mine, :]

    for load in loads[7:]:
        load.wait()
    for copy in q_copies:
        copy.wait_recv()

    g_out[0] = jnp.zeros_like(g_out[0])

    def from_unit(ref, unit):
        return ref[pl.ds(pl.multiple_of(lax.rem(unit - me + 16, 16) * ROWS, ROWS), ROWS), :]

    def head_back(grad, value, gain):
        turned = grad * sin[...]
        turned = jnp.concatenate([turned[:, HD // 2 :], -turned[:, : HD // 2]], axis=1)
        back, gain_sum = rms_back(grad * cos[...] + turned, value, gain)
        return back.astype(BF16), gain_sum

    @pl.loop(0, 4)
    def _(s):
        rows = pl.ds(pl.multiple_of(s * ROWS, ROWS), ROWS)
        for h in range(4):
            at = (h // 2) * half + (h % 2) * HD
            grad = from_unit(q_got, s * 4 + h).astype(F32)
            back, gain_sum = head_back(grad, raw[rows, at : at + HD], q_gain[...])
            low_q[rows, h * HD : (h + 1) * HD] = back
            g_out[0, 32:33, :] += gain_sum

    q_core_copy = q_cores()
    mlp_copy.start()
    waits.append(mlp_copy)
    branch_finish()
    o_core_copy = o_cores()
    for copy in kv_copies:
        copy.wait_recv()

    @pl.loop(0, 4)
    def _(s):
        rows = pl.ds(pl.multiple_of(s * ROWS, ROWS), ROWS)
        for kv in range(2):
            at = kv * half + 2 * HD
            grad = from_unit(kv_got, s * 4 + kv * 2).astype(F32)
            back, gain_sum = head_back(grad, raw[rows, at : at + HD], k_gain[...])
            low_kv[rows, kv * 2 * HD : (kv * 2 + 1) * HD] = back
            g_out[0, 33:34, :] += gain_sum
            low_kv[rows, (kv * 2 + 1) * HD : (kv * 2 + 2) * HD] = from_unit(kv_got, s * 4 + kv * 2 + 1)

    kv_core_copy = kv_cores()
    out_pass()
    q_x_pass, q_x_finish = q_x(q_core_copy)
    @pl.loop(0, parts.shape[1] // WIDE)
    def _(n):
        cols = pl.ds(pl.multiple_of(n * WIDE, WIDE), WIDE)
        total = dot(low_q[:, : half // 2], w_own[cols, : half // 2], ((1,), (1,)))
        total += dot(low_q[:, half // 2 :], w_par[cols, : half // 2], ((1,), (1,)))
        total += dot(low_kv[:, : half // 2], w_own[cols, half // 2 :], ((1,), (1,)))
        total += dot(low_kv[:, half // 2 :], w_par[cols, half // 2 :], ((1,), (1,)))
        parts[:, cols] = total.astype(BF16)
        by_gain[:, cols] = jnp.sum(total * normed[:, cols].astype(F32), axis=0, keepdims=True) / attn_gain[:, cols]

    for i in range(16):
        g_out[0, i : i + 1, :] = by_gain[:, i * HD : (i + 1) * HD]
        g_out[0, 16 + i : 17 + i, :] = mlp_gain_grad[:, i * HD : (i + 1) * HD]
    y_pass, y_finish = scatter_ring(
        row_slots(parts),
        lambda h: relay.at[pl.ds(ROWS + h * (ROWS // 2), ROWS // 2), :],
        lambda r, h: row_slots(y_got)(r, h),
        along_y, y_sent, y_land, waits,
    )

    def gain_stage(stage, places):
        copies = []
        for i, (place, back_slot) in enumerate(places):
            copy = remote(
                g_out.at[stage], g_got.at[stage, back_slot], g_sent.at[stage * 3 + i],
                g_land.at[stage * 3 + back_slot], place,
            )
            copy.start()
            copies.append(copy)
        waits.extend(copies)
        return copies

    def gain_sum_of(stage, copies):
        for copy in copies:
            copy.wait_recv()
        total = g_out[stage]
        for i in range(len(copies)):
            total = total + g_got[stage, i]
        return total

    copies = gain_stage(0, [(along_y(k), 3 - k) for k in (1, 2, 3)])
    kv_x_pass, kv_x_finish = kv_x(kv_core_copy)
    q_x_pass()
    o_x_pass, o_x_finish = o_x(o_core_copy)
    out_finish()
    value = part[:ROWS, :].astype(F32)
    for i in range(2):
        value += out_got[i * ROWS : (i + 1) * ROWS, :].astype(F32)
    part[:ROWS, :] = value.astype(BF16)
    across_copy = remote(part.at[pl.ds(0, ROWS), :], out_across, across_sem.at[0], across_sem.at[1], zs[2])
    across_copy.start()
    waits.append(across_copy)
    y_pass()
    kv_x_pass()
    g_out[1] = gain_sum_of(0, copies)
    copies = gain_stage(1, [(along_x(k), 3 - k) for k in (1, 2, 3)])
    o_x_pass()
    mlp_copy.wait_recv()
    width = gate_wgrad.shape[1]
    gate_wgrad[...] = mlp_sum[:, :width] + mlp_got[:, :width].astype(F32)
    up_wgrad[...] = mlp_sum[:, width : 2 * width] + mlp_got[:, width : 2 * width].astype(F32)
    for i in range(width // HD):
        cols = slice(2 * width + i * HD, 2 * width + (i + 1) * HD)
        down_wgrad[i * HD : (i + 1) * HD, :] = (mlp_sum[:, cols] + mlp_got[:, cols].astype(F32)).T
    q_z_copies = q_z(q_x_finish)
    g_out[2] = gain_sum_of(1, copies)
    copies = gain_stage(2, [(zs[d], d - 1) for d in (1, 2, 3)])
    across_copy.wait_recv()
    out_rows[...] = (middle[...] + out_across[...].astype(F32)).astype(BF16)
    kv_z_copies = kv_z(kv_x_finish)

    y_finish()
    grad = parts[:ROWS, :].astype(F32)
    for i in range(2):
        grad += y_got[i * ROWS : (i + 1) * ROWS, :].astype(F32)
    rows_back, _ = rms_back(grad, tokens[...].astype(F32), attn_gain[...])
    tokens_grad[...] = (middle_grad[...] + rows_back).astype(BF16)
    g_out[3] = gain_sum_of(2, copies)
    copies = gain_stage(3, [(other_core, 0)])
    o_z_copies = o_z(o_x_finish)
    q_wgrad[...] = q_finish(q_z_copies)
    value = kv_finish(kv_z_copies)
    k_wgrad[...] = value[:, :HD]
    v_wgrad[...] = value[:, HD:]
    value = o_finish(o_z_copies)
    for i in range(2):
        o_wgrad[i * HD : (i + 1) * HD, :] = value[:, i * HD : (i + 1) * HD].T
    gains = gain_sum_of(3, copies)
    for i in range(16):
        attn_total[:, i * HD : (i + 1) * HD] = gains[i : i + 1, :]
        mlp_total[:, i * HD : (i + 1) * HD] = gains[16 + i : 17 + i, :]
    q_total[...] = gains[32:33, :]
    k_total[...] = gains[33:34, :]
    for copy in waits:
        copy.wait_send()


def stage_buffers(rows):
    wide = 4 * HD
    low = functools.partial(pltpu.VMEM, dtype=BF16)
    return (
        low((8, rows, wide)),
        low((8, rows, wide)),
        low((8, rows, wide)),
        low((2, rows, wide)),
        low((2, 2, rows, wide)),
        pltpu.VMEM((2, rows, wide), F32),
        low((2, rows, wide)),
        low((3, rows, wide // 2)),
    )


def back(place, stored, doc_lengths, log_total, cos, sin, q_gain, k_gain, attn_gain, mlp_gain_grad, grad_in, q_pos, k_pos,
         v_pos, part, branch, att, raw, normed, w_own, w_par, middle, tokens, middle_grad, mlp_sum, mlp_low):
    rows, model = tokens.shape
    wide = raw.shape[1]
    width = mlp_sum.shape[1] // 3
    anywhere = pl.BlockSpec(memory_space=pl.ANY)
    vmem = pl.BlockSpec(memory_space=pltpu.VMEM)
    dma = pltpu.SemaphoreType.DMA
    return pl.pallas_call(
        back_kernel,
        out_shape=(
            jax.ShapeDtypeStruct((rows, model), BF16),
            jax.ShapeDtypeStruct((rows, model), BF16),
            jax.ShapeDtypeStruct((rows, 2 * HD), F32),
            jax.ShapeDtypeStruct((rows, HD), F32),
            jax.ShapeDtypeStruct((rows, HD), F32),
            jax.ShapeDtypeStruct((2 * HD, rows), F32),
            jax.ShapeDtypeStruct((1, model), F32),
            jax.ShapeDtypeStruct((1, model), F32),
            jax.ShapeDtypeStruct((1, HD), F32),
            jax.ShapeDtypeStruct((1, HD), F32),
            jax.ShapeDtypeStruct((rows, width), F32),
            jax.ShapeDtypeStruct((rows, width), F32),
            jax.ShapeDtypeStruct((width, rows), F32),
        ),
        in_specs=[pl.BlockSpec(memory_space=pltpu.SMEM)] * 3 + [vmem] * 7 + [anywhere] * 16,
        out_specs=(vmem,) * 13,
        scratch_shapes=[pltpu.VMEM((rows, 3 * width), F32), pltpu.VMEM((rows, 3 * width), BF16)]
        + [pltpu.VMEM((16 * rows // BLK, BLK, HD), BF16)]
        + [pltpu.VMEM((16 * rows, HD), BF16)] * 4
        + [pltpu.VMEM((16 * rows // BLK, BLK, HD), BF16)]
        + [pltpu.VMEM((16 * rows, HD), BF16)] * 2
        + [pltpu.VMEM((16 * rows // BLK, BLK, HD), F32)] * 2
        + [pltpu.VMEM((16 * rows, HD), F32)]
        + [
            pltpu.VMEM((4 * rows, wide), F32),
            pltpu.VMEM((rows, model), F32),
            pltpu.VMEM((rows, model), BF16),
            pltpu.VMEM((rows, model), F32),
            pltpu.VMEM((4 * rows, model), BF16),
            pltpu.VMEM((model, wide // 2), BF16),
            pltpu.VMEM((model, wide // 2), BF16),
            pltpu.VMEM((4 * rows, model), BF16),
            pltpu.VMEM((4 * rows, 4 * HD), BF16),
            pltpu.VMEM((4 * rows, model), BF16),
            pltpu.VMEM((2 * rows, model), BF16),
            pltpu.VMEM((2 * rows, model), BF16),
            pltpu.VMEM((rows, model), BF16),
            pltpu.VMEM((16 * rows, HD), BF16),
            pltpu.VMEM((16 * rows, HD), BF16),
            pltpu.VMEM((16 * rows, HD), BF16),
            pltpu.VMEM((16 * rows, HD), BF16),
            pltpu.VMEM((4 * rows, wide // 2), BF16),
            pltpu.VMEM((4 * rows, wide // 2), BF16),
            pltpu.VMEM((4 * rows, model), BF16),
            pltpu.VMEM((2 * rows, model), BF16),
            stage_buffers(rows),
            stage_buffers(rows),
            stage_buffers(rows),
            pltpu.VMEM((4, 40, HD), F32),
            pltpu.VMEM((4, 3, 40, HD), F32),
            pltpu.VMEM((1, model), F32),
            dma((15,)),
            dma((2,)),
            dma((2,)),
            dma((2,)),
            dma((16,)),
            dma((16,)),
            dma((16,)),
            dma((16,)),
            dma((6,)),
            dma((6,)),
            dma((6,)),
            dma((6,)),
            dma((4,)),
            dma((4,)),
            dma((3,)),
            dma((3,)),
            dma((3, 6)),
            dma((3, 6)),
            dma((9,)),
            dma((9,)),
            dma((12,)),
            dma((12,)),
        ],
        compiler_params=pltpu.CompilerParams(
            collective_id=2, has_side_effects=True, vmem_limit_bytes=62 * 2**20
        ),
        cost_estimate=pl.CostEstimate(
            flops=4 * 4 * rows * model * wide, bytes_accessed=24 * 2**20, transcendentals=0
        ),
        name="back",
    )(
        place, stored, doc_lengths, log_total, cos, sin, q_gain, k_gain, attn_gain, mlp_gain_grad,
        grad_in.reshape(-1, BLK, HD), q_pos, k_pos, v_pos, part, branch, att, raw, normed, w_own, w_par, middle, tokens, middle_grad, mlp_sum, mlp_low,
    )


def results_kernel(*refs):
    count = (len(refs) - 2) // 3
    arrays, outs, held, (in_sem, out_sem) = refs[:count], refs[count : 2 * count], refs[2 * count : 3 * count], refs[-2:]
    copies = [pltpu.make_async_copy(arrays[i], held[i], in_sem.at[i]) for i in range(count)]
    for copy in copies:
        copy.start()
    for i in range(count):
        copies[i].wait()
        copies[i] = pltpu.make_async_copy(held[i], outs[i], out_sem.at[i])
        copies[i].start()
    for copy in copies:
        copy.wait()


def results(arrays):
    anywhere = pl.BlockSpec(memory_space=pl.ANY)
    return pl.pallas_call(
        results_kernel,
        out_shape=tuple(jax.ShapeDtypeStruct(a.shape, a.dtype) for a in arrays),
        in_specs=[anywhere] * len(arrays),
        out_specs=(anywhere,) * len(arrays),
        scratch_shapes=[pltpu.VMEM(a.shape, a.dtype) for a in arrays] + [pltpu.SemaphoreType.DMA((len(arrays),))] * 2,
        compiler_params=pltpu.CompilerParams(vmem_limit_bytes=62 * 2**20),
        name="results",
    )(*arrays)


def per_device(
    tokens,
    cotangent,
    attn_gain,
    q_weight,
    k_weight,
    v_weight,
    q_gain,
    k_gain,
    o_weight,
    mlp_gain,
    gate_weight,
    up_weight,
    down_weight,
    doc_lengths,
    block_place,
):
    rows = tokens.shape[1]
    zl, x, core = (lax.axis_index(a) for a in CTX)
    ctx_place = zl * 8 + x * 2 + core
    numbers = jnp.arange(block_place.shape[0], dtype=jnp.int32)
    stored = jnp.sum(jnp.where(block_place[None, :] == numbers[:, None], numbers[None, :], 0), axis=1, dtype=jnp.int32)
    own_blocks = lax.dynamic_slice_in_dim(block_place, ctx_place * (rows // BLK), rows // BLK)
    own_positions = (own_blocks[:, None] * BLK + jnp.arange(BLK, dtype=jnp.int32)[None, :]).reshape(-1)
    cos_rows, sin_rows = tables(own_positions, HD)
    q_gain, k_gain = q_gain.reshape(1, HD), k_gain.reshape(1, HD)
    attn_gain, mlp_gain = attn_gain.reshape(1, -1), mlp_gain.reshape(1, -1)
    cot = cotangent[0]

    log_total, out, q_pos, k_pos, v_pos, raw, normed, w_own, w_par, o_par, cot_half = pre(
        block_place, stored, doc_lengths, tokens[0], cos_rows, sin_rows, attn_gain, q_gain, k_gain, cot, q_weight, k_weight,
        v_weight, o_weight,
    )
    (
        middle, middle_grad, mlp_gain_grad, mlp_sum, mlp_low, grad_in, att, branch, part, _,
    ) = middle_part(tokens[0], cot, mlp_gain, out, o_weight, o_par, cot_half, gate_weight, up_weight, down_weight)
    (
        tokens_grad, out_rows, q_wgrad, k_wgrad, v_wgrad, o_wgrad, attn_gain_grad, mlp_gain_grad, q_gain_grad, k_gain_grad,
        gate_wgrad, up_wgrad, down_wgrad,
    ) = back(
        block_place, stored, doc_lengths, log_total, cos_rows, sin_rows, q_gain, k_gain, attn_gain, mlp_gain_grad, grad_in,
        q_pos, k_pos, v_pos, part, branch, att, raw, normed, w_own, w_par, middle, tokens[0], middle_grad, mlp_sum, mlp_low,
    )
    (
        out_rows, tokens_grad, attn_gain_grad, q_wgrad, k_wgrad, v_wgrad, q_gain_grad, k_gain_grad, o_wgrad, mlp_gain_grad,
        gate_wgrad, up_wgrad, down_wgrad,
    ) = results(
        (
            out_rows, tokens_grad, attn_gain_grad, q_wgrad, k_wgrad, v_wgrad, q_gain_grad, k_gain_grad, o_wgrad,
            mlp_gain_grad, gate_wgrad, up_wgrad, down_wgrad,
        )
    )
    return (
        out_rows[None],
        tokens_grad[None],
        attn_gain_grad[0],
        q_wgrad,
        k_wgrad,
        v_wgrad,
        q_gain_grad[0],
        k_gain_grad[0],
        o_wgrad,
        mlp_gain_grad[0],
        gate_wgrad,
        up_wgrad,
        down_wgrad,
    )


def solution(mesh):
    fine = Mesh(mesh.devices.reshape(SIZES), AXES)
    rows = P(FSDP, CTX, None)
    in_specs = (
        rows,
        rows,
        P(),
        P(None, FSDP),
        P(None, FSDP),
        P(None, FSDP),
        P(),
        P(),
        P(FSDP, None),
        P(),
        P(None, FSDP),
        P(None, FSDP),
        P(FSDP, None),
        P(),
        P(),
    )
    out_specs = (
        rows,
        rows,
        P(),
        P(CTX, FSDP),
        P(CTX, FSDP),
        P(CTX, FSDP),
        P(),
        P(),
        P(FSDP, CTX),
        P(),
        P(CTX, FSDP),
        P(CTX, FSDP),
        P(FSDP, CTX),
    )
    return jax.shard_map(
        per_device, mesh=fine, in_specs=in_specs, out_specs=out_specs, check_vma=False
    )
```
